256 devices in a mesh: rows: 32 (over z, y_hi, core), cols: 8 (over x, y_lo).
Axes of the slice: x: 4, y: 4 (y_hi: 2, y_lo: 2; y = y_hi * 2 + y_lo), z: 8, core: 2. Of those that a mesh axis runs over, the one named last changes fastest.
Arguments:
- latent: bfloat16 [256, 1024, 128], P('rows', 'cols'), may hold values from -36 to 36, as said below
- cotangent: bfloat16 [256, 1024, 128], P('rows', 'cols'), may hold values from -6 to 6
- w_qkv: bfloat16 [2, 128, 384], replicated, may hold values from -0.5 to 0.5
- w_proj: bfloat16 [2, 128, 128], replicated, may hold values from -0.5 to 0.5
- w_up: bfloat16 [2, 128, 512], replicated, may hold values from -0.5 to 0.5
- w_down: bfloat16 [2, 512, 128], replicated, may hold values from -0.25 to 0.25
- gains: float32 [2, 2, 128], replicated, may hold values from 0.5 to 1.5
- attn_bias: float32 [2, 4, 64, 64], replicated, may hold values from -4 to 300
Outputs:
- latent_grad: bfloat16 [256, 1024, 128], P('rows', 'cols')
- qkv_grad: float32 [2, 128, 384], replicated
- proj_grad: float32 [2, 128, 128], replicated
- up_grad: float32 [2, 128, 512], replicated
- down_grad: float32 [2, 512, 128], replicated
- gains_grad: float32 [2, 2, 128], replicated
- bias_grad: float32 [2, 4, 64, 64], replicated
The draws below stay inside these ranges and needn't reach their ends.
Inputs may be any that keep to these rules, and one draw needn't show every extreme that they name: `latent`: token and channel scales vary.
All inputs are finite; a program needn't handle non-finite values.
Results may differ from the reference program's by a relative error of at most 0.03.
Values may be sent and summed in bfloat16 or wider, within the bound.
No kernel may reach another device: no remote copies, remote signals or barrier semaphores. Data moves between devices by JAX's collectives and lax.ppermute only.
A program may use at most 64 MiB of HBM per device.

```python
import math
from functools import partial
import jax
import jax.numpy as jnp
from jax import lax

WIDTH = 128
HEADS = 4
FFN = 512
WINDOW = 8
LAT_ROWS = 256
LAT_COLS = 1024


def draw_latent(key, part):
    key = jax.random.fold_in(key, 5)
    key_base, key_rows, key_chan = jax.random.split(key, 3)
    row_scale = 0.3 * jnp.exp(jax.random.uniform(key_rows, (LAT_ROWS, LAT_COLS, 1), jnp.float32, 0.0, math.log(10.0)))
    chan_scale = 0.3 * jnp.exp(jax.random.uniform(key_chan, (1, 1, WIDTH), jnp.float32, 0.0, math.log(10.0)))
    drawn = jax.random.normal(key_base, (LAT_ROWS, LAT_COLS, WIDTH), jnp.float32)
    return jnp.clip(drawn * row_scale * chan_scale, -36.0, 36.0).astype(jnp.bfloat16)


def draw_attn_bias(key, part):
    key = jax.random.fold_in(key, 9)
    key_base = jax.random.fold_in(key, 0)
    positions = WINDOW * WINDOW
    shape_all = (2, HEADS, positions, positions)
    drawn = jnp.clip(jax.random.normal(key_base, shape_all, jnp.float32), -4.0, 4.0)
    return drawn


def block_scale(own_key, extent, pieces, least, largest):
    loudness, own = 1.0, jax.random.fold_in(own_key, 6)
    for position, blocks in pieces:
        heights = jnp.exp(jax.random.uniform(jax.random.fold_in(own, position), (blocks,), jnp.float32, least / len(pieces), largest / len(pieces)))
        loudness = loudness * jnp.repeat(heights, extent[position] // blocks).reshape([-1 if axis == position else 1 for axis in range(len(extent))])
    return loudness


def gaussian(own_key, shape, scale, most, shards=(), kind=jnp.bfloat16):
    entries = scale * jax.random.normal(own_key, shape, jnp.float32)
    if shards:
        entries = entries * block_scale(own_key, shape, shards, -0.22, 0.18)
    return jnp.clip(entries, -most, most).astype(kind)


def setup_inputs(seed: int = 0) -> dict:
    streams_of = jax.random.split(jax.random.key(seed), 9)
    return {
        "latent": draw_latent(jax.random.fold_in(streams_of[8], 71), 0),
        "cotangent": gaussian(streams_of[1], (LAT_ROWS, LAT_COLS, WIDTH), 1.0, 6.0, ((0, 32), (1, 8))),
        "w_qkv": gaussian(streams_of[2], (2, WIDTH, 3 * WIDTH), WIDTH ** -0.5, 0.5),
        "w_proj": gaussian(streams_of[3], (2, WIDTH, WIDTH), WIDTH ** -0.5, 0.5),
        "w_up": gaussian(streams_of[4], (2, WIDTH, FFN), WIDTH ** -0.5, 0.5),
        "w_down": gaussian(streams_of[5], (2, FFN, WIDTH), FFN ** -0.5, 0.25),
        "gains": jnp.clip(1.0 + 0.1 * jax.random.normal(streams_of[6], (2, 2, WIDTH), jnp.float32), 0.5, 1.5),
        "attn_bias": draw_attn_bias(jax.random.fold_in(streams_of[8], 71), 0),
    }


NORM_EPS = 1e-05

def norm(values, gain_vec):
    centre = values - lax.optimization_barrier(jnp.mean(values, axis=-1, keepdims=True))
    spread = lax.optimization_barrier(jnp.mean(centre * centre, axis=-1, keepdims=True))
    return centre * lax.rsqrt(spread + NORM_EPS) * gain_vec

def product(pattern, left_op, right_op):
    return jnp.einsum(pattern, left_op.astype(jnp.float32), right_op.astype(jnp.float32), precision=lax.Precision.HIGHEST)

def forward(inputs, w_qkv, w_proj, w_up, w_down, gain_attn, gain_mlp, bias):
    win_count, length, channels = inputs.shape
    head_count = bias.shape[0]
    head_size = channels // head_count
    score_scale = head_size ** (-0.5)
    stream = inputs.astype(jnp.float32)
    normed = norm(stream, gain_attn).astype(jnp.bfloat16)
    packed = product('wlc,cd->wld', normed, w_qkv).astype(jnp.bfloat16)
    queries = packed[..., :channels].reshape(win_count, length, head_count, head_size)
    key_rows = packed[..., channels:2 * channels].reshape(win_count, length, head_count, head_size)
    value_rows = packed[..., 2 * channels:].reshape(win_count, length, head_count, head_size)
    scores = product('wihd,wjhd->whij', queries, key_rows) * score_scale + bias
    probabilities = jax.nn.softmax(scores, axis=-1)
    weights = probabilities.astype(jnp.bfloat16)
    mixed_out = product('whij,wjhd->wihd', weights, value_rows).reshape(win_count, length, channels).astype(jnp.bfloat16)
    middle = (stream + product('wlc,cd->wld', mixed_out, w_proj)).astype(jnp.bfloat16)
    middle_f = middle.astype(jnp.float32)
    normed_two = norm(middle_f, gain_mlp).astype(jnp.bfloat16)
    hidden_pre = product('wlc,cf->wlf', normed_two, w_up)
    hidden = jax.nn.gelu(hidden_pre, approximate=True).astype(jnp.bfloat16)
    result = (middle_f + product('wlf,fc->wlc', hidden, w_down)).astype(jnp.bfloat16)
    stored = (stream, normed, queries, key_rows, value_rows, probabilities, weights, mixed_out, middle_f, normed_two, hidden_pre, hidden)
    return (result, stored)

def backward(stored, grad_out, w_qkv, w_proj, w_up, w_down, gain_attn, gain_mlp, bias):
    stream, normed, queries, key_rows, value_rows, probabilities, weights, mixed_out, middle_f, normed_two, hidden_pre, hidden = stored
    win_count, length, head_count, head_size = queries.shape
    channels = head_count * head_size
    score_scale = head_size ** (-0.5)
    grad_f = grad_out.astype(jnp.float32)
    d_hidden = product('wlc,fc->wlf', grad_out, w_down)
    g_down = product('wlf,wlc->fc', hidden, grad_out)
    _, gelu_pull = jax.vjp(partial(jax.nn.gelu, approximate=True), hidden_pre)
    d_pre = gelu_pull(d_hidden)[0].astype(jnp.bfloat16)
    g_up = product('wlc,wlf->cf', normed_two, d_pre)
    d_normed_two = product('wlf,cf->wlc', d_pre, w_up)
    _, pull_two = jax.vjp(norm, middle_f, gain_mlp)
    d_middle_part, g_gain_mlp = pull_two(d_normed_two)
    d_middle = grad_f + d_middle_part
    d_middle_b = d_middle.astype(jnp.bfloat16)
    g_proj = product('wlc,wld->cd', mixed_out, d_middle_b)
    d_mixed = product('wld,cd->wlc', d_middle_b, w_proj).astype(jnp.bfloat16).reshape(win_count, length, head_count, head_size)
    d_values = product('whij,wihd->wjhd', weights, d_mixed)
    d_weights = product('wihd,wjhd->whij', d_mixed, value_rows)
    d_scores = probabilities * (d_weights - lax.optimization_barrier(jnp.sum(d_weights * probabilities, axis=-1, keepdims=True)))
    g_bias = lax.optimization_barrier(jnp.sum(d_scores, axis=0))
    d_scores_b = d_scores.astype(jnp.bfloat16)
    d_queries = product('whij,wjhd->wihd', d_scores_b, key_rows) * score_scale
    d_keys = product('whij,wihd->wjhd', d_scores_b, queries) * score_scale
    d_packed = jnp.concatenate([d_queries.reshape(win_count, length, channels), d_keys.reshape(win_count, length, channels), d_values.reshape(win_count, length, channels)], axis=-1).astype(jnp.bfloat16)
    g_qkv = product('wlc,wld->cd', normed, d_packed)
    d_normed = product('wld,cd->wlc', d_packed, w_qkv)
    _, pull_one = jax.vjp(norm, stream, gain_attn)
    d_stream_part, g_gain_attn = pull_one(d_normed)
    d_input = (d_middle + d_stream_part).astype(jnp.bfloat16)
    return (d_input, (g_qkv, g_proj, g_up, g_down, g_gain_attn, g_gain_mlp, g_bias))

def reference(latent, cotangent, w_qkv, w_proj, w_up, w_down, gains, attn_bias):
    row_count, col_count, channels = latent.shape
    ffn_units = w_up.shape[2]
    half_win = WINDOW // 2
    band_count = row_count // WINDOW
    first_params = (w_qkv[0], w_proj[0], w_up[0], w_down[0], gains[0, 0], gains[0, 1], attn_bias[0])
    second_params = (w_qkv[1], w_proj[1], w_up[1], w_down[1], gains[1, 0], gains[1, 1], attn_bias[1])

    def split_band(band_rows):
        return band_rows.reshape(WINDOW, col_count // WINDOW, WINDOW, channels).transpose(1, 0, 2, 3).reshape(col_count // WINDOW, WINDOW * WINDOW, channels)

    def join_band(windows):
        return windows.reshape(col_count // WINDOW, WINDOW, WINDOW, channels).transpose(1, 0, 2, 3).reshape(WINDOW, col_count, channels)

    def as_bands(field):
        return field.reshape(band_count, WINDOW, col_count, channels)

    def first_step(carry, band_rows):
        result, _ = forward(split_band(band_rows), *first_params)
        return (carry, join_band(result))
    _, stacked = lax.scan(first_step, jnp.zeros((), jnp.float32), as_bands(latent))
    after_first = stacked.reshape(row_count, col_count, channels)
    moved_x = jnp.roll(after_first, (-half_win, -half_win), (0, 1))
    moved_g = jnp.roll(cotangent, (-half_win, -half_win), (0, 1))

    def grad_step(params):

        def scan_step(totals, inputs_pair):
            band_rows, grad_rows = inputs_pair
            _, stored = forward(split_band(band_rows), *params)
            d_input, grads = backward(stored, split_band(grad_rows), *params)
            return (tuple((left_sum + right_sum for left_sum, right_sum in zip(totals, grads))), join_band(d_input))
        return scan_step
    zero_grads = (jnp.zeros((channels, 3 * channels), jnp.float32), jnp.zeros((channels, channels), jnp.float32), jnp.zeros((channels, ffn_units), jnp.float32), jnp.zeros((ffn_units, channels), jnp.float32), jnp.zeros((channels,), jnp.float32), jnp.zeros((channels,), jnp.float32), jnp.zeros(attn_bias.shape[1:], jnp.float32))
    totals_two, d_moved = lax.scan(grad_step(second_params), zero_grads, (as_bands(moved_x), as_bands(moved_g)))
    d_after = jnp.roll(d_moved.reshape(row_count, col_count, channels), (half_win, half_win), (0, 1))
    totals_one, d_latent = lax.scan(grad_step(first_params), zero_grads, (as_bands(latent), as_bands(d_after)))
    gains_grad = jnp.stack([jnp.stack([totals_one[4], totals_one[5]]), jnp.stack([totals_two[4], totals_two[5]])])
    return (d_latent.reshape(row_count, col_count, channels), jnp.stack([totals_one[0], totals_two[0]]), jnp.stack([totals_one[1], totals_two[1]]), jnp.stack([totals_one[2], totals_two[2]]), jnp.stack([totals_one[3], totals_two[3]]), gains_grad, jnp.stack([totals_one[6], totals_two[6]]))
```

```python
import functools

import jax
import jax.numpy as jnp
from jax import lax
from jax.experimental import pallas as pl
from jax.experimental.pallas import tpu as pltpu
from jax.sharding import PartitionSpec as P

WIN = 8
HALF = 4
LEN = 64
CH = 128
HEADS = 4
FFN = 512
EPS = 1e-05
SCALE = (CH // HEADS) ** -0.5
F32 = jnp.float32
BF16 = jnp.bfloat16
VMEM_LIMIT = 32 * 1024 * 1024
FIRST_LIMIT = 55 * 1000 * 1000

ROW_QKV, ROW_PROJ, ROW_UP, ROW_DOWN, ROW_BIAS, ROW_GAIN, ROWS = 0, 384, 512, 1024, 1536, 1664, 1792
AXES = ("z", "yh", "core", "x", "yl")
PLANE = ("yh", "x", "yl")


def nn(a, b):
    return lax.dot_general(a, b, (((1,), (0,)), ((), ())), preferred_element_type=F32)


def nt(a, b):
    return lax.dot_general(a, b, (((1,), (1,)), ((), ())), preferred_element_type=F32)


def tn(a, b):
    return lax.dot_general(a, b, (((0,), (0,)), ((), ())), preferred_element_type=F32)


def lane_means(parts):
    width = len(parts) * CH
    block = lax.broadcasted_iota(jnp.int32, (width, width), 0) // CH == lax.broadcasted_iota(jnp.int32, (width, width), 1) // CH
    ones = (block.astype(F32) * (1.0 / CH)).astype(BF16)
    sums = nn(jnp.concatenate([p.astype(BF16) for p in parts], axis=1), ones)
    return [sums[:, CH * i : CH * (i + 1)] for i in range(len(parts))]


def normalise(v):
    centre = v - jnp.mean(v, axis=-1, keepdims=True)
    spread = jnp.mean(centre * centre, axis=-1, keepdims=True)
    inv = lax.rsqrt(spread + EPS)
    return centre * inv, inv


def normalise_back(dn, hat, inv, gain):
    d_hat = dn * gain
    mean, along = lane_means([d_hat, d_hat * hat])
    return inv * (d_hat - mean - hat * along)


def head_mask():
    rows = lax.broadcasted_iota(jnp.int32, (HEADS * LEN, CH), 0) // LEN
    lanes = lax.broadcasted_iota(jnp.int32, (HEADS * LEN, CH), 1) // (CH // HEADS)
    return (rows == lanes).astype(F32).astype(BF16)


def spread_heads(v, mask):
    return jnp.concatenate([v] * HEADS, axis=0) * mask


def gather_heads(v):
    lane = lax.broadcasted_iota(jnp.int32, (LEN, CH), 1)
    size = CH // HEADS
    out = v[3 * LEN :]
    for h in (2, 1, 0):
        out = jnp.where(lane < (h + 1) * size, v[h * LEN : (h + 1) * LEN], out)
    return out


def attention(qkv, bias_t, mask):
    q, k, v = qkv[:, :CH], qkv[:, CH : 2 * CH], qkv[:, 2 * CH :]
    scores = nt(k, spread_heads(q, mask)) * SCALE + bias_t
    top = jnp.max(scores, axis=0, keepdims=True)
    e = jnp.exp(scores - top)
    p = (e * (1.0 / jnp.sum(e, axis=0, keepdims=True))).astype(BF16)
    return gather_heads(tn(p, v)).astype(BF16), p


def attention_back(d_o, qkv, p, mask):
    q, k, v = qkv[:, :CH], qkv[:, CH : 2 * CH], qkv[:, 2 * CH :]
    do_spread = spread_heads(d_o, mask)
    dv = nn(p, do_spread)
    dp = nt(v, do_spread)
    pf = p.astype(F32)
    ds = pf * (dp - jnp.sum(dp * pf, axis=0, keepdims=True))
    dsb = ds.astype(BF16)
    dk = nn(dsb, spread_heads(q, mask)) * SCALE
    dq = gather_heads(tn(dsb, k)) * SCALE
    return jnp.concatenate([dq, dk, dv], axis=1).astype(BF16), ds


def gelu_and_slope(u):
    c = 0.7978845608028654
    sq = u * u
    s = 0.5 * jnp.tanh(u * (c + (c * 0.044715) * sq)) + 0.5
    m = u * s
    return m, s + m * (1.0 - s) * (2.0 * c + (6.0 * c * 0.044715) * sq)


def forward(x, w_qkv, w_proj, g1, g2, bias_t, mask):
    hat1, inv1 = normalise(x)
    a1 = (hat1 * g1).astype(BF16)
    qkv = nn(a1, w_qkv).astype(BF16)
    outs, weights = [], []
    for w in range(x.shape[0] // LEN):
        o, p = attention(qkv[w * LEN : (w + 1) * LEN], bias_t, mask)
        outs.append(o)
        weights.append(p)
    o = jnp.concatenate(outs, axis=0)
    h = (x + nn(o, w_proj)).astype(BF16).astype(F32)
    hat2, inv2 = normalise(h)
    a2 = (hat2 * g2).astype(BF16)
    return h, (hat1, inv1, a1, jnp.concatenate(weights, axis=0), o, hat2, inv2, a2), qkv


def backward(gy, kept, qkv, w_qkv, w_proj, w_up, w_down, g1, g2, mask):
    hat1, inv1, a1, p, o, hat2, inv2, a2 = kept
    m, slope = gelu_and_slope(nn(a2, w_up))
    m = m.astype(BF16)
    du = (nt(gy, w_down) * slope).astype(BF16)
    da2 = nt(du, w_up)
    gain2 = jnp.sum(da2 * hat2, axis=0, keepdims=True)
    dh = gy.astype(F32) + normalise_back(da2, hat2, inv2, g2)
    dhb = dh.astype(BF16)
    d_o = nt(dhb, w_proj).astype(BF16)
    parts, bias = [], None
    for w in range(gy.shape[0] // LEN):
        at = slice(w * LEN, (w + 1) * LEN)
        part, ds = attention_back(d_o[at], qkv[at], p[at], mask)
        parts.append(part)
        bias = ds if bias is None else bias + ds
    dqkv = jnp.concatenate(parts, axis=0)
    da1 = nt(dqkv, w_qkv)
    gain1 = jnp.sum(da1 * hat1, axis=0, keepdims=True)
    dx = dh + normalise_back(da1, hat1, inv1, g1)
    return dx, (gy, m, a2, du, o, dhb, a1, dqkv), bias, gain1, gain2


def pack(pack_ref, pairs, bias, gain1, gain2):
    gy, m, a2, du, o, dhb, a1, dqkv = pairs
    down, up, qkv = tn(gy, m), tn(a2, du), tn(a1, dqkv)
    for j in range(3):
        pack_ref[ROW_QKV + CH * j : ROW_QKV + CH * (j + 1)] = qkv[:, CH * j : CH * (j + 1)]
    pack_ref[ROW_PROJ : ROW_PROJ + CH] = tn(o, dhb)
    for j in range(4):
        pack_ref[ROW_UP + CH * j : ROW_UP + CH * (j + 1)] = up[:, CH * j : CH * (j + 1)]
        pack_ref[ROW_DOWN + CH * j : ROW_DOWN + CH * (j + 1)] = down[:, CH * j : CH * (j + 1)].T
    pack_ref[ROW_BIAS : ROW_BIAS + LEN] = bias[:, :CH]
    pack_ref[ROW_BIAS + LEN : ROW_BIAS + 2 * LEN] = bias[:, CH:]
    pack_ref[ROW_GAIN : ROW_GAIN + 1] = gain1
    pack_ref[ROW_GAIN + 1 : ROW_GAIN + 2] = gain2
    pack_ref[ROW_GAIN + 2 :] = jnp.zeros((ROWS - ROW_GAIN - 2, CH), F32)


def to_windows(tile):
    rows, cols, ch = tile.shape
    return tile.reshape(WIN, cols // WIN, WIN, ch).transpose(1, 0, 2, 3).reshape(-1, ch)


def from_windows(tokens):
    count = tokens.shape[0] // LEN
    return tokens.reshape(count, WIN, WIN, CH).transpose(1, 0, 2, 3).reshape(WIN, count * WIN, CH)


def turned_bias(bias):
    return jnp.concatenate([bias[h].T for h in range(HEADS)], axis=1)


def first_kernel(*refs):
    (latent_hbm, bias_hbm), weights_hbm, refs = refs[:2], refs[2:7], refs[7:]
    (top_ref, low_ref), kept_refs, refs = refs[:2], refs[2:10], refs[10:]
    (x_ref, bias_ref, sem), weight_refs = refs[:3], refs[3:]
    w_qkv_ref, w_proj_ref, w_up_ref, w_down_ref, gain_ref = weight_refs
    moves = [(latent_hbm, x_ref), (bias_hbm.at[0], bias_ref)]
    moves += [(source.at[0], target) for source, target in zip(weights_hbm, weight_refs)]
    copies = [pltpu.make_async_copy(source, target, sem.at[i]) for i, (source, target) in enumerate(moves)]
    for copy in copies:
        copy.start()
    mask = head_mask()
    for copy in copies:
        copy.wait()
    x = to_windows(x_ref[...].astype(F32))
    h, kept, _ = forward(
        x, w_qkv_ref[...], w_proj_ref[...], gain_ref[0:1], gain_ref[1:2], turned_bias(bias_ref), mask
    )
    for ref, value in zip(kept_refs, kept):
        ref[...] = jnp.broadcast_to(value, ref.shape).astype(ref.dtype)
    m, _ = gelu_and_slope(nn(kept[7], w_up_ref[...]))
    tile = from_windows(h + nn(m.astype(BF16), w_down_ref[...]))
    top_ref[...] = tile[:HALF].astype(BF16)
    low_ref[...] = tile[HALF:].astype(BF16)


def second_kernel(*refs):
    x_own_ref, x_low_ref, g_own_ref, g_low_ref, edge_ref = refs[:5]
    w_qkv_ref, w_proj_ref, w_up_ref, w_down_ref, gain_ref, bias_ref = refs[5:11]
    (dtop_ref, dlow_ref), pair_refs, (bias_out_ref, gain_out_ref, frame_ref) = refs[11:13], refs[13:21], refs[21:]
    cols = x_own_ref.shape[1]

    def shifted(own, low, right):
        frame_ref[0:HALF, 0:cols] = own[...].astype(F32)
        frame_ref[HALF:, 0:cols] = low[...].astype(F32)
        frame_ref[:, cols : cols + WIN] = right.astype(F32)
        return to_windows(frame_ref[:, HALF : HALF + cols])

    mask = head_mask()
    x = shifted(x_own_ref, x_low_ref, edge_ref[0:WIN])
    gy = shifted(g_own_ref, g_low_ref, edge_ref[WIN:]).astype(BF16)
    w_qkv, w_proj, w_up, g1, g2 = w_qkv_ref[1], w_proj_ref[1], w_up_ref[1], gain_ref[1, 0:1], gain_ref[1, 1:2]
    _, kept, qkv = forward(x, w_qkv, w_proj, g1, g2, turned_bias(bias_ref[1]), mask)
    dx, pairs, bias, gain1, gain2 = backward(gy, kept, qkv, w_qkv, w_proj, w_up, w_down_ref[1], g1, g2, mask)
    for ref, value in zip(pair_refs, pairs):
        ref[...] = value
    bias_out_ref[...] = bias
    gain_out_ref[0:1] = gain1
    gain_out_ref[1:2] = gain2
    tile = from_windows(dx)
    dtop_ref[...] = tile[:HALF].astype(BF16)
    dlow_ref[...] = tile[HALF:].astype(BF16)


def weights_kernel(*refs):
    pairs, (bias_ref, gain_ref, pack_ref) = refs[:8], refs[8:]
    pack(pack_ref, [ref[...] for ref in pairs], bias_ref[...], gain_ref[0:1], gain_ref[1:2])


def last_kernel(*refs):
    (own, above, left), kept_refs, refs = refs[:3], refs[3:11], refs[11:]
    w_qkv_ref, w_proj_ref, w_up_ref, w_down_ref, gain_ref, other_ref, core_ref = refs[:7]
    dx_ref, keep_ref, send_ref, frame_ref, pack_ref = refs[7:]
    cols = own.shape[1]
    frame_ref[:, 0:WIN] = left[...].astype(F32)
    first = frame_ref[:, HALF:WIN]
    frame_ref[:, 0:HALF] = first
    frame_ref[HALF:, HALF : HALF + cols] = own[...].astype(F32)
    frame_ref[0:HALF, HALF : HALF + cols] = above[...].astype(F32)
    gy = to_windows(frame_ref[:, 0:cols]).astype(BF16)
    kept = [ref[...].astype(F32) if i in (0, 1, 5, 6) else ref[...] for i, ref in enumerate(kept_refs)]
    g1, g2 = gain_ref[0, 0:1], gain_ref[0, 1:2]
    dx, pairs, bias, gain1, gain2 = backward(
        gy, kept, nn(kept[2], w_qkv_ref[0]).astype(BF16), w_qkv_ref[0], w_proj_ref[0], w_up_ref[0], w_down_ref[0], g1, g2, head_mask()
    )
    dx_ref[...] = from_windows(dx).astype(BF16)
    pack(pack_ref, pairs, bias, gain1, gain2)
    first_core = core_ref[0] == 0

    @pl.when(first_core)
    def _():
        keep_ref[...] = pack_ref[...]
        send_ref[...] = other_ref[...].astype(BF16)

    @pl.when(jnp.logical_not(first_core))
    def _():
        keep_ref[...] = other_ref[...]
        send_ref[...] = pack_ref[...].astype(BF16)


def unpack_kernel(core_ref, own_ref, other_ref, *refs):
    qkv_ref, proj_ref, up_ref, down_ref, gain_ref, bias_ref, whole_ref = refs
    at = pl.multiple_of(core_ref[0] * ROWS, ROWS)
    whole_ref[pl.ds(at, ROWS)] = own_ref[...].astype(F32)
    whole_ref[pl.ds(ROWS - at, ROWS)] = other_ref[...].astype(F32)
    for b in range(2):
        at = b * ROWS
        for j in range(3):
            qkv_ref[b, :, CH * j : CH * (j + 1)] = whole_ref[at + ROW_QKV + CH * j : at + ROW_QKV + CH * (j + 1)]
        proj_ref[b] = whole_ref[at + ROW_PROJ : at + ROW_PROJ + CH]
        for j in range(4):
            up_ref[b, :, CH * j : CH * (j + 1)] = whole_ref[at + ROW_UP + CH * j : at + ROW_UP + CH * (j + 1)]
        down_ref[b] = whole_ref[at + ROW_DOWN : at + ROW_DOWN + FFN]
        for j in range(2):
            turned = whole_ref[at + ROW_BIAS + LEN * j : at + ROW_BIAS + LEN * (j + 1)].T
            bias_ref[b, 2 * j] = turned[:LEN]
            bias_ref[b, 2 * j + 1] = turned[LEN:]
        gain_ref[b] = whole_ref[at + ROW_GAIN : at + ROW_GAIN + 2]


def vmem(count):
    return [pl.BlockSpec(memory_space=pltpu.VMEM)] * count


def cost(flops, moved):
    return pl.CostEstimate(flops=flops, bytes_accessed=moved, transcendentals=0)


def shift(value, down, right):
    tall, wide = 32, 8
    pairs = []
    for r in range(tall):
        for c in range(wide):
            pairs.append((r * wide + c, (r + down) % tall * wide + (c + right) % wide))
    return lax.ppermute(value, AXES, pairs)


def swap_core(value):
    return lax.ppermute(value, "core", [(0, 1), (1, 0)])


def scatter_sum(value, axis, count):
    pieces = value.astype(BF16).reshape(count, value.shape[0] // count, CH)
    return jnp.sum(lax.all_to_all(pieces, axis, 0, 0).astype(F32), axis=0)


def collect(value, axis, count):
    spread = jnp.broadcast_to(value[None], (count, *value.shape))
    return lax.all_to_all(spread, axis, 0, 0)


def sum_over_devices(keep, send):
    total = keep + swap_core(send).astype(F32)
    total = scatter_sum(total, PLANE, 16)
    total = jnp.sum(collect(total.astype(BF16), "z", 8).astype(F32), axis=0).astype(BF16)
    total = collect(total, PLANE, 16).reshape(ROWS, CH)
    return total, swap_core(total)


def body(latent, cotangent, w_qkv, w_proj, w_up, w_down, gains, attn_bias):
    cols = latent.shape[1]
    half = jax.ShapeDtypeStruct((HALF, cols, CH), BF16)
    params = pltpu.CompilerParams(vmem_limit_bytes=VMEM_LIMIT)
    packed = jax.ShapeDtypeStruct((ROWS, CH), F32)
    core = lax.axis_index("core").reshape(1)
    weights = (w_qkv, w_proj, w_up, w_down, gains)
    g_low = cotangent[HALF:]
    g_below = shift(cotangent[:HALF], -1, 0)
    tokens = WIN * cols

    def table(width):
        return jax.ShapeDtypeStruct((tokens, width), BF16)

    kept_shapes = [table(CH), table(CH), table(CH), table(HEADS * LEN), table(CH)]
    kept_shapes += [table(CH), table(CH), table(CH)]
    pair_shapes = [table(CH), table(FFN), table(CH), table(FFN), table(CH), table(CH), table(CH), table(3 * CH)]
    top, low, *kept = pl.pallas_call(
        first_kernel,
        out_shape=(half, half, *kept_shapes),
        in_specs=[pl.BlockSpec(memory_space=pltpu.HBM)] * 7,
        out_specs=vmem(10),
        scratch_shapes=[
            pltpu.VMEM(latent.shape, BF16),
            pltpu.VMEM(attn_bias.shape[1:], F32),
            pltpu.SemaphoreType.DMA((7,)),
        ]
        + [pltpu.VMEM(w.shape[1:], w.dtype) for w in weights],
        compiler_params=pltpu.CompilerParams(vmem_limit_bytes=FIRST_LIMIT),
        cost_estimate=cost(500_000_000, 1_500_000),
        name="forward_first",
    )(latent, attn_bias, *weights)
    top, g_below = lax.optimization_barrier((top, g_below))
    x_below = shift(top, -1, 0)
    edge = jnp.concatenate([v[:, :WIN] for v in (low, x_below, g_low, g_below)], axis=0)
    edge = shift(edge, 0, -1)
    frame = pltpu.VMEM((WIN, cols + 2 * WIN, CH), F32)
    d_top, d_low, *pairs = pl.pallas_call(
        second_kernel,
        out_shape=(
            half,
            half,
            *pair_shapes,
            jax.ShapeDtypeStruct((LEN, HEADS * LEN), F32),
            jax.ShapeDtypeStruct((2, CH), F32),
        ),
        in_specs=vmem(11),
        out_specs=vmem(12),
        scratch_shapes=[frame],
        compiler_params=params,
        cost_estimate=cost(1_500_000_000, 3_000_000),
        name="backward_second",
    )(low, x_below, g_low, g_below, edge, *weights, attn_bias)
    pack_two = pl.pallas_call(
        weights_kernel,
        out_shape=packed,
        in_specs=vmem(10),
        out_specs=vmem(1)[0],
        compiler_params=params,
        cost_estimate=cost(500_000_000, 5_000_000),
        name="weights_second",
    )(*pairs)
    d_above = shift(d_low, 1, 0)
    d_above, pack_two = lax.optimization_barrier((d_above, pack_two))
    d_left = shift(jnp.concatenate([v[:, cols - WIN :] for v in (d_above, d_top)], axis=0), 0, 1)
    dx, keep, send = pl.pallas_call(
        last_kernel,
        out_shape=(
            jax.ShapeDtypeStruct(latent.shape, BF16),
            packed,
            jax.ShapeDtypeStruct((ROWS, CH), BF16),
        ),
        in_specs=vmem(17) + [pl.BlockSpec(memory_space=pltpu.SMEM)],
        out_specs=vmem(3),
        scratch_shapes=[frame, pltpu.VMEM((ROWS, CH), F32)],
        compiler_params=params,
        cost_estimate=cost(1_500_000_000, 4_000_000),
        name="backward_first",
    )(d_top, d_above, d_left, *kept, *weights, pack_two, core)
    parts = sum_over_devices(keep, send)
    qkv, proj, up, down, gain, bias = pl.pallas_call(
        unpack_kernel,
        out_shape=(
            jax.ShapeDtypeStruct((2, CH, 3 * CH), F32),
            jax.ShapeDtypeStruct((2, CH, CH), F32),
            jax.ShapeDtypeStruct((2, CH, FFN), F32),
            jax.ShapeDtypeStruct((2, FFN, CH), F32),
            jax.ShapeDtypeStruct((2, 2, CH), F32),
            jax.ShapeDtypeStruct((2, HEADS, LEN, LEN), F32),
        ),
        in_specs=[pl.BlockSpec(memory_space=pltpu.SMEM)] + vmem(2),
        out_specs=vmem(6),
        scratch_shapes=[pltpu.VMEM((2 * ROWS, CH), F32)],
        compiler_params=params,
        cost_estimate=cost(1_000_000, 4_000_000),
        name="unpack",
    )(core, *parts)
    return dx, qkv, proj, up, down, gain, bias


def solution(mesh):
    fine = jax.sharding.Mesh(mesh.devices.reshape(8, 2, 2, 4, 2), AXES)
    tiles = P(("z", "yh", "core"), ("x", "yl"), None)
    in_specs = (tiles, tiles, P(), P(), P(), P(), P(), P())
    out_specs = (tiles, P(), P(), P(), P(), P(), P())
    return jax.shard_map(body, mesh=fine, in_specs=in_specs, out_specs=out_specs, check_vma=False)
```

```python
import functools

import jax
import jax.numpy as jnp
from jax import lax
from jax.experimental import pallas as pl
from jax.experimental.pallas import tpu as pltpu
from jax.sharding import PartitionSpec as P

WIN = 8
HALF = 4
LEN = 64
CH = 128
HEADS = 4
FFN = 512
EPS = 1e-05
SCALE = (CH // HEADS) ** -0.5
F32 = jnp.float32
BF16 = jnp.bfloat16
VMEM_LIMIT = 32 * 1024 * 1024
FIRST_LIMIT = 57 * 1000 * 1000

ROW_QKV, ROW_PROJ, ROW_UP, ROW_DOWN, ROW_BIAS, ROW_GAIN, ROWS = 0, 384, 512, 1024, 1536, 1664, 1792
AXES = ("z", "yh", "core", "x", "yl")
PLANE = ("yh", "x", "yl")


def nn(a, b):
    return lax.dot_general(a, b, (((1,), (0,)), ((), ())), preferred_element_type=F32)


def nt(a, b):
    return lax.dot_general(a, b, (((1,), (1,)), ((), ())), preferred_element_type=F32)


def tn(a, b):
    return lax.dot_general(a, b, (((0,), (0,)), ((), ())), preferred_element_type=F32)


def lane_means(parts):
    width = len(parts) * CH
    block = lax.broadcasted_iota(jnp.int32, (width, width), 0) // CH == lax.broadcasted_iota(jnp.int32, (width, width), 1) // CH
    ones = (block.astype(F32) * (1.0 / CH)).astype(BF16)
    sums = nn(jnp.concatenate([p.astype(BF16) for p in parts], axis=1), ones)
    return [sums[:, CH * i : CH * (i + 1)] for i in range(len(parts))]


def normalise(v):
    centre = v - jnp.mean(v, axis=-1, keepdims=True)
    spread = jnp.mean(centre * centre, axis=-1, keepdims=True)
    inv = lax.rsqrt(spread + EPS)
    return centre * inv, inv


def normalise_back(dn, hat, inv, gain):
    d_hat = dn * gain
    mean, along = lane_means([d_hat, d_hat * hat])
    return inv * (d_hat - mean - hat * along)


def head_mask():
    rows = lax.broadcasted_iota(jnp.int32, (HEADS * LEN, CH), 0) // LEN
    lanes = lax.broadcasted_iota(jnp.int32, (HEADS * LEN, CH), 1) // (CH // HEADS)
    return (rows == lanes).astype(F32).astype(BF16)


def spread_heads(v, mask):
    return jnp.concatenate([v] * HEADS, axis=0) * mask


def gather_heads(v):
    lane = lax.broadcasted_iota(jnp.int32, (LEN, CH), 1)
    size = CH // HEADS
    out = v[3 * LEN :]
    for h in (2, 1, 0):
        out = jnp.where(lane < (h + 1) * size, v[h * LEN : (h + 1) * LEN], out)
    return out


def attention(qkv, bias_t, mask):
    q, k, v = qkv[:, :CH], qkv[:, CH : 2 * CH], qkv[:, 2 * CH :]
    scores = nt(k, spread_heads(q, mask)) * SCALE + bias_t
    top = jnp.max(scores, axis=0, keepdims=True)
    e = jnp.exp(scores - top)
    p = (e * (1.0 / jnp.sum(e, axis=0, keepdims=True))).astype(BF16)
    return gather_heads(tn(p, v)).astype(BF16), p


def attention_back(d_o, qkv, p, mask):
    q, k, v = qkv[:, :CH], qkv[:, CH : 2 * CH], qkv[:, 2 * CH :]
    do_spread = spread_heads(d_o, mask)
    dv = nn(p, do_spread)
    dp = nt(v, do_spread)
    pf = p.astype(F32)
    ds = pf * (dp - jnp.sum(dp * pf, axis=0, keepdims=True))
    dsb = ds.astype(BF16)
    dk = nn(dsb, spread_heads(q, mask)) * SCALE
    dq = gather_heads(tn(dsb, k)) * SCALE
    return jnp.concatenate([dq, dk, dv], axis=1).astype(BF16), ds


def gelu_and_slope(u):
    c = 0.7978845608028654
    sq = u * u
    s = 0.5 * jnp.tanh(u * (c + (c * 0.044715) * sq)) + 0.5
    m = u * s
    return m, s + m * (1.0 - s) * (2.0 * c + (6.0 * c * 0.044715) * sq)


def forward(x, w_qkv, w_proj, g1, g2, bias_t, mask):
    hat1, inv1 = normalise(x)
    a1 = (hat1 * g1).astype(BF16)
    qkv = nn(a1, w_qkv).astype(BF16)
    outs, weights = [], []
    for w in range(x.shape[0] // LEN):
        o, p = attention(qkv[w * LEN : (w + 1) * LEN], bias_t, mask)
        outs.append(o)
        weights.append(p)
    o = jnp.concatenate(outs, axis=0)
    h = (x + nn(o, w_proj)).astype(BF16).astype(F32)
    hat2, inv2 = normalise(h)
    a2 = (hat2 * g2).astype(BF16)
    return h, (hat1, inv1, a1, jnp.concatenate(weights, axis=0), o, hat2, inv2, a2), qkv


def backward(gy, kept, qkv, w_qkv, w_proj, w_up, w_down, g1, g2, mask):
    hat1, inv1, a1, p, o, hat2, inv2, a2 = kept
    m, slope = gelu_and_slope(nn(a2, w_up))
    m = m.astype(BF16)
    du = (nt(gy, w_down) * slope).astype(BF16)
    da2 = nt(du, w_up)
    gain2 = jnp.sum(da2 * hat2, axis=0, keepdims=True)
    dh = gy.astype(F32) + normalise_back(da2, hat2, inv2, g2)
    dhb = dh.astype(BF16)
    d_o = nt(dhb, w_proj).astype(BF16)
    parts, bias = [], None
    for w in range(gy.shape[0] // LEN):
        at = slice(w * LEN, (w + 1) * LEN)
        part, ds = attention_back(d_o[at], qkv[at], p[at], mask)
        parts.append(part)
        bias = ds if bias is None else bias + ds
    dqkv = jnp.concatenate(parts, axis=0)
    da1 = nt(dqkv, w_qkv)
    gain1 = jnp.sum(da1 * hat1, axis=0, keepdims=True)
    dx = dh + normalise_back(da1, hat1, inv1, g1)
    return dx, (gy, m, a2, du, o, dhb, a1, dqkv), bias, gain1, gain2


def pack(pack_ref, pairs, bias, gain1, gain2):
    gy, m, a2, du, o, dhb, a1, dqkv = pairs
    down, up, qkv = tn(gy, m), tn(a2, du), tn(a1, dqkv)
    for j in range(3):
        pack_ref[ROW_QKV + CH * j : ROW_QKV + CH * (j + 1)] = qkv[:, CH * j : CH * (j + 1)]
    pack_ref[ROW_PROJ : ROW_PROJ + CH] = tn(o, dhb)
    for j in range(4):
        pack_ref[ROW_UP + CH * j : ROW_UP + CH * (j + 1)] = up[:, CH * j : CH * (j + 1)]
        pack_ref[ROW_DOWN + CH * j : ROW_DOWN + CH * (j + 1)] = down[:, CH * j : CH * (j + 1)].T
    pack_ref[ROW_BIAS : ROW_BIAS + LEN] = bias[:, :CH]
    pack_ref[ROW_BIAS + LEN : ROW_BIAS + 2 * LEN] = bias[:, CH:]
    pack_ref[ROW_GAIN : ROW_GAIN + 1] = gain1
    pack_ref[ROW_GAIN + 1 : ROW_GAIN + 2] = gain2
    pack_ref[ROW_GAIN + 2 :] = jnp.zeros((ROWS - ROW_GAIN - 2, CH), F32)


def to_windows(tile):
    rows, cols, ch = tile.shape
    return tile.reshape(WIN, cols // WIN, WIN, ch).transpose(1, 0, 2, 3).reshape(-1, ch)


def from_windows(tokens):
    count = tokens.shape[0] // LEN
    return tokens.reshape(count, WIN, WIN, CH).transpose(1, 0, 2, 3).reshape(WIN, count * WIN, CH)


def turned_bias(bias):
    return jnp.concatenate([bias[h].T for h in range(HEADS)], axis=1)


def first_half(x, w_qkv, w_proj, w_up, w_down, gain_ref, bias, top_ref, low_ref):
    h, kept, _ = forward(to_windows(x.astype(F32)), w_qkv, w_proj, gain_ref[0:1], gain_ref[1:2], turned_bias(bias), head_mask())
    m, _ = gelu_and_slope(nn(kept[7], w_up))
    tile = from_windows(h + nn(m.astype(BF16), w_down))
    top_ref[...] = tile[:HALF].astype(BF16)
    low_ref[...] = tile[HALF:].astype(BF16)


def first_kernel(*refs):
    (latent_hbm, bias_hbm), weights_hbm, refs = refs[:2], refs[2:7], refs[7:]
    (top_ref, low_ref), refs = refs[:2], refs[2:]
    (x_ref, bias_ref, sem), weight_refs = refs[:3], refs[3:]
    w_qkv_ref, w_proj_ref, w_up_ref, w_down_ref, gain_ref = weight_refs
    wide = latent_hbm.shape[1] // 2
    moves = [(latent_hbm.at[:, 0:wide], x_ref), (bias_hbm.at[0], bias_ref)]
    moves += [(source.at[0], target) for source, target in zip(weights_hbm, weight_refs)]
    copies = [pltpu.make_async_copy(source, target, sem.at[i]) for i, (source, target) in enumerate(moves)]
    for copy in copies:
        copy.start()
    for copy in copies:
        copy.wait()
    weights = (w_qkv_ref[...], w_proj_ref[...], w_up_ref[...], w_down_ref[...])
    first_half(x_ref[...], *weights, gain_ref, bias_ref, top_ref, low_ref)


def next_kernel(x_ref, w_qkv_ref, w_proj_ref, w_up_ref, w_down_ref, gain_ref, bias_ref, top_ref, low_ref):
    wide = x_ref.shape[1] // 2
    weights = (w_qkv_ref[0], w_proj_ref[0], w_up_ref[0], w_down_ref[0])
    first_half(x_ref[:, wide:], *weights, gain_ref.at[0], bias_ref.at[0], top_ref, low_ref)


def keep_kernel(part, x_ref, w_qkv_ref, w_proj_ref, gain_ref, bias_ref, *kept_refs):
    wide = x_ref.shape[1] // 2
    x = to_windows(x_ref[:, part * wide : (part + 1) * wide].astype(F32))
    g1, g2 = gain_ref[0, 0:1], gain_ref[0, 1:2]
    _, kept, _ = forward(x, w_qkv_ref[0], w_proj_ref[0], g1, g2, turned_bias(bias_ref[0]), head_mask())
    for ref, value in zip(kept_refs, kept):
        ref[...] = jnp.broadcast_to(value, ref.shape).astype(ref.dtype)


def second_half(x, gy, w_qkv_ref, w_proj_ref, w_up_ref, w_down_ref, gain_ref, bias_ref):
    mask = head_mask()
    w_qkv, w_proj, w_up, g1, g2 = w_qkv_ref[1], w_proj_ref[1], w_up_ref[1], gain_ref[1, 0:1], gain_ref[1, 1:2]
    _, kept, qkv = forward(to_windows(x), w_qkv, w_proj, g1, g2, turned_bias(bias_ref[1]), mask)
    return backward(to_windows(gy).astype(BF16), kept, qkv, w_qkv, w_proj, w_up, w_down_ref[1], g1, g2, mask)


def second_kernel(*refs):
    low_ref, below_ref, g_own_ref, g_below_ref = refs[:4]
    weights, (dx_ref, *pair_refs), (bias_out_ref, gain_out_ref, frame_ref) = refs[4:10], refs[10:19], refs[19:]
    wide = low_ref.shape[1]
    frame_ref[0:HALF, 0:wide] = low_ref[...].astype(F32)
    frame_ref[HALF:, 0:wide] = below_ref[...].astype(F32)
    x = frame_ref[:, HALF : wide - HALF]
    frame_ref[0:HALF, 0:wide] = g_own_ref[HALF:, 0:wide].astype(F32)
    frame_ref[HALF:, 0:wide] = g_below_ref[0:HALF, 0:wide].astype(F32)
    gy = frame_ref[:, HALF : wide - HALF]
    dx, pairs, bias, gain1, gain2 = second_half(x, gy, *weights)
    dx_ref[...] = dx
    for ref, value in zip(pair_refs, pairs):
        ref[...] = value
    bias_out_ref[...] = bias
    gain_out_ref[0:1] = gain1
    gain_out_ref[1:2] = gain2


def third_kernel(*refs):
    low_a_ref, low_b_ref, below_a_ref, below_b_ref, g_own_ref, g_below_ref, edge_ref = refs[:7]
    weights, (dx_ref, bias_ref, gain_ref) = refs[7:13], refs[13:16]
    (dtop_ref, dlow_ref), pair_refs, (bias_out_ref, gain_out_ref, frame_ref) = refs[16:18], refs[18:26], refs[26:]
    wide, cols = low_a_ref.shape[1], g_own_ref.shape[1]
    span = cols - wide + WIN
    frame_ref[0:HALF, 0:WIN] = low_a_ref[:, wide - WIN :].astype(F32)
    frame_ref[HALF:, 0:WIN] = below_a_ref[:, wide - WIN :].astype(F32)
    frame_ref[0:HALF, WIN:span] = low_b_ref[...].astype(F32)
    frame_ref[HALF:, WIN:span] = below_b_ref[...].astype(F32)
    frame_ref[:, span : span + WIN] = edge_ref[0:WIN].astype(F32)
    x = frame_ref[:, HALF : span + HALF]
    frame_ref[0:HALF, 0:span] = g_own_ref[HALF:, wide - WIN :].astype(F32)
    frame_ref[HALF:, 0:span] = g_below_ref[0:HALF, wide - WIN :].astype(F32)
    frame_ref[:, span : span + WIN] = edge_ref[WIN:].astype(F32)
    gy = frame_ref[:, HALF : span + HALF]
    dx, pairs, bias, gain1, gain2 = second_half(x, gy, *weights)
    for ref, value in zip(pair_refs, pairs):
        ref[...] = value
    bias_out_ref[...] = bias_ref[...] + bias
    gain_out_ref[0:1] = gain_ref[0:1] + gain1
    gain_out_ref[1:2] = gain_ref[1:2] + gain2
    tile = from_windows(jnp.concatenate([dx_ref[...], dx], axis=0))
    dtop_ref[...] = tile[:HALF].astype(BF16)
    dlow_ref[...] = tile[HALF:].astype(BF16)


def weights_kernel(*refs):
    first, second, (bias_ref, gain_ref, pack_ref) = refs[:8], refs[8:16], refs[16:]
    pairs = [jnp.concatenate([a[...], b[...]], axis=0) for a, b in zip(first, second)]
    pack(pack_ref, pairs, bias_ref[...], gain_ref[0:1], gain_ref[1:2])


def last_kernel(*refs):
    (own, above, left), kept_refs, refs = refs[:3], refs[3:19], refs[19:]
    w_qkv_ref, w_proj_ref, w_up_ref, w_down_ref, gain_ref, other_ref, core_ref = refs[:7]
    dx_ref, keep_ref, send_ref, frame_ref, pack_ref = refs[7:]
    cols = own.shape[1]
    frame_ref[:, 0:WIN] = left[...].astype(F32)
    first = frame_ref[:, HALF:WIN]
    frame_ref[:, 0:HALF] = first
    frame_ref[HALF:, HALF : HALF + cols] = own[...].astype(F32)
    frame_ref[0:HALF, HALF : HALF + cols] = above[...].astype(F32)
    gy = to_windows(frame_ref[:, 0:cols]).astype(BF16)
    kept = [jnp.concatenate([a[...], b[...]], axis=0) for a, b in zip(kept_refs[:8], kept_refs[8:])]
    kept = [v.astype(F32) if i in (0, 1, 5, 6) else v for i, v in enumerate(kept)]
    g1, g2 = gain_ref[0, 0:1], gain_ref[0, 1:2]
    dx, pairs, bias, gain1, gain2 = backward(
        gy, kept, nn(kept[2], w_qkv_ref[0]).astype(BF16), w_qkv_ref[0], w_proj_ref[0], w_up_ref[0], w_down_ref[0], g1, g2, head_mask()
    )
    dx_ref[...] = from_windows(dx).astype(BF16)
    pack(pack_ref, pairs, bias, gain1, gain2)
    first_core = core_ref[0] == 0

    @pl.when(first_core)
    def _():
        keep_ref[...] = pack_ref[...]
        send_ref[...] = other_ref[...].astype(BF16)

    @pl.when(jnp.logical_not(first_core))
    def _():
        keep_ref[...] = other_ref[...]
        send_ref[...] = pack_ref[...].astype(BF16)


def unpack_kernel(core_ref, own_ref, other_ref, *refs):
    qkv_ref, proj_ref, up_ref, down_ref, gain_ref, bias_ref, whole_ref = refs
    at = pl.multiple_of(core_ref[0] * ROWS, ROWS)
    whole_ref[pl.ds(at, ROWS)] = own_ref[...].astype(F32)
    whole_ref[pl.ds(ROWS - at, ROWS)] = other_ref[...].astype(F32)
    for b in range(2):
        at = b * ROWS
        for j in range(3):
            qkv_ref[b, :, CH * j : CH * (j + 1)] = whole_ref[at + ROW_QKV + CH * j : at + ROW_QKV + CH * (j + 1)]
        proj_ref[b] = whole_ref[at + ROW_PROJ : at + ROW_PROJ + CH]
        for j in range(4):
            up_ref[b, :, CH * j : CH * (j + 1)] = whole_ref[at + ROW_UP + CH * j : at + ROW_UP + CH * (j + 1)]
        down_ref[b] = whole_ref[at + ROW_DOWN : at + ROW_DOWN + FFN]
        for j in range(2):
            turned = whole_ref[at + ROW_BIAS + LEN * j : at + ROW_BIAS + LEN * (j + 1)].T
            bias_ref[b, 2 * j] = turned[:LEN]
            bias_ref[b, 2 * j + 1] = turned[LEN:]
        gain_ref[b] = whole_ref[at + ROW_GAIN : at + ROW_GAIN + 2]


def vmem(count):
    return [pl.BlockSpec(memory_space=pltpu.VMEM)] * count


def cost(flops, moved):
    return pl.CostEstimate(flops=flops, bytes_accessed=moved, transcendentals=0)


def shift(value, down, right):
    tall, wide = 32, 8
    pairs = []
    for r in range(tall):
        for c in range(wide):
            pairs.append((r * wide + c, (r + down) % tall * wide + (c + right) % wide))
    return lax.ppermute(value, AXES, pairs)


def swap_core(value):
    return lax.ppermute(value, "core", [(0, 1), (1, 0)])


def scatter_sum(value, axis, count):
    pieces = value.astype(BF16).reshape(count, value.shape[0] // count, CH)
    return jnp.sum(lax.all_to_all(pieces, axis, 0, 0).astype(F32), axis=0)


def collect(value, axis, count):
    spread = jnp.broadcast_to(value[None], (count, *value.shape))
    return lax.all_to_all(spread, axis, 0, 0)


def sum_over_devices(keep, send):
    total = keep + swap_core(send).astype(F32)
    total = scatter_sum(total, PLANE, 16)
    total = jnp.sum(collect(total.astype(BF16), "z", 8).astype(F32), axis=0).astype(BF16)
    total = collect(total, PLANE, 16).reshape(ROWS, CH)
    return total, swap_core(total)


def body(latent, cotangent, w_qkv, w_proj, w_up, w_down, gains, attn_bias):
    cols = latent.shape[1]
    half = jax.ShapeDtypeStruct((HALF, cols, CH), BF16)
    params = pltpu.CompilerParams(vmem_limit_bytes=VMEM_LIMIT)
    packed = jax.ShapeDtypeStruct((ROWS, CH), F32)
    core = lax.axis_index("core").reshape(1)
    weights = (w_qkv, w_proj, w_up, w_down, gains)
    g_below = shift(cotangent, -1, 0)
    tokens = WIN * cols

    def table(width, share=1):
        return jax.ShapeDtypeStruct((tokens // share, width), BF16)

    kept_shapes = [table(width, 2) for width in (CH, CH, CH, HEADS * LEN, CH, CH, CH, CH)]
    pair_widths = (CH, FFN, CH, FFN, CH, CH, CH, 3 * CH)
    wide = cols // 2
    part_a, part_b = WIN * (wide - WIN), WIN * (cols - wide + WIN)
    small = [jax.ShapeDtypeStruct((LEN, HEADS * LEN), F32), jax.ShapeDtypeStruct((2, CH), F32)]
    side = jax.ShapeDtypeStruct((HALF, wide, CH), BF16)
    top_a, low_a = pl.pallas_call(
        first_kernel,
        out_shape=(side, side),
        in_specs=[pl.BlockSpec(memory_space=pltpu.HBM)] * 7,
        out_specs=vmem(2),
        scratch_shapes=[
            pltpu.VMEM((WIN, wide, CH), BF16),
            pltpu.VMEM(attn_bias.shape[1:], F32),
            pltpu.SemaphoreType.DMA((7,)),
        ]
        + [pltpu.VMEM(w.shape[1:], w.dtype) for w in weights],
        compiler_params=pltpu.CompilerParams(vmem_limit_bytes=FIRST_LIMIT),
        cost_estimate=cost(300_000_000, 1_500_000),
        name="forward_first",
    )(latent, attn_bias, *weights)
    below_a = shift(top_a, -1, 0)
    top_b, low_b = pl.pallas_call(
        next_kernel,
        out_shape=(side, side),
        in_specs=vmem(7),
        out_specs=vmem(2),
        compiler_params=params,
        cost_estimate=cost(300_000_000, 1_500_000),
        name="forward_next",
    )(latent, *weights, attn_bias)
    top_b, below_a, g_below = lax.optimization_barrier((top_b, below_a, g_below))
    below_b = shift(top_b, -1, 0)
    rows = (low_a, below_a, cotangent[HALF:], g_below[:HALF])
    edge = shift(jnp.concatenate([v[:, :WIN] for v in rows], axis=0), 0, -1)
    weights = (*weights, attn_bias)
    frame = pltpu.VMEM((WIN, cols + 2 * WIN, CH), F32)
    dx_a, *pairs_a, bias_a, gain_a = pl.pallas_call(
        second_kernel,
        out_shape=(
            jax.ShapeDtypeStruct((part_a, CH), F32),
            *[jax.ShapeDtypeStruct((part_a, width), BF16) for width in pair_widths],
            *small,
        ),
        in_specs=vmem(10),
        out_specs=vmem(11),
        scratch_shapes=[frame],
        compiler_params=params,
        cost_estimate=cost(700_000_000, 3_000_000),
        name="backward_second",
    )(low_a, below_a, cotangent, g_below, *weights)
    edge, below_b, dx_a = lax.optimization_barrier((edge, below_b, dx_a))
    d_top, d_low, *pairs_b, bias_b, gain_b = pl.pallas_call(
        third_kernel,
        out_shape=(half, half, *[jax.ShapeDtypeStruct((part_b, width), BF16) for width in pair_widths], *small),
        in_specs=vmem(16),
        out_specs=vmem(12),
        scratch_shapes=[frame],
        compiler_params=params,
        cost_estimate=cost(800_000_000, 3_000_000),
        name="backward_third",
    )(low_a, low_b, below_a, below_b, cotangent, g_below, edge, *weights, dx_a, bias_a, gain_a)
    pack_two = pl.pallas_call(
        weights_kernel,
        out_shape=packed,
        in_specs=vmem(18),
        out_specs=vmem(1)[0],
        compiler_params=params,
        cost_estimate=cost(500_000_000, 5_000_000),
        name="weights_second",
    )(*pairs_a, *pairs_b, bias_b, gain_b)
    d_above = shift(d_low, 1, 0)
    kept = []
    for part in range(2):
        made = pl.pallas_call(
            functools.partial(keep_kernel, part),
            out_shape=kept_shapes,
            in_specs=vmem(5),
            out_specs=vmem(8),
            compiler_params=params,
            cost_estimate=cost(300_000_000, 2_000_000),
            name="keep_first",
        )(latent, w_qkv, w_proj, gains, attn_bias)
        if part == 0:
            d_above, pack_two, made = lax.optimization_barrier((d_above, pack_two, made))
            d_left = shift(jnp.concatenate([v[:, cols - WIN :] for v in (d_above, d_top)], axis=0), 0, 1)
        else:
            d_left, made = lax.optimization_barrier((d_left, made))
        kept += made
    dx, keep, send = pl.pallas_call(
        last_kernel,
        out_shape=(
            jax.ShapeDtypeStruct(latent.shape, BF16),
            packed,
            jax.ShapeDtypeStruct((ROWS, CH), BF16),
        ),
        in_specs=vmem(25) + [pl.BlockSpec(memory_space=pltpu.SMEM)],
        out_specs=vmem(3),
        scratch_shapes=[frame, pltpu.VMEM((ROWS, CH), F32)],
        compiler_params=params,
        cost_estimate=cost(1_500_000_000, 4_000_000),
        name="backward_first",
    )(d_top, d_above, d_left, *kept, *weights[:5], pack_two, core)
    parts = sum_over_devices(keep, send)
    qkv, proj, up, down, gain, bias = pl.pallas_call(
        unpack_kernel,
        out_shape=(
            jax.ShapeDtypeStruct((2, CH, 3 * CH), F32),
            jax.ShapeDtypeStruct((2, CH, CH), F32),
            jax.ShapeDtypeStruct((2, CH, FFN), F32),
            jax.ShapeDtypeStruct((2, FFN, CH), F32),
            jax.ShapeDtypeStruct((2, 2, CH), F32),
            jax.ShapeDtypeStruct((2, HEADS, LEN, LEN), F32),
        ),
        in_specs=[pl.BlockSpec(memory_space=pltpu.SMEM)] + vmem(2),
        out_specs=vmem(6),
        scratch_shapes=[pltpu.VMEM((2 * ROWS, CH), F32)],
        compiler_params=params,
        cost_estimate=cost(1_000_000, 4_000_000),
        name="unpack",
    )(core, *parts)
    return dx, qkv, proj, up, down, gain, bias


def solution(mesh):
    fine = jax.sharding.Mesh(mesh.devices.reshape(8, 2, 2, 4, 2), AXES)
    tiles = P(("z", "yh", "core"), ("x", "yl"), None)
    in_specs = (tiles, tiles, P(), P(), P(), P(), P(), P())
    out_specs = (tiles, P(), P(), P(), P(), P(), P())
    return jax.shard_map(body, mesh=fine, in_specs=in_specs, out_specs=out_specs, check_vma=False)
```

```python
import functools

import jax
import jax.numpy as jnp
from jax import lax
from jax.experimental import pallas as pl
from jax.experimental.pallas import tpu as pltpu
from jax.sharding import PartitionSpec as P

WIN = 8
HALF = 4
LEN = 64
CH = 128
HEADS = 4
FFN = 512
EPS = 1e-05
SCALE = (CH // HEADS) ** -0.5
F32 = jnp.float32
BF16 = jnp.bfloat16
VMEM_LIMIT = 32 * 1024 * 1024
FIRST_LIMIT = 57 * 1000 * 1000

ROW_QKV, ROW_PROJ, ROW_UP, ROW_DOWN, ROW_BIAS, ROW_GAIN, ROWS = 0, 384, 512, 1024, 1536, 1664, 1792
AXES = ("z", "yh", "core", "x", "yl")
PLANE = ("yh", "x", "yl")


def nn(a, b):
    return lax.dot_general(a, b, (((1,), (0,)), ((), ())), preferred_element_type=F32)


def nt(a, b):
    return lax.dot_general(a, b, (((1,), (1,)), ((), ())), preferred_element_type=F32)


def tn(a, b):
    return lax.dot_general(a, b, (((0,), (0,)), ((), ())), preferred_element_type=F32)


def lane_means(parts):
    width = len(parts) * CH
    block = lax.broadcasted_iota(jnp.int32, (width, width), 0) // CH == lax.broadcasted_iota(jnp.int32, (width, width), 1) // CH
    ones = (block.astype(F32) * (1.0 / CH)).astype(BF16)
    sums = nn(jnp.concatenate([p.astype(BF16) for p in parts], axis=1), ones)
    return [sums[:, CH * i : CH * (i + 1)] for i in range(len(parts))]


def normalise(v):
    centre = v - jnp.mean(v, axis=-1, keepdims=True)
    spread = jnp.mean(centre * centre, axis=-1, keepdims=True)
    inv = lax.rsqrt(spread + EPS)
    return centre * inv, inv


def normalise_back(dn, hat, inv, gain):
    d_hat = dn * gain
    mean, along = lane_means([d_hat, d_hat * hat])
    return inv * (d_hat - mean - hat * along)


def head_mask():
    rows = lax.broadcasted_iota(jnp.int32, (HEADS * LEN, CH), 0) // LEN
    lanes = lax.broadcasted_iota(jnp.int32, (HEADS * LEN, CH), 1) // (CH // HEADS)
    return (rows == lanes).astype(F32).astype(BF16)


def spread_heads(v, mask):
    return jnp.concatenate([v] * HEADS, axis=0) * mask


def gather_heads(v):
    lane = lax.broadcasted_iota(jnp.int32, (LEN, CH), 1)
    size = CH // HEADS
    out = v[3 * LEN :]
    for h in (2, 1, 0):
        out = jnp.where(lane < (h + 1) * size, v[h * LEN : (h + 1) * LEN], out)
    return out


def attention(qkv, bias_t, mask):
    q, k, v = qkv[:, :CH], qkv[:, CH : 2 * CH], qkv[:, 2 * CH :]
    scores = nt(k, spread_heads(q, mask)) * SCALE + bias_t
    top = jnp.max(scores, axis=0, keepdims=True)
    e = jnp.exp(scores - top)
    p = (e * (1.0 / jnp.sum(e, axis=0, keepdims=True))).astype(BF16)
    return gather_heads(tn(p, v)).astype(BF16), p


def attention_back(d_o, qkv, p, mask):
    q, k, v = qkv[:, :CH], qkv[:, CH : 2 * CH], qkv[:, 2 * CH :]
    do_spread = spread_heads(d_o, mask)
    dv = nn(p, do_spread)
    dp = nt(v, do_spread)
    pf = p.astype(F32)
    ds = pf * (dp - jnp.sum(dp * pf, axis=0, keepdims=True))
    dsb = ds.astype(BF16)
    dk = nn(dsb, spread_heads(q, mask)) * SCALE
    dq = gather_heads(tn(dsb, k)) * SCALE
    return jnp.concatenate([dq, dk, dv], axis=1).astype(BF16), ds


def gelu_and_slope(u):
    c = 0.7978845608028654
    sq = u * u
    s = 0.5 * jnp.tanh(u * (c + (c * 0.044715) * sq)) + 0.5
    m = u * s
    return m, s + m * (1.0 - s) * (2.0 * c + (6.0 * c * 0.044715) * sq)


def forward(x, w_qkv, w_proj, gains, bias, mask):
    hat1, inv1 = normalise(x)
    gain = gains()
    a1 = (hat1 * gain[0:1]).astype(BF16)
    qkv = nn(a1, w_qkv()).astype(BF16)
    bias_t = turned_bias(bias())
    outs, weights = [], []
    for w in range(x.shape[0] // LEN):
        o, p = attention(qkv[w * LEN : (w + 1) * LEN], bias_t, mask)
        outs.append(o)
        weights.append(p)
    o = jnp.concatenate(outs, axis=0)
    h = (x + nn(o, w_proj())).astype(BF16).astype(F32)
    hat2, inv2 = normalise(h)
    a2 = (hat2 * gain[1:2]).astype(BF16)
    return h, (hat1, inv1, a1, jnp.concatenate(weights, axis=0), o, hat2, inv2, a2), qkv


def backward(gy, kept, qkv, w_qkv, w_proj, w_up, w_down, g1, g2, mask):
    hat1, inv1, a1, p, o, hat2, inv2, a2 = kept
    m, slope = gelu_and_slope(nn(a2, w_up))
    m = m.astype(BF16)
    du = (nt(gy, w_down) * slope).astype(BF16)
    da2 = nt(du, w_up)
    gain2 = jnp.sum(da2 * hat2, axis=0, keepdims=True)
    dh = gy.astype(F32) + normalise_back(da2, hat2, inv2, g2)
    dhb = dh.astype(BF16)
    d_o = nt(dhb, w_proj).astype(BF16)
    parts, bias = [], None
    for w in range(gy.shape[0] // LEN):
        at = slice(w * LEN, (w + 1) * LEN)
        part, ds = attention_back(d_o[at], qkv[at], p[at], mask)
        parts.append(part)
        bias = ds if bias is None else bias + ds
    dqkv = jnp.concatenate(parts, axis=0)
    da1 = nt(dqkv, w_qkv)
    gain1 = jnp.sum(da1 * hat1, axis=0, keepdims=True)
    dx = dh + normalise_back(da1, hat1, inv1, g1)
    return dx, (gy, m, a2, du, o, dhb, a1, dqkv), bias, gain1, gain2


def pack(pack_ref, pairs, bias, gain1, gain2, old=None):
    gy, m, a2, du, o, dhb, a1, dqkv = pairs

    def put(at, value):
        rows = slice(at, at + value.shape[0])
        pack_ref[rows] = value if old is None else value + old[rows].astype(F32)

    down, up, qkv = tn(gy, m), tn(a2, du), tn(a1, dqkv)
    for j in range(3):
        put(ROW_QKV + CH * j, qkv[:, CH * j : CH * (j + 1)])
    put(ROW_PROJ, tn(o, dhb))
    for j in range(4):
        put(ROW_UP + CH * j, up[:, CH * j : CH * (j + 1)])
        put(ROW_DOWN + CH * j, down[:, CH * j : CH * (j + 1)].T)
    put(ROW_BIAS, bias[:, :CH])
    put(ROW_BIAS + LEN, bias[:, CH:])
    put(ROW_GAIN, jnp.concatenate([gain1, gain2, jnp.zeros((ROWS - ROW_GAIN - 2, CH), F32)], axis=0))


def to_windows(tile):
    rows, cols, ch = tile.shape
    return tile.reshape(WIN, cols // WIN, WIN, ch).transpose(1, 0, 2, 3).reshape(-1, ch)


def from_windows(tokens):
    count = tokens.shape[0] // LEN
    return tokens.reshape(count, WIN, WIN, CH).transpose(1, 0, 2, 3).reshape(WIN, count * WIN, CH)


def turned_bias(bias):
    return jnp.concatenate([bias[h].T for h in range(HEADS)], axis=1)


def first_half(x, w_qkv, w_proj, w_up, w_down, gains, bias):
    h, kept, _ = forward(to_windows(x.astype(F32)), w_qkv, w_proj, gains, bias, head_mask())
    m, _ = gelu_and_slope(nn(kept[7], w_up()))
    return from_windows(h + nn(m.astype(BF16), w_down()))


def first_kernel(*refs):
    sources, (top_ref, low_ref, edge_ref), refs = refs[:8], refs[8:11], refs[11:]
    targets, sem = refs[:8], refs[8]
    wide = sources[0].shape[1] // 2
    moves = [(sources[0].at[:, 0:wide], targets[0])]
    moves += [(source.at[0], target) for source, target in zip(sources[1:7], targets[1:7])]
    moves += [(sources[7].at[HALF:, 0:WIN], targets[7])]
    copies = [pltpu.make_async_copy(source, target, sem.at[i]) for i, (source, target) in enumerate(moves)]
    for copy in copies:
        copy.start()

    def fetched(i):
        copies[i].wait()
        return targets[i][...]

    parts = [functools.partial(fetched, i) for i in range(1, 7)]
    tile = first_half(fetched(0), *parts)
    top_ref[...] = tile[:HALF].astype(BF16)
    low_ref[...] = tile[HALF:].astype(BF16)
    edge_ref[0:HALF] = tile[HALF:, 0:WIN].astype(BF16)
    edge_ref[HALF:] = fetched(7)


def at(ref, i):
    return lambda: ref[i]


def next_kernel(x_ref, w_qkv_ref, w_proj_ref, w_up_ref, w_down_ref, gain_ref, bias_ref, top_ref, low_ref):
    wide = x_ref.shape[1] // 2
    parts = [at(ref, 0) for ref in (w_qkv_ref, w_proj_ref, w_up_ref, w_down_ref, gain_ref, bias_ref)]
    tile = first_half(x_ref[:, wide:], *parts)
    top_ref[...] = tile[:HALF].astype(BF16)
    low_ref[...] = tile[HALF:].astype(BF16)


KEPT = (CH, CH, CH, HEADS * LEN, CH, CH, CH, CH)


def kept_slices():
    starts = [sum(KEPT[:i]) for i in range(len(KEPT))]
    return [slice(start, start + width) for start, width in zip(starts, KEPT)]


def keep_kernel(part, x_ref, w_qkv_ref, w_proj_ref, gain_ref, bias_ref, kept_ref):
    wide = x_ref.shape[1] // 2
    x = to_windows(x_ref[:, part * wide : (part + 1) * wide].astype(F32))
    _, kept, _ = forward(x, at(w_qkv_ref, 0), at(w_proj_ref, 0), at(gain_ref, 0), at(bias_ref, 0), head_mask())
    for place, value, width in zip(kept_slices(), kept, KEPT):
        kept_ref[:, place] = jnp.broadcast_to(value, (x.shape[0], width)).astype(BF16)


def second_half(x, gy, w_qkv_ref, w_proj_ref, w_up_ref, w_down_ref, gain_ref, bias_ref):
    mask = head_mask()
    _, kept, qkv = forward(
        to_windows(x), at(w_qkv_ref, 1), at(w_proj_ref, 1), at(gain_ref, 1), at(bias_ref, 1), mask
    )
    w_qkv, w_proj, w_up, w_down = w_qkv_ref[1], w_proj_ref[1], w_up_ref[1], w_down_ref[1]
    g1, g2 = gain_ref[1, 0:1], gain_ref[1, 1:2]
    return backward(to_windows(gy).astype(BF16), kept, qkv, w_qkv, w_proj, w_up, w_down, g1, g2, mask)


def second_kernel(*refs):
    low_ref, below_ref, g_own_ref, g_below_ref = refs[:4]
    weights, (dx_ref, pack_ref, frame_ref) = refs[4:10], refs[10:]
    wide = low_ref.shape[1]
    frame_ref[0:HALF, 0:wide] = low_ref[...].astype(F32)
    frame_ref[HALF:, 0:wide] = below_ref[...].astype(F32)
    x = frame_ref[:, HALF : wide - HALF]
    frame_ref[0:HALF, 0:wide] = g_own_ref[HALF:, 0:wide].astype(F32)
    frame_ref[HALF:, 0:wide] = g_below_ref[0:HALF, 0:wide].astype(F32)
    gy = frame_ref[:, HALF : wide - HALF]
    dx, *sums = second_half(x, gy, *weights)
    dx_ref[...] = dx.astype(BF16)
    pack(pack_ref, *sums)


def third_kernel(*refs):
    low_a_ref, low_b_ref, below_a_ref, below_b_ref, g_own_ref, g_below_ref, edge_ref = refs[:7]
    weights, (dx_ref, old_ref, dtop_ref, dlow_ref, dedge_ref, pack_ref, frame_ref) = refs[7:13], refs[13:]
    wide, cols = low_a_ref.shape[1], g_own_ref.shape[1]
    span = cols - wide + WIN
    frame_ref[0:HALF, 0:WIN] = low_a_ref[:, wide - WIN :].astype(F32)
    frame_ref[HALF:, 0:WIN] = below_a_ref[:, wide - WIN :].astype(F32)
    frame_ref[0:HALF, WIN:span] = low_b_ref[...].astype(F32)
    frame_ref[HALF:, WIN:span] = below_b_ref[...].astype(F32)
    frame_ref[0:HALF, span : span + WIN] = edge_ref[0:HALF].astype(F32)
    frame_ref[HALF:, span : span + WIN] = edge_ref[WIN : WIN + HALF].astype(F32)
    x = frame_ref[:, HALF : span + HALF]
    frame_ref[0:HALF, 0:span] = g_own_ref[HALF:, wide - WIN :].astype(F32)
    frame_ref[HALF:, 0:span] = g_below_ref[0:HALF, wide - WIN :].astype(F32)
    frame_ref[0:HALF, span : span + WIN] = edge_ref[HALF:WIN].astype(F32)
    frame_ref[HALF:, span : span + WIN] = edge_ref[WIN + HALF :].astype(F32)
    gy = frame_ref[:, HALF : span + HALF]
    dx, *sums = second_half(x, gy, *weights)
    pack(pack_ref, *sums, old_ref)
    tile = from_windows(jnp.concatenate([dx_ref[...].astype(F32), dx], axis=0))
    dtop_ref[...] = tile[:HALF].astype(BF16)
    dlow_ref[...] = tile[HALF:].astype(BF16)
    dedge_ref[...] = tile[:HALF, cols - WIN :].astype(BF16)


def last_kernel(*refs):
    (own, above, left), kept_refs, refs = refs[:3], refs[3:5], refs[5:]
    w_qkv_ref, w_proj_ref, w_up_ref, w_down_ref, gain_ref, other_ref, core_ref = refs[:7]
    dx_ref, keep_ref, send_ref, frame_ref, pack_ref = refs[7:]
    cols = own.shape[1]
    frame_ref[:, 0:WIN] = left[...].astype(F32)
    first = frame_ref[:, HALF:WIN]
    frame_ref[:, 0:HALF] = first
    frame_ref[HALF:, HALF : HALF + cols] = own[...].astype(F32)
    frame_ref[0:HALF, HALF : HALF + cols] = above[...].astype(F32)
    gy = to_windows(frame_ref[:, 0:cols]).astype(BF16)
    kept = [jnp.concatenate([ref[:, place] for ref in kept_refs], axis=0) for place in kept_slices()]
    kept = [v.astype(F32) if i in (0, 1, 5, 6) else v for i, v in enumerate(kept)]
    g1, g2 = gain_ref[0, 0:1], gain_ref[0, 1:2]
    dx, pairs, bias, gain1, gain2 = backward(
        gy, kept, nn(kept[2], w_qkv_ref[0]).astype(BF16), w_qkv_ref[0], w_proj_ref[0], w_up_ref[0], w_down_ref[0], g1, g2, head_mask()
    )
    dx_ref[...] = from_windows(dx).astype(BF16)
    pack(pack_ref, pairs, bias, gain1, gain2)
    first_core = core_ref[0] == 0

    @pl.when(first_core)
    def _():
        keep_ref[...] = pack_ref[...]
        send_ref[...] = other_ref[...].astype(BF16)

    @pl.when(jnp.logical_not(first_core))
    def _():
        keep_ref[...] = other_ref[...]
        send_ref[...] = pack_ref[...].astype(BF16)


def unpack_kernel(core_ref, own_ref, other_ref, *refs):
    qkv_ref, proj_ref, up_ref, down_ref, gain_ref, bias_ref, whole_ref = refs
    at = pl.multiple_of(core_ref[0] * ROWS, ROWS)
    whole_ref[pl.ds(at, ROWS)] = own_ref[...].astype(F32)
    whole_ref[pl.ds(ROWS - at, ROWS)] = other_ref[...].astype(F32)
    for b in range(2):
        at = b * ROWS
        for j in range(3):
            qkv_ref[b, :, CH * j : CH * (j + 1)] = whole_ref[at + ROW_QKV + CH * j : at + ROW_QKV + CH * (j + 1)]
        proj_ref[b] = whole_ref[at + ROW_PROJ : at + ROW_PROJ + CH]
        for j in range(4):
            up_ref[b, :, CH * j : CH * (j + 1)] = whole_ref[at + ROW_UP + CH * j : at + ROW_UP + CH * (j + 1)]
        down_ref[b] = whole_ref[at + ROW_DOWN : at + ROW_DOWN + FFN]
        for j in range(2):
            turned = whole_ref[at + ROW_BIAS + LEN * j : at + ROW_BIAS + LEN * (j + 1)].T
            bias_ref[b, 2 * j] = turned[:LEN]
            bias_ref[b, 2 * j + 1] = turned[LEN:]
        gain_ref[b] = whole_ref[at + ROW_GAIN : at + ROW_GAIN + 2]


def vmem(count):
    return [pl.BlockSpec(memory_space=pltpu.VMEM)] * count


def cost(flops, moved):
    return pl.CostEstimate(flops=flops, bytes_accessed=moved, transcendentals=0)


def shift(value, down, right):
    tall, wide = 32, 8
    pairs = []
    for r in range(tall):
        for c in range(wide):
            pairs.append((r * wide + c, (r + down) % tall * wide + (c + right) % wide))
    return lax.ppermute(value, AXES, pairs)


def swap_core(value):
    return lax.ppermute(value, "core", [(0, 1), (1, 0)])


def scatter_sum(value, axis, count):
    pieces = value.astype(BF16).reshape(count, value.shape[0] // count, CH)
    return jnp.sum(lax.all_to_all(pieces, axis, 0, 0).astype(F32), axis=0)


def collect(value, axis, count):
    spread = jnp.broadcast_to(value[None], (count, *value.shape))
    return lax.all_to_all(spread, axis, 0, 0)


def sum_over_devices(keep, send):
    total = keep + swap_core(send).astype(F32)
    total = scatter_sum(total, PLANE, 16)
    total = jnp.sum(collect(total.astype(BF16), "z", 8).astype(F32), axis=0).astype(BF16)
    total = collect(total, PLANE, 16).reshape(ROWS, CH)
    return total, swap_core(total)


def body(latent, cotangent, w_qkv, w_proj, w_up, w_down, gains, attn_bias):
    cols = latent.shape[1]
    half = jax.ShapeDtypeStruct((HALF, cols, CH), BF16)
    params = pltpu.CompilerParams(vmem_limit_bytes=VMEM_LIMIT)
    packed = jax.ShapeDtypeStruct((ROWS, CH), F32)
    core = lax.axis_index("core").reshape(1)
    weights = (w_qkv, w_proj, w_up, w_down, gains)
    g_below = shift(cotangent, -1, 0)
    tokens = WIN * cols

    wide = cols // 2
    part_a = WIN * (wide - WIN)
    side = jax.ShapeDtypeStruct((HALF, wide, CH), BF16)
    corner = jax.ShapeDtypeStruct((WIN, WIN, CH), BF16)
    top_a, low_a, edge_own = pl.pallas_call(
        first_kernel,
        out_shape=(side, side, corner),
        in_specs=[pl.BlockSpec(memory_space=pltpu.HBM)] * 8,
        out_specs=vmem(3),
        scratch_shapes=[pltpu.VMEM((WIN, wide, CH), BF16)]
        + [pltpu.VMEM(w.shape[1:], w.dtype) for w in (*weights, attn_bias)]
        + [pltpu.VMEM((HALF, WIN, CH), BF16), pltpu.SemaphoreType.DMA((8,))],
        compiler_params=pltpu.CompilerParams(vmem_limit_bytes=FIRST_LIMIT),
        cost_estimate=cost(300_000_000, 1_500_000),
        name="forward_first",
    )(latent, *weights, attn_bias, cotangent)
    below_a = shift(top_a, -1, 0)
    top_b, low_b = pl.pallas_call(
        next_kernel,
        out_shape=(side, side),
        in_specs=vmem(7),
        out_specs=vmem(2),
        compiler_params=params,
        cost_estimate=cost(300_000_000, 1_500_000),
        name="forward_next",
    )(latent, *weights, attn_bias)
    top_b, below_a, g_below = lax.optimization_barrier((top_b, below_a, g_below))
    below_b = shift(top_b, -1, 0)
    edge = shift(jnp.concatenate([edge_own, below_a[:, :WIN], g_below[:HALF, :WIN]], axis=0), 0, -1)
    weights = (*weights, attn_bias)
    frame = pltpu.VMEM((WIN, cols + 2 * WIN, CH), F32)
    dx_a, pack_a = pl.pallas_call(
        second_kernel,
        out_shape=(jax.ShapeDtypeStruct((part_a, CH), BF16), packed),
        in_specs=vmem(10),
        out_specs=vmem(2),
        scratch_shapes=[frame],
        compiler_params=params,
        cost_estimate=cost(700_000_000, 3_000_000),
        name="backward_second",
    )(low_a, below_a, cotangent, g_below, *weights)
    edge, below_b, dx_a = lax.optimization_barrier((edge, below_b, dx_a))
    d_top, d_low, d_edge, pack_two = pl.pallas_call(
        third_kernel,
        out_shape=(half, half, jax.ShapeDtypeStruct((HALF, WIN, CH), BF16), packed),
        in_specs=vmem(15),
        out_specs=vmem(4),
        scratch_shapes=[frame],
        compiler_params=params,
        cost_estimate=cost(800_000_000, 3_000_000),
        name="backward_third",
    )(low_a, low_b, below_a, below_b, cotangent, g_below, edge, *weights, dx_a, pack_a)
    d_above = shift(d_low, 1, 0)
    kept = []
    for part in range(2):
        made = pl.pallas_call(
            functools.partial(keep_kernel, part),
            out_shape=jax.ShapeDtypeStruct((WIN * wide, sum(KEPT)), BF16),
            in_specs=vmem(5),
            out_specs=vmem(1)[0],
            compiler_params=params,
            cost_estimate=cost(300_000_000, 2_000_000),
            name="keep_first",
        )(latent, w_qkv, w_proj, gains, attn_bias)
        if part == 0:
            d_above, made = lax.optimization_barrier((d_above, made))
            d_left = shift(jnp.concatenate([d_above[:, cols - WIN :], d_edge], axis=0), 0, 1)
        else:
            d_left, made = lax.optimization_barrier((d_left, made))
        kept.append(made)
    dx, keep, send = pl.pallas_call(
        last_kernel,
        out_shape=(
            jax.ShapeDtypeStruct(latent.shape, BF16),
            packed,
            jax.ShapeDtypeStruct((ROWS, CH), BF16),
        ),
        in_specs=vmem(11) + [pl.BlockSpec(memory_space=pltpu.SMEM)],
        out_specs=vmem(3),
        scratch_shapes=[frame, pltpu.VMEM((ROWS, CH), F32)],
        compiler_params=params,
        cost_estimate=cost(1_500_000_000, 4_000_000),
        name="backward_first",
    )(d_top, d_above, d_left, *kept, *weights[:5], pack_two, core)
    parts = sum_over_devices(keep, send)
    qkv, proj, up, down, gain, bias = pl.pallas_call(
        unpack_kernel,
        out_shape=(
            jax.ShapeDtypeStruct((2, CH, 3 * CH), F32),
            jax.ShapeDtypeStruct((2, CH, CH), F32),
            jax.ShapeDtypeStruct((2, CH, FFN), F32),
            jax.ShapeDtypeStruct((2, FFN, CH), F32),
            jax.ShapeDtypeStruct((2, 2, CH), F32),
            jax.ShapeDtypeStruct((2, HEADS, LEN, LEN), F32),
        ),
        in_specs=[pl.BlockSpec(memory_space=pltpu.SMEM)] + vmem(2),
        out_specs=vmem(6),
        scratch_shapes=[pltpu.VMEM((2 * ROWS, CH), F32)],
        compiler_params=params,
        cost_estimate=cost(1_000_000, 4_000_000),
        name="unpack",
    )(core, *parts)
    return dx, qkv, proj, up, down, gain, bias


def solution(mesh):
    fine = jax.sharding.Mesh(mesh.devices.reshape(8, 2, 2, 4, 2), AXES)
    tiles = P(("z", "yh", "core"), ("x", "yl"), None)
    in_specs = (tiles, tiles, P(), P(), P(), P(), P(), P())
    out_specs = (tiles, P(), P(), P(), P(), P(), P())
    return jax.shard_map(body, mesh=fine, in_specs=in_specs, out_specs=out_specs, check_vma=False)
```

```python
import functools

import jax
import jax.numpy as jnp
from jax import lax
from jax.experimental import pallas as pl
from jax.experimental.pallas import tpu as pltpu
from jax.sharding import PartitionSpec as P

WIN = 8
HALF = 4
LEN = 64
CH = 128
HEADS = 4
FFN = 512
EPS = 1e-05
SCALE = (CH // HEADS) ** -0.5
F32 = jnp.float32
BF16 = jnp.bfloat16
VMEM_LIMIT = 32 * 1024 * 1024
FIRST_LIMIT = 57 * 1000 * 1000

ROW_QKV, ROW_PROJ, ROW_UP, ROW_DOWN, ROW_BIAS, ROW_GAIN, ROWS = 0, 384, 512, 1024, 1536, 1664, 1792
AXES = ("z", "yh", "core", "x", "yl")
PLANE = ("yh", "x", "yl")


def nn(a, b):
    return lax.dot_general(a, b, (((1,), (0,)), ((), ())), preferred_element_type=F32)


def nt(a, b):
    return lax.dot_general(a, b, (((1,), (1,)), ((), ())), preferred_element_type=F32)


def tn(a, b):
    return lax.dot_general(a, b, (((0,), (0,)), ((), ())), preferred_element_type=F32)


def lane_means(parts):
    width = len(parts) * CH
    block = lax.broadcasted_iota(jnp.int32, (width, width), 0) // CH == lax.broadcasted_iota(jnp.int32, (width, width), 1) // CH
    ones = (block.astype(F32) * (1.0 / CH)).astype(BF16)
    sums = nn(jnp.concatenate([p.astype(BF16) for p in parts], axis=1), ones)
    return [sums[:, CH * i : CH * (i + 1)] for i in range(len(parts))]


def normalise(v):
    centre = v - jnp.mean(v, axis=-1, keepdims=True)
    spread = jnp.mean(centre * centre, axis=-1, keepdims=True)
    inv = lax.rsqrt(spread + EPS)
    return centre * inv, inv


def normalise_back(dn, hat, inv, gain):
    d_hat = dn * gain
    mean, along = lane_means([d_hat, d_hat * hat])
    return inv * (d_hat - mean - hat * along)


def head_mask():
    rows = lax.broadcasted_iota(jnp.int32, (HEADS * LEN, CH), 0) // LEN
    lanes = lax.broadcasted_iota(jnp.int32, (HEADS * LEN, CH), 1) // (CH // HEADS)
    return (rows == lanes).astype(F32).astype(BF16)


def spread_heads(v, mask):
    return jnp.concatenate([v] * HEADS, axis=0) * mask


def gather_heads(v):
    lane = lax.broadcasted_iota(jnp.int32, (LEN, CH), 1)
    size = CH // HEADS
    out = v[3 * LEN :]
    for h in (2, 1, 0):
        out = jnp.where(lane < (h + 1) * size, v[h * LEN : (h + 1) * LEN], out)
    return out


def attention(qkv, bias_t, mask):
    q, k, v = qkv[:, :CH], qkv[:, CH : 2 * CH], qkv[:, 2 * CH :]
    scores = nt(k, spread_heads(q, mask)) * SCALE + bias_t
    top = jnp.max(scores, axis=0, keepdims=True)
    e = jnp.exp(scores - top)
    p = (e * (1.0 / jnp.sum(e, axis=0, keepdims=True))).astype(BF16)
    return gather_heads(tn(p, v)).astype(BF16), p


def attention_back(d_o, qkv, p, mask):
    q, k, v = qkv[:, :CH], qkv[:, CH : 2 * CH], qkv[:, 2 * CH :]
    do_spread = spread_heads(d_o, mask)
    dv = nn(p, do_spread)
    dp = nt(v, do_spread)
    pf = p.astype(F32)
    ds = pf * (dp - jnp.sum(dp * pf, axis=0, keepdims=True))
    dsb = ds.astype(BF16)
    dk = nn(dsb, spread_heads(q, mask)) * SCALE
    dq = gather_heads(tn(dsb, k)) * SCALE
    return jnp.concatenate([dq, dk, dv], axis=1).astype(BF16), ds


CHUNK = 32


def mlp_scratch(tokens):
    return [pltpu.VMEM((tokens, FFN), kind) for kind in (F32, F32, BF16, BF16)]


def gelu_and_slope(u):
    c = 0.7978845608028654
    sq = u * u
    s = 0.5 * jnp.tanh(u * (c + (c * 0.044715) * sq)) + 0.5
    m = u * s
    return m, s + m * (1.0 - s) * (2.0 * c + (6.0 * c * 0.044715) * sq)


def forward(x, w_qkv, w_proj, gains, bias, mask):
    hat1, inv1 = normalise(x)
    gain = gains()
    a1 = (hat1 * gain[0:1]).astype(BF16)
    qkv = nn(a1, w_qkv()).astype(BF16)
    bias_t = turned_bias(bias())
    outs, weights = [], []
    for w in range(x.shape[0] // LEN):
        o, p = attention(qkv[w * LEN : (w + 1) * LEN], bias_t, mask)
        outs.append(o)
        weights.append(p)
    o = jnp.concatenate(outs, axis=0)
    h = (x + nn(o, w_proj())).astype(BF16).astype(F32)
    hat2, inv2 = normalise(h)
    a2 = (hat2 * gain[1:2]).astype(BF16)
    return h, (hat1, inv1, a1, jnp.concatenate(weights, axis=0), o, hat2, inv2, a2), qkv


def backward(gy, kept, qkv, w_qkv, w_proj, w_up, w_down, g1, g2, mask, scratch):
    hat1, inv1, a1, p, o, hat2, inv2, a2 = kept
    u_ref, dm_ref, m_ref, du_ref = scratch
    tokens = gy.shape[0]
    u_ref[0:tokens] = nn(a2, w_up)
    dm_ref[0:tokens] = nt(gy, w_down)
    for start in range(0, tokens, CHUNK):
        rows = slice(start, start + CHUNK)
        part, slope = gelu_and_slope(u_ref[rows])
        m_ref[rows] = part.astype(BF16)
        du_ref[rows] = (dm_ref[rows] * slope).astype(BF16)
    m, du = m_ref[0:tokens], du_ref[0:tokens]
    da2 = nt(du, w_up)
    gain2 = jnp.sum(da2 * hat2, axis=0, keepdims=True)
    dh = gy.astype(F32) + normalise_back(da2, hat2, inv2, g2)
    dhb = dh.astype(BF16)
    d_o = nt(dhb, w_proj).astype(BF16)
    parts, bias = [], None
    for w in range(gy.shape[0] // LEN):
        at = slice(w * LEN, (w + 1) * LEN)
        part, ds = attention_back(d_o[at], qkv[at], p[at], mask)
        parts.append(part)
        bias = ds if bias is None else bias + ds
    dqkv = jnp.concatenate(parts, axis=0)
    da1 = nt(dqkv, w_qkv)
    gain1 = jnp.sum(da1 * hat1, axis=0, keepdims=True)
    dx = dh + normalise_back(da1, hat1, inv1, g1)
    return dx, (gy, m, a2, du, o, dhb, a1, dqkv), bias, gain1, gain2


def pack(pack_ref, pairs, bias, gain1, gain2, old=None):
    gy, m, a2, du, o, dhb, a1, dqkv = pairs

    def put(at, value):
        rows = slice(at, at + value.shape[0])
        pack_ref[rows] = value if old is None else value + old[rows].astype(F32)

    down, up, qkv = tn(gy, m), tn(a2, du), tn(a1, dqkv)
    for j in range(3):
        put(ROW_QKV + CH * j, qkv[:, CH * j : CH * (j + 1)])
    put(ROW_PROJ, tn(o, dhb))
    for j in range(4):
        put(ROW_UP + CH * j, up[:, CH * j : CH * (j + 1)])
        put(ROW_DOWN + CH * j, down[:, CH * j : CH * (j + 1)].T)
    put(ROW_BIAS, bias[:, :CH])
    put(ROW_BIAS + LEN, bias[:, CH:])
    put(ROW_GAIN, jnp.concatenate([gain1, gain2, jnp.zeros((ROWS - ROW_GAIN - 2, CH), F32)], axis=0))


def to_windows(tile):
    rows, cols, ch = tile.shape
    return tile.reshape(WIN, cols // WIN, WIN, ch).transpose(1, 0, 2, 3).reshape(-1, ch)


def from_windows(tokens):
    count = tokens.shape[0] // LEN
    return tokens.reshape(count, WIN, WIN, CH).transpose(1, 0, 2, 3).reshape(WIN, count * WIN, CH)


def turned_bias(bias):
    return jnp.concatenate([bias[h].T for h in range(HEADS)], axis=1)


def first_half(x, w_qkv, w_proj, w_up, w_down, gains, bias):
    h, kept, _ = forward(to_windows(x.astype(F32)), w_qkv, w_proj, gains, bias, head_mask())
    m, _ = gelu_and_slope(nn(kept[7], w_up()))
    return from_windows(h + nn(m.astype(BF16), w_down()))


def first_kernel(*refs):
    sources, (top_ref, low_ref, edge_ref), refs = refs[:8], refs[8:11], refs[11:]
    targets, sem = refs[:8], refs[8]
    wide = sources[0].shape[1] // 2
    moves = [(sources[0].at[:, 0:wide], targets[0])]
    moves += [(source.at[0], target) for source, target in zip(sources[1:7], targets[1:7])]
    moves += [(sources[7].at[HALF:, 0:WIN], targets[7])]
    copies = [pltpu.make_async_copy(source, target, sem.at[i]) for i, (source, target) in enumerate(moves)]
    for i in (0, 5, 1, 6, 2, 3, 4, 7):
        copies[i].start(priority=1)

    def fetched(i):
        copies[i].wait()
        return targets[i][...]

    parts = [functools.partial(fetched, i) for i in range(1, 7)]
    tile = first_half(fetched(0), *parts)
    top_ref[...] = tile[:HALF].astype(BF16)
    low_ref[...] = tile[HALF:].astype(BF16)
    edge_ref[0:HALF] = tile[HALF:, 0:WIN].astype(BF16)
    edge_ref[HALF:] = fetched(7)


def at(ref, i):
    return lambda: ref[i]


def next_kernel(x_ref, w_qkv_ref, w_proj_ref, w_up_ref, w_down_ref, gain_ref, bias_ref, top_ref, low_ref):
    wide = x_ref.shape[1] // 2
    parts = [at(ref, 0) for ref in (w_qkv_ref, w_proj_ref, w_up_ref, w_down_ref, gain_ref, bias_ref)]
    tile = first_half(x_ref[:, wide:], *parts)
    top_ref[...] = tile[:HALF].astype(BF16)
    low_ref[...] = tile[HALF:].astype(BF16)


KEPT = (CH, CH, CH, HEADS * LEN, CH, CH, CH, CH)


def kept_slices():
    starts = [sum(KEPT[:i]) for i in range(len(KEPT))]
    return [slice(start, start + width) for start, width in zip(starts, KEPT)]


def keep_kernel(part, x_ref, w_qkv_ref, w_proj_ref, gain_ref, bias_ref, kept_ref):
    wide = x_ref.shape[1] // 2
    x = to_windows(x_ref[:, part * wide : (part + 1) * wide].astype(F32))
    _, kept, _ = forward(x, at(w_qkv_ref, 0), at(w_proj_ref, 0), at(gain_ref, 0), at(bias_ref, 0), head_mask())
    for place, value, width in zip(kept_slices(), kept, KEPT):
        kept_ref[:, place] = jnp.broadcast_to(value, (x.shape[0], width)).astype(BF16)


def second_half(x, gy, scratch, w_qkv_ref, w_proj_ref, w_up_ref, w_down_ref, gain_ref, bias_ref):
    mask = head_mask()
    _, kept, qkv = forward(
        to_windows(x), at(w_qkv_ref, 1), at(w_proj_ref, 1), at(gain_ref, 1), at(bias_ref, 1), mask
    )
    w_qkv, w_proj, w_up, w_down = w_qkv_ref[1], w_proj_ref[1], w_up_ref[1], w_down_ref[1]
    g1, g2 = gain_ref[1, 0:1], gain_ref[1, 1:2]
    return backward(to_windows(gy).astype(BF16), kept, qkv, w_qkv, w_proj, w_up, w_down, g1, g2, mask, scratch)


def second_kernel(*refs):
    low_ref, below_ref, g_own_ref, g_below_ref = refs[:4]
    weights, (dx_ref, pack_ref, frame_ref, *scratch) = refs[4:10], refs[10:]
    wide = low_ref.shape[1]
    frame_ref[0:HALF, 0:wide] = low_ref[...].astype(F32)
    frame_ref[HALF:, 0:wide] = below_ref[...].astype(F32)
    x = frame_ref[:, HALF : wide - HALF]
    frame_ref[0:HALF, 0:wide] = g_own_ref[HALF:, 0:wide].astype(F32)
    frame_ref[HALF:, 0:wide] = g_below_ref[0:HALF, 0:wide].astype(F32)
    gy = frame_ref[:, HALF : wide - HALF]
    dx, *sums = second_half(x, gy, scratch, *weights)
    dx_ref[...] = dx.astype(BF16)
    pack(pack_ref, *sums)


def third_kernel(*refs):
    low_a_ref, low_b_ref, below_a_ref, below_b_ref, g_own_ref, g_below_ref, edge_ref = refs[:7]
    weights, (dx_ref, old_ref, dtop_ref, dlow_ref, dedge_ref, pack_ref, frame_ref, *scratch) = refs[7:13], refs[13:]
    wide, cols = low_a_ref.shape[1], g_own_ref.shape[1]
    span = cols - wide + WIN
    frame_ref[0:HALF, 0:WIN] = low_a_ref[:, wide - WIN :].astype(F32)
    frame_ref[HALF:, 0:WIN] = below_a_ref[:, wide - WIN :].astype(F32)
    frame_ref[0:HALF, WIN:span] = low_b_ref[...].astype(F32)
    frame_ref[HALF:, WIN:span] = below_b_ref[...].astype(F32)
    frame_ref[0:HALF, span : span + WIN] = edge_ref[0:HALF].astype(F32)
    frame_ref[HALF:, span : span + WIN] = edge_ref[WIN : WIN + HALF].astype(F32)
    x = frame_ref[:, HALF : span + HALF]
    frame_ref[0:HALF, 0:span] = g_own_ref[HALF:, wide - WIN :].astype(F32)
    frame_ref[HALF:, 0:span] = g_below_ref[0:HALF, wide - WIN :].astype(F32)
    frame_ref[0:HALF, span : span + WIN] = edge_ref[HALF:WIN].astype(F32)
    frame_ref[HALF:, span : span + WIN] = edge_ref[WIN + HALF :].astype(F32)
    gy = frame_ref[:, HALF : span + HALF]
    dx, *sums = second_half(x, gy, scratch, *weights)
    pack(pack_ref, *sums, old_ref)
    tile = from_windows(jnp.concatenate([dx_ref[...].astype(F32), dx], axis=0))
    dtop_ref[...] = tile[:HALF].astype(BF16)
    dlow_ref[...] = tile[HALF:].astype(BF16)
    dedge_ref[...] = tile[:HALF, cols - WIN :].astype(BF16)


def last_kernel(*refs):
    (own, above, left), kept_refs, refs = refs[:3], refs[3:5], refs[5:]
    w_qkv_ref, w_proj_ref, w_up_ref, w_down_ref, gain_ref, other_ref, core_ref = refs[:7]
    dx_ref, keep_ref, send_ref, frame_ref, pack_ref, *scratch = refs[7:]
    cols = own.shape[1]
    frame_ref[:, 0:WIN] = left[...].astype(F32)
    first = frame_ref[:, HALF:WIN]
    frame_ref[:, 0:HALF] = first
    frame_ref[HALF:, HALF : HALF + cols] = own[...].astype(F32)
    frame_ref[0:HALF, HALF : HALF + cols] = above[...].astype(F32)
    gy = to_windows(frame_ref[:, 0:cols]).astype(BF16)
    kept = [jnp.concatenate([ref[:, place] for ref in kept_refs], axis=0) for place in kept_slices()]
    kept = [v.astype(F32) if i in (0, 1, 5, 6) else v for i, v in enumerate(kept)]
    g1, g2 = gain_ref[0, 0:1], gain_ref[0, 1:2]
    dx, pairs, bias, gain1, gain2 = backward(
        gy, kept, nn(kept[2], w_qkv_ref[0]).astype(BF16), w_qkv_ref[0], w_proj_ref[0], w_up_ref[0], w_down_ref[0], g1, g2, head_mask(), scratch
    )
    dx_ref[...] = from_windows(dx).astype(BF16)
    pack(pack_ref, pairs, bias, gain1, gain2)
    first_core = core_ref[0] == 0

    @pl.when(first_core)
    def _():
        keep_ref[...] = pack_ref[...]
        send_ref[...] = other_ref[...].astype(BF16)

    @pl.when(jnp.logical_not(first_core))
    def _():
        keep_ref[...] = other_ref[...]
        send_ref[...] = pack_ref[...].astype(BF16)


def unpack_kernel(core_ref, own_ref, other_ref, *refs):
    qkv_ref, proj_ref, up_ref, down_ref, gain_ref, bias_ref, whole_ref = refs
    at = pl.multiple_of(core_ref[0] * ROWS, ROWS)
    whole_ref[pl.ds(at, ROWS)] = own_ref[...].astype(F32)
    whole_ref[pl.ds(ROWS - at, ROWS)] = other_ref[...].astype(F32)
    for b in range(2):
        at = b * ROWS
        for j in range(3):
            qkv_ref[b, :, CH * j : CH * (j + 1)] = whole_ref[at + ROW_QKV + CH * j : at + ROW_QKV + CH * (j + 1)]
        proj_ref[b] = whole_ref[at + ROW_PROJ : at + ROW_PROJ + CH]
        for j in range(4):
            up_ref[b, :, CH * j : CH * (j + 1)] = whole_ref[at + ROW_UP + CH * j : at + ROW_UP + CH * (j + 1)]
        down_ref[b] = whole_ref[at + ROW_DOWN : at + ROW_DOWN + FFN]
        for j in range(2):
            turned = whole_ref[at + ROW_BIAS + LEN * j : at + ROW_BIAS + LEN * (j + 1)].T
            bias_ref[b, 2 * j] = turned[:LEN]
            bias_ref[b, 2 * j + 1] = turned[LEN:]
        gain_ref[b] = whole_ref[at + ROW_GAIN : at + ROW_GAIN + 2]


def vmem(count):
    return [pl.BlockSpec(memory_space=pltpu.VMEM)] * count


def cost(flops, moved):
    return pl.CostEstimate(flops=flops, bytes_accessed=moved, transcendentals=0)


def shift(value, down, right):
    tall, wide = 32, 8
    pairs = []
    for r in range(tall):
        for c in range(wide):
            pairs.append((r * wide + c, (r + down) % tall * wide + (c + right) % wide))
    return lax.ppermute(value, AXES, pairs)


def swap_core(value):
    return lax.ppermute(value, "core", [(0, 1), (1, 0)])


def scatter_sum(value, axis, count):
    pieces = value.astype(BF16).reshape(count, value.shape[0] // count, CH)
    return jnp.sum(lax.all_to_all(pieces, axis, 0, 0).astype(F32), axis=0)


def collect(value, axis, count):
    spread = jnp.broadcast_to(value[None], (count, *value.shape))
    return lax.all_to_all(spread, axis, 0, 0)


def sum_over_devices(keep, send):
    total = keep + swap_core(send).astype(F32)
    total = scatter_sum(total, PLANE, 16)
    total = jnp.sum(collect(total.astype(BF16), "z", 8).astype(F32), axis=0).astype(BF16)
    total = collect(total, PLANE, 16).reshape(ROWS, CH)
    return total, swap_core(total)


def body(latent, cotangent, w_qkv, w_proj, w_up, w_down, gains, attn_bias):
    cols = latent.shape[1]
    half = jax.ShapeDtypeStruct((HALF, cols, CH), BF16)
    params = pltpu.CompilerParams(vmem_limit_bytes=VMEM_LIMIT)
    packed = jax.ShapeDtypeStruct((ROWS, CH), F32)
    core = lax.axis_index("core").reshape(1)
    weights = (w_qkv, w_proj, w_up, w_down, gains)
    g_below = shift(cotangent, -1, 0)
    tokens = WIN * cols

    wide = cols // 2
    part_a = WIN * (wide - WIN)
    side = jax.ShapeDtypeStruct((HALF, wide, CH), BF16)
    corner = jax.ShapeDtypeStruct((WIN, WIN, CH), BF16)
    top_a, low_a, edge_own = pl.pallas_call(
        first_kernel,
        out_shape=(side, side, corner),
        in_specs=[pl.BlockSpec(memory_space=pltpu.HBM)] * 8,
        out_specs=vmem(3),
        scratch_shapes=[pltpu.VMEM((WIN, wide, CH), BF16)]
        + [pltpu.VMEM(w.shape[1:], w.dtype) for w in (*weights, attn_bias)]
        + [pltpu.VMEM((HALF, WIN, CH), BF16), pltpu.SemaphoreType.DMA((8,))],
        compiler_params=pltpu.CompilerParams(vmem_limit_bytes=FIRST_LIMIT),
        cost_estimate=cost(300_000_000, 1_500_000),
        name="forward_first",
    )(latent, *weights, attn_bias, cotangent)
    below_a = shift(top_a, -1, 0)
    top_b, low_b = pl.pallas_call(
        next_kernel,
        out_shape=(side, side),
        in_specs=vmem(7),
        out_specs=vmem(2),
        compiler_params=params,
        cost_estimate=cost(300_000_000, 1_500_000),
        name="forward_next",
    )(latent, *weights, attn_bias)
    below_b = shift(top_b, -1, 0)
    edge = shift(jnp.concatenate([edge_own, below_a[:, :WIN], g_below[:HALF, :WIN]], axis=0), 0, -1)
    weights = (*weights, attn_bias)
    frame = pltpu.VMEM((WIN, cols + 2 * WIN, CH), F32)
    dx_a, pack_a = pl.pallas_call(
        second_kernel,
        out_shape=(jax.ShapeDtypeStruct((part_a, CH), BF16), packed),
        in_specs=vmem(10),
        out_specs=vmem(2),
        scratch_shapes=[frame, *mlp_scratch(part_a)],
        compiler_params=params,
        cost_estimate=cost(700_000_000, 3_000_000),
        name="backward_second",
    )(low_a, below_a, cotangent, g_below, *weights)
    edge, below_b, dx_a = lax.optimization_barrier((edge, below_b, dx_a))
    d_top, d_low, d_edge, pack_two = pl.pallas_call(
        third_kernel,
        out_shape=(half, half, jax.ShapeDtypeStruct((HALF, WIN, CH), BF16), packed),
        in_specs=vmem(15),
        out_specs=vmem(4),
        scratch_shapes=[frame, *mlp_scratch(WIN * cols - part_a)],
        compiler_params=params,
        cost_estimate=cost(800_000_000, 3_000_000),
        name="backward_third",
    )(low_a, low_b, below_a, below_b, cotangent, g_below, edge, *weights, dx_a, pack_a)
    d_above = shift(d_low, 1, 0)
    kept = []
    for part in range(2):
        made = pl.pallas_call(
            functools.partial(keep_kernel, part),
            out_shape=jax.ShapeDtypeStruct((WIN * wide, sum(KEPT)), BF16),
            in_specs=vmem(5),
            out_specs=vmem(1)[0],
            compiler_params=params,
            cost_estimate=cost(300_000_000, 2_000_000),
            name="keep_first",
        )(latent, w_qkv, w_proj, gains, attn_bias)
        if part == 0:
            d_above, made = lax.optimization_barrier((d_above, made))
            d_left = shift(jnp.concatenate([d_above[:, cols - WIN :], d_edge], axis=0), 0, 1)
        else:
            d_left, made = lax.optimization_barrier((d_left, made))
        kept.append(made)
    dx, keep, send = pl.pallas_call(
        last_kernel,
        out_shape=(
            jax.ShapeDtypeStruct(latent.shape, BF16),
            packed,
            jax.ShapeDtypeStruct((ROWS, CH), BF16),
        ),
        in_specs=vmem(11) + [pl.BlockSpec(memory_space=pltpu.SMEM)],
        out_specs=vmem(3),
        scratch_shapes=[frame, pltpu.VMEM((ROWS, CH), F32), *mlp_scratch(WIN * cols)],
        compiler_params=params,
        cost_estimate=cost(1_500_000_000, 4_000_000),
        name="backward_first",
    )(d_top, d_above, d_left, *kept, *weights[:5], pack_two, core)
    parts = sum_over_devices(keep, send)
    qkv, proj, up, down, gain, bias = pl.pallas_call(
        unpack_kernel,
        out_shape=(
            jax.ShapeDtypeStruct((2, CH, 3 * CH), F32),
            jax.ShapeDtypeStruct((2, CH, CH), F32),
            jax.ShapeDtypeStruct((2, CH, FFN), F32),
            jax.ShapeDtypeStruct((2, FFN, CH), F32),
            jax.ShapeDtypeStruct((2, 2, CH), F32),
            jax.ShapeDtypeStruct((2, HEADS, LEN, LEN), F32),
        ),
        in_specs=[pl.BlockSpec(memory_space=pltpu.SMEM)] + vmem(2),
        out_specs=vmem(6),
        scratch_shapes=[pltpu.VMEM((2 * ROWS, CH), F32)],
        compiler_params=params,
        cost_estimate=cost(1_000_000, 4_000_000),
        name="unpack",
    )(core, *parts)
    return dx, qkv, proj, up, down, gain, bias


def solution(mesh):
    fine = jax.sharding.Mesh(mesh.devices.reshape(8, 2, 2, 4, 2), AXES)
    tiles = P(("z", "yh", "core"), ("x", "yl"), None)
    in_specs = (tiles, tiles, P(), P(), P(), P(), P(), P())
    out_specs = (tiles, P(), P(), P(), P(), P(), P())
    return jax.shard_map(body, mesh=fine, in_specs=in_specs, out_specs=out_specs, check_vma=False)
```

```python
import functools

import jax
import jax.numpy as jnp
from jax import lax
from jax.experimental import pallas as pl
from jax.experimental.pallas import tpu as pltpu
from jax.sharding import PartitionSpec as P

WIN = 8
HALF = 4
LEN = 64
CH = 128
HEADS = 4
FFN = 512
EPS = 1e-05
SCALE = (CH // HEADS) ** -0.5
F32 = jnp.float32
BF16 = jnp.bfloat16
VMEM_LIMIT = 32 * 1024 * 1024
FIRST_LIMIT = 57 * 1000 * 1000

ROW_QKV, ROW_PROJ, ROW_UP, ROW_DOWN, ROW_BIAS, ROW_GAIN, ROWS = 0, 384, 512, 1024, 1536, 1664, 1792
AXES = ("z", "yh", "core", "x", "yl")
PLANE = ("yh", "x", "yl")


def nn(a, b):
    return lax.dot_general(a, b, (((1,), (0,)), ((), ())), preferred_element_type=F32)


def nt(a, b):
    return lax.dot_general(a, b, (((1,), (1,)), ((), ())), preferred_element_type=F32)


def tn(a, b):
    return lax.dot_general(a, b, (((0,), (0,)), ((), ())), preferred_element_type=F32)


def lane_means(parts):
    width = len(parts) * CH
    block = lax.broadcasted_iota(jnp.int32, (width, width), 0) // CH == lax.broadcasted_iota(jnp.int32, (width, width), 1) // CH
    ones = (block.astype(F32) * (1.0 / CH)).astype(BF16)
    sums = nn(jnp.concatenate([p.astype(BF16) for p in parts], axis=1), ones)
    return [sums[:, CH * i : CH * (i + 1)] for i in range(len(parts))]


def normalise(v):
    centre = v - jnp.mean(v, axis=-1, keepdims=True)
    spread = jnp.mean(centre * centre, axis=-1, keepdims=True)
    inv = lax.rsqrt(spread + EPS)
    return centre * inv, inv


def normalise_back(dn, hat, inv, gain):
    d_hat = dn * gain
    mean, along = lane_means([d_hat, d_hat * hat])
    return inv * (d_hat - mean - hat * along)


def head_mask():
    rows = lax.broadcasted_iota(jnp.int32, (HEADS * LEN, CH), 0) // LEN
    lanes = lax.broadcasted_iota(jnp.int32, (HEADS * LEN, CH), 1) // (CH // HEADS)
    return (rows == lanes).astype(F32).astype(BF16)


def spread_heads(v, mask):
    return jnp.concatenate([v] * HEADS, axis=0) * mask


def gather_heads(v):
    lane = lax.broadcasted_iota(jnp.int32, (LEN, CH), 1)
    size = CH // HEADS
    out = v[3 * LEN :]
    for h in (2, 1, 0):
        out = jnp.where(lane < (h + 1) * size, v[h * LEN : (h + 1) * LEN], out)
    return out


def rows_of(values, w):
    return values[w * LEN : (w + 1) * LEN]


def groups_of(tokens, group):
    count = tokens // LEN
    return [range(start, min(start + group, count)) for start in range(0, count, group)]


def attention(qkv, bias_t, mask, group):
    outs, weights = [], []
    for windows in groups_of(qkv.shape[0], group):
        parts = [rows_of(qkv, w) for w in windows]
        scores = [nt(x[:, CH : 2 * CH], spread_heads(x[:, :CH], mask)) * SCALE + bias_t for x in parts]
        e = [jnp.exp(x - jnp.max(x, axis=0, keepdims=True)) for x in scores]
        p = [(x * (1.0 / jnp.sum(x, axis=0, keepdims=True))).astype(BF16) for x in e]
        o = [tn(x, y[:, 2 * CH :]) for x, y in zip(p, parts)]
        outs += [gather_heads(x).astype(BF16) for x in o]
        weights += p
    return jnp.concatenate(outs, axis=0), jnp.concatenate(weights, axis=0)


def attention_back(d_o, qkv, p, mask, group):
    done, bias = [], None
    for windows in groups_of(qkv.shape[0], group):
        parts = [rows_of(qkv, w) for w in windows]
        weights = [rows_of(p, w) for w in windows]
        do_spread = [spread_heads(rows_of(d_o, w), mask) for w in windows]
        dp = [nt(x[:, 2 * CH :], y) for x, y in zip(parts, do_spread)]
        dv = [nn(x, y) for x, y in zip(weights, do_spread)]
        weights = [x.astype(F32) for x in weights]
        ds = [x * (y - jnp.sum(y * x, axis=0, keepdims=True)) for x, y in zip(weights, dp)]
        dsb = [x.astype(BF16) for x in ds]
        dk = [nn(x, spread_heads(y[:, :CH], mask)) * SCALE for x, y in zip(dsb, parts)]
        dq = [gather_heads(tn(x, y[:, CH : 2 * CH])) * SCALE for x, y in zip(dsb, parts)]
        for x in ds:
            bias = x if bias is None else bias + x
        done += [jnp.concatenate(x, axis=1).astype(BF16) for x in zip(dq, dk, dv)]
    return jnp.concatenate(done, axis=0), bias


def gelu_and_slope(u):
    c = 0.7978845608028654
    sq = u * u
    s = 0.5 * jnp.tanh(u * (c + (c * 0.044715) * sq)) + 0.5
    m = u * s
    return m, s + m * (1.0 - s) * (2.0 * c + (6.0 * c * 0.044715) * sq)


def forward(x, w_qkv, w_proj, gains, bias, mask, group):
    hat1, inv1 = normalise(x)
    gain = gains()
    a1 = (hat1 * gain[0:1]).astype(BF16)
    qkv = nn(a1, w_qkv()).astype(BF16)
    o, p = attention(qkv, turned_bias(bias()), mask, group)
    h = (x + nn(o, w_proj())).astype(BF16).astype(F32)
    hat2, inv2 = normalise(h)
    a2 = (hat2 * gain[1:2]).astype(BF16)
    return h, (hat1, inv1, a1, p, o, hat2, inv2, a2), qkv


def backward(gy, kept, qkv, w_qkv, w_proj, w_up, w_down, g1, g2, mask, group):
    hat1, inv1, a1, p, o, hat2, inv2, a2 = kept
    m, slope = gelu_and_slope(nn(a2, w_up))
    m = m.astype(BF16)
    du = (nt(gy, w_down) * slope).astype(BF16)
    da2 = nt(du, w_up)
    gain2 = jnp.sum(da2 * hat2, axis=0, keepdims=True)
    dh = gy.astype(F32) + normalise_back(da2, hat2, inv2, g2)
    dhb = dh.astype(BF16)
    d_o = nt(dhb, w_proj).astype(BF16)
    dqkv, bias = attention_back(d_o, qkv, p, mask, group)
    da1 = nt(dqkv, w_qkv)
    gain1 = jnp.sum(da1 * hat1, axis=0, keepdims=True)
    dx = dh + normalise_back(da1, hat1, inv1, g1)
    return dx, (gy, m, a2, du, o, dhb, a1, dqkv), bias, gain1, gain2


def pack(pack_ref, pairs, bias, gain1, gain2, old=None):
    gy, m, a2, du, o, dhb, a1, dqkv = pairs

    def put(at, value):
        rows = slice(at, at + value.shape[0])
        pack_ref[rows] = value if old is None else value + old[rows].astype(F32)

    down, up, qkv = tn(gy, m), tn(a2, du), tn(a1, dqkv)
    for j in range(3):
        put(ROW_QKV + CH * j, qkv[:, CH * j : CH * (j + 1)])
    put(ROW_PROJ, tn(o, dhb))
    for j in range(4):
        put(ROW_UP + CH * j, up[:, CH * j : CH * (j + 1)])
        put(ROW_DOWN + CH * j, down[:, CH * j : CH * (j + 1)].T)
    put(ROW_BIAS, bias[:, :CH])
    put(ROW_BIAS + LEN, bias[:, CH:])
    put(ROW_GAIN, jnp.concatenate([gain1, gain2, jnp.zeros((ROWS - ROW_GAIN - 2, CH), F32)], axis=0))


def to_windows(tile):
    rows, cols, ch = tile.shape
    return tile.reshape(WIN, cols // WIN, WIN, ch).transpose(1, 0, 2, 3).reshape(-1, ch)


def from_windows(tokens):
    count = tokens.shape[0] // LEN
    return tokens.reshape(count, WIN, WIN, CH).transpose(1, 0, 2, 3).reshape(WIN, count * WIN, CH)


def turned_bias(bias):
    return jnp.concatenate([bias[h].T for h in range(HEADS)], axis=1)


def first_half(x, group, w_qkv, w_proj, w_up, w_down, gains, bias):
    h, kept, _ = forward(to_windows(x.astype(F32)), w_qkv, w_proj, gains, bias, head_mask(), group)
    m, _ = gelu_and_slope(nn(kept[7], w_up()))
    return from_windows(h + nn(m.astype(BF16), w_down()))


def first_kernel(*refs):
    sources, (top_ref, low_ref, edge_ref), refs = refs[:8], refs[8:11], refs[11:]
    targets, sem = refs[:8], refs[8]
    wide = sources[0].shape[1] // 2
    moves = [(sources[0].at[:, 0:wide], targets[0])]
    moves += [(source.at[0], target) for source, target in zip(sources[1:7], targets[1:7])]
    moves += [(sources[7].at[HALF:, 0:WIN], targets[7])]
    copies = [pltpu.make_async_copy(source, target, sem.at[i]) for i, (source, target) in enumerate(moves)]
    for i in (0, 5, 1, 6, 2, 3, 4, 7):
        copies[i].start(priority=1)

    def fetched(i):
        copies[i].wait()
        return targets[i][...]

    parts = [functools.partial(fetched, i) for i in range(1, 7)]
    tile = first_half(fetched(0), 2, *parts)
    top_ref[...] = tile[:HALF].astype(BF16)
    low_ref[...] = tile[HALF:].astype(BF16)
    edge_ref[0:HALF] = tile[HALF:, 0:WIN].astype(BF16)
    edge_ref[HALF:] = fetched(7)


def at(ref, i):
    return lambda: ref[i]


def next_kernel(x_ref, w_qkv_ref, w_proj_ref, w_up_ref, w_down_ref, gain_ref, bias_ref, top_ref, low_ref):
    wide = x_ref.shape[1] // 2
    parts = [at(ref, 0) for ref in (w_qkv_ref, w_proj_ref, w_up_ref, w_down_ref, gain_ref, bias_ref)]
    tile = first_half(x_ref[:, wide:], 4, *parts)
    top_ref[...] = tile[:HALF].astype(BF16)
    low_ref[...] = tile[HALF:].astype(BF16)


KEPT = (CH, CH, CH, HEADS * LEN, CH, CH, CH, CH)


def kept_slices():
    starts = [sum(KEPT[:i]) for i in range(len(KEPT))]
    return [slice(start, start + width) for start, width in zip(starts, KEPT)]


def keep_kernel(part, x_ref, w_qkv_ref, w_proj_ref, gain_ref, bias_ref, kept_ref):
    wide = x_ref.shape[1] // 2
    x = to_windows(x_ref[:, part * wide : (part + 1) * wide].astype(F32))
    _, kept, _ = forward(x, at(w_qkv_ref, 0), at(w_proj_ref, 0), at(gain_ref, 0), at(bias_ref, 0), head_mask(), (8, 2)[part])
    for place, value, width in zip(kept_slices(), kept, KEPT):
        kept_ref[:, place] = jnp.broadcast_to(value, (x.shape[0], width)).astype(BF16)


def second_half(x, gy, group, w_qkv_ref, w_proj_ref, w_up_ref, w_down_ref, gain_ref, bias_ref):
    mask = head_mask()
    _, kept, qkv = forward(
        to_windows(x), at(w_qkv_ref, 1), at(w_proj_ref, 1), at(gain_ref, 1), at(bias_ref, 1), mask, group
    )
    w_qkv, w_proj, w_up, w_down = w_qkv_ref[1], w_proj_ref[1], w_up_ref[1], w_down_ref[1]
    g1, g2 = gain_ref[1, 0:1], gain_ref[1, 1:2]
    return backward(to_windows(gy).astype(BF16), kept, qkv, w_qkv, w_proj, w_up, w_down, g1, g2, mask, group)


def second_kernel(*refs):
    low_ref, below_ref, g_own_ref, g_below_ref = refs[:4]
    weights, (dx_ref, pack_ref, frame_ref) = refs[4:10], refs[10:]
    wide = low_ref.shape[1]
    frame_ref[0:HALF, 0:wide] = low_ref[...].astype(F32)
    frame_ref[HALF:, 0:wide] = below_ref[...].astype(F32)
    x = frame_ref[:, HALF : wide - HALF]
    frame_ref[0:HALF, 0:wide] = g_own_ref[HALF:, 0:wide].astype(F32)
    frame_ref[HALF:, 0:wide] = g_below_ref[0:HALF, 0:wide].astype(F32)
    gy = frame_ref[:, HALF : wide - HALF]
    dx, *sums = second_half(x, gy, 7, *weights)
    dx_ref[...] = dx.astype(BF16)
    pack(pack_ref, *sums)


def third_kernel(*refs):
    low_a_ref, low_b_ref, below_a_ref, below_b_ref, g_own_ref, g_below_ref, edge_ref = refs[:7]
    weights, (dx_ref, old_ref, dtop_ref, dlow_ref, dedge_ref, pack_ref, frame_ref) = refs[7:13], refs[13:]
    wide, cols = low_a_ref.shape[1], g_own_ref.shape[1]
    span = cols - wide + WIN
    frame_ref[0:HALF, 0:WIN] = low_a_ref[:, wide - WIN :].astype(F32)
    frame_ref[HALF:, 0:WIN] = below_a_ref[:, wide - WIN :].astype(F32)
    frame_ref[0:HALF, WIN:span] = low_b_ref[...].astype(F32)
    frame_ref[HALF:, WIN:span] = below_b_ref[...].astype(F32)
    frame_ref[0:HALF, span : span + WIN] = edge_ref[0:HALF].astype(F32)
    frame_ref[HALF:, span : span + WIN] = edge_ref[WIN : WIN + HALF].astype(F32)
    x = frame_ref[:, HALF : span + HALF]
    frame_ref[0:HALF, 0:span] = g_own_ref[HALF:, wide - WIN :].astype(F32)
    frame_ref[HALF:, 0:span] = g_below_ref[0:HALF, wide - WIN :].astype(F32)
    frame_ref[0:HALF, span : span + WIN] = edge_ref[HALF:WIN].astype(F32)
    frame_ref[HALF:, span : span + WIN] = edge_ref[WIN + HALF :].astype(F32)
    gy = frame_ref[:, HALF : span + HALF]
    dx, *sums = second_half(x, gy, 3, *weights)
    pack(pack_ref, *sums, old_ref)
    tile = from_windows(jnp.concatenate([dx_ref[...].astype(F32), dx], axis=0))
    dtop_ref[...] = tile[:HALF].astype(BF16)
    dlow_ref[...] = tile[HALF:].astype(BF16)
    dedge_ref[...] = tile[:HALF, cols - WIN :].astype(BF16)


def last_kernel(*refs):
    (own, above, left), kept_refs, refs = refs[:3], refs[3:5], refs[5:]
    w_qkv_ref, w_proj_ref, w_up_ref, w_down_ref, gain_ref, other_ref, core_ref = refs[:7]
    dx_ref, keep_ref, send_ref, frame_ref, pack_ref = refs[7:]
    cols = own.shape[1]
    frame_ref[:, 0:WIN] = left[...].astype(F32)
    first = frame_ref[:, HALF:WIN]
    frame_ref[:, 0:HALF] = first
    frame_ref[HALF:, HALF : HALF + cols] = own[...].astype(F32)
    frame_ref[0:HALF, HALF : HALF + cols] = above[...].astype(F32)
    gy = to_windows(frame_ref[:, 0:cols]).astype(BF16)
    kept = [jnp.concatenate([ref[:, place] for ref in kept_refs], axis=0) for place in kept_slices()]
    kept = [v.astype(F32) if i in (0, 1, 5, 6) else v for i, v in enumerate(kept)]
    g1, g2 = gain_ref[0, 0:1], gain_ref[0, 1:2]
    dx, pairs, bias, gain1, gain2 = backward(
        gy, kept, nn(kept[2], w_qkv_ref[0]).astype(BF16), w_qkv_ref[0], w_proj_ref[0], w_up_ref[0], w_down_ref[0], g1, g2, head_mask(), 4
    )
    dx_ref[...] = from_windows(dx).astype(BF16)
    pack(pack_ref, pairs, bias, gain1, gain2)
    first_core = core_ref[0] == 0

    @pl.when(first_core)
    def _():
        keep_ref[...] = pack_ref[...]
        send_ref[...] = other_ref[...].astype(BF16)

    @pl.when(jnp.logical_not(first_core))
    def _():
        keep_ref[...] = other_ref[...]
        send_ref[...] = pack_ref[...].astype(BF16)


def unpack_kernel(core_ref, own_ref, other_ref, *refs):
    qkv_ref, proj_ref, up_ref, down_ref, gain_ref, bias_ref, whole_ref = refs
    at = pl.multiple_of(core_ref[0] * ROWS, ROWS)
    whole_ref[pl.ds(at, ROWS)] = own_ref[...].astype(F32)
    whole_ref[pl.ds(ROWS - at, ROWS)] = other_ref[...].astype(F32)
    for b in range(2):
        at = b * ROWS
        for j in range(3):
            qkv_ref[b, :, CH * j : CH * (j + 1)] = whole_ref[at + ROW_QKV + CH * j : at + ROW_QKV + CH * (j + 1)]
        proj_ref[b] = whole_ref[at + ROW_PROJ : at + ROW_PROJ + CH]
        for j in range(4):
            up_ref[b, :, CH * j : CH * (j + 1)] = whole_ref[at + ROW_UP + CH * j : at + ROW_UP + CH * (j + 1)]
        down_ref[b] = whole_ref[at + ROW_DOWN : at + ROW_DOWN + FFN]
        for j in range(2):
            turned = whole_ref[at + ROW_BIAS + LEN * j : at + ROW_BIAS + LEN * (j + 1)].T
            bias_ref[b, 2 * j] = turned[:LEN]
            bias_ref[b, 2 * j + 1] = turned[LEN:]
        gain_ref[b] = whole_ref[at + ROW_GAIN : at + ROW_GAIN + 2]


def vmem(count):
    return [pl.BlockSpec(memory_space=pltpu.VMEM)] * count


def cost(flops, moved):
    return pl.CostEstimate(flops=flops, bytes_accessed=moved, transcendentals=0)


def shift(value, down, right):
    tall, wide = 32, 8
    pairs = []
    for r in range(tall):
        for c in range(wide):
            pairs.append((r * wide + c, (r + down) % tall * wide + (c + right) % wide))
    return lax.ppermute(value, AXES, pairs)


def swap_core(value):
    return lax.ppermute(value, "core", [(0, 1), (1, 0)])


def scatter_sum(value, axis, count):
    pieces = value.astype(BF16).reshape(count, value.shape[0] // count, CH)
    return jnp.sum(lax.all_to_all(pieces, axis, 0, 0).astype(F32), axis=0)


def collect(value, axis, count):
    spread = jnp.broadcast_to(value[None], (count, *value.shape))
    return lax.all_to_all(spread, axis, 0, 0)


def sum_over_devices(keep, send):
    total = keep + swap_core(send).astype(F32)
    total = scatter_sum(total, PLANE, 16)
    total = jnp.sum(collect(total.astype(BF16), "z", 8).astype(F32), axis=0).astype(BF16)
    total = collect(total, PLANE, 16).reshape(ROWS, CH)
    return total, swap_core(total)


def body(latent, cotangent, w_qkv, w_proj, w_up, w_down, gains, attn_bias):
    cols = latent.shape[1]
    half = jax.ShapeDtypeStruct((HALF, cols, CH), BF16)
    params = pltpu.CompilerParams(vmem_limit_bytes=VMEM_LIMIT)
    packed = jax.ShapeDtypeStruct((ROWS, CH), F32)
    core = lax.axis_index("core").reshape(1)
    weights = (w_qkv, w_proj, w_up, w_down, gains)
    g_below = shift(cotangent, -1, 0)
    tokens = WIN * cols

    wide = cols // 2
    part_a = WIN * (wide - WIN)
    side = jax.ShapeDtypeStruct((HALF, wide, CH), BF16)
    corner = jax.ShapeDtypeStruct((WIN, WIN, CH), BF16)
    top_a, low_a, edge_own = pl.pallas_call(
        first_kernel,
        out_shape=(side, side, corner),
        in_specs=[pl.BlockSpec(memory_space=pltpu.HBM)] * 8,
        out_specs=vmem(3),
        scratch_shapes=[pltpu.VMEM((WIN, wide, CH), BF16)]
        + [pltpu.VMEM(w.shape[1:], w.dtype) for w in (*weights, attn_bias)]
        + [pltpu.VMEM((HALF, WIN, CH), BF16), pltpu.SemaphoreType.DMA((8,))],
        compiler_params=pltpu.CompilerParams(vmem_limit_bytes=FIRST_LIMIT),
        cost_estimate=cost(300_000_000, 1_500_000),
        name="forward_first",
    )(latent, *weights, attn_bias, cotangent)
    below_a = shift(top_a, -1, 0)
    top_b, low_b = pl.pallas_call(
        next_kernel,
        out_shape=(side, side),
        in_specs=vmem(7),
        out_specs=vmem(2),
        compiler_params=params,
        cost_estimate=cost(300_000_000, 1_500_000),
        name="forward_next",
    )(latent, *weights, attn_bias)
    below_b = shift(top_b, -1, 0)
    edge = shift(jnp.concatenate([edge_own, below_a[:, :WIN], g_below[:HALF, :WIN]], axis=0), 0, -1)
    weights = (*weights, attn_bias)
    frame = pltpu.VMEM((WIN, cols + 2 * WIN, CH), F32)
    dx_a, pack_a = pl.pallas_call(
        second_kernel,
        out_shape=(jax.ShapeDtypeStruct((part_a, CH), BF16), packed),
        in_specs=vmem(10),
        out_specs=vmem(2),
        scratch_shapes=[frame],
        compiler_params=params,
        cost_estimate=cost(700_000_000, 3_000_000),
        name="backward_second",
    )(low_a, below_a, cotangent, g_below, *weights)
    edge, below_b, dx_a = lax.optimization_barrier((edge, below_b, dx_a))
    d_top, d_low, d_edge, pack_two = pl.pallas_call(
        third_kernel,
        out_shape=(half, half, jax.ShapeDtypeStruct((HALF, WIN, CH), BF16), packed),
        in_specs=vmem(15),
        out_specs=vmem(4),
        scratch_shapes=[frame],
        compiler_params=params,
        cost_estimate=cost(800_000_000, 3_000_000),
        name="backward_third",
    )(low_a, low_b, below_a, below_b, cotangent, g_below, edge, *weights, dx_a, pack_a)
    d_above = shift(d_low, 1, 0)
    kept = []
    for part in range(2):
        made = pl.pallas_call(
            functools.partial(keep_kernel, part),
            out_shape=jax.ShapeDtypeStruct((WIN * wide, sum(KEPT)), BF16),
            in_specs=vmem(5),
            out_specs=vmem(1)[0],
            compiler_params=params,
            cost_estimate=cost(300_000_000, 2_000_000),
            name="keep_first",
        )(latent, w_qkv, w_proj, gains, attn_bias)
        if part == 0:
            d_above, made = lax.optimization_barrier((d_above, made))
            d_left = shift(jnp.concatenate([d_above[:, cols - WIN :], d_edge], axis=0), 0, 1)
        else:
            d_left, made = lax.optimization_barrier((d_left, made))
        kept.append(made)
    dx, keep, send = pl.pallas_call(
        last_kernel,
        out_shape=(
            jax.ShapeDtypeStruct(latent.shape, BF16),
            packed,
            jax.ShapeDtypeStruct((ROWS, CH), BF16),
        ),
        in_specs=vmem(11) + [pl.BlockSpec(memory_space=pltpu.SMEM)],
        out_specs=vmem(3),
        scratch_shapes=[frame, pltpu.VMEM((ROWS, CH), F32)],
        compiler_params=params,
        cost_estimate=cost(1_500_000_000, 4_000_000),
        name="backward_first",
    )(d_top, d_above, d_left, *kept, *weights[:5], pack_two, core)
    parts = sum_over_devices(keep, send)
    qkv, proj, up, down, gain, bias = pl.pallas_call(
        unpack_kernel,
        out_shape=(
            jax.ShapeDtypeStruct((2, CH, 3 * CH), F32),
            jax.ShapeDtypeStruct((2, CH, CH), F32),
            jax.ShapeDtypeStruct((2, CH, FFN), F32),
            jax.ShapeDtypeStruct((2, FFN, CH), F32),
            jax.ShapeDtypeStruct((2, 2, CH), F32),
            jax.ShapeDtypeStruct((2, HEADS, LEN, LEN), F32),
        ),
        in_specs=[pl.BlockSpec(memory_space=pltpu.SMEM)] + vmem(2),
        out_specs=vmem(6),
        scratch_shapes=[pltpu.VMEM((2 * ROWS, CH), F32)],
        compiler_params=params,
        cost_estimate=cost(1_000_000, 4_000_000),
        name="unpack",
    )(core, *parts)
    return dx, qkv, proj, up, down, gain, bias


def solution(mesh):
    fine = jax.sharding.Mesh(mesh.devices.reshape(8, 2, 2, 4, 2), AXES)
    tiles = P(("z", "yh", "core"), ("x", "yl"), None)
    in_specs = (tiles, tiles, P(), P(), P(), P(), P(), P())
    out_specs = (tiles, P(), P(), P(), P(), P(), P())
    return jax.shard_map(body, mesh=fine, in_specs=in_specs, out_specs=out_specs, check_vma=False)
```

```python
import functools

import jax
import jax.numpy as jnp
from jax import lax
from jax.experimental import pallas as pl
from jax.experimental.pallas import tpu as pltpu
from jax.sharding import PartitionSpec as P

WIN = 8
HALF = 4
LEN = 64
CH = 128
HEADS = 4
FFN = 512
EPS = 1e-05
SCALE = (CH // HEADS) ** -0.5
F32 = jnp.float32
BF16 = jnp.bfloat16
VMEM_LIMIT = 32 * 1024 * 1024
FIRST_LIMIT = 57 * 1000 * 1000

ROW_QKV, ROW_PROJ, ROW_UP, ROW_DOWN, ROW_BIAS, ROW_GAIN, ROWS = 0, 384, 512, 1024, 1536, 1664, 1792
AXES = ("z", "yh", "core", "x", "yl")
PLANE = ("yh", "x", "yl")


def nn(a, b):
    return lax.dot_general(a, b, (((1,), (0,)), ((), ())), preferred_element_type=F32)


def nt(a, b):
    return lax.dot_general(a, b, (((1,), (1,)), ((), ())), preferred_element_type=F32)


def tn(a, b):
    return lax.dot_general(a, b, (((0,), (0,)), ((), ())), preferred_element_type=F32)


def lane_means(parts):
    width = len(parts) * CH
    block = lax.broadcasted_iota(jnp.int32, (width, width), 0) // CH == lax.broadcasted_iota(jnp.int32, (width, width), 1) // CH
    ones = (block.astype(F32) * (1.0 / CH)).astype(BF16)
    sums = nn(jnp.concatenate([p.astype(BF16) for p in parts], axis=1), ones)
    return [sums[:, CH * i : CH * (i + 1)] for i in range(len(parts))]


def normalise(v):
    centre = v - jnp.mean(v, axis=-1, keepdims=True)
    spread = jnp.mean(centre * centre, axis=-1, keepdims=True)
    inv = lax.rsqrt(spread + EPS)
    return centre * inv, inv


def normalise_back(dn, hat, inv, gain):
    d_hat = dn * gain
    mean, along = lane_means([d_hat, d_hat * hat])
    return inv * (d_hat - mean - hat * along)


def head_mask():
    rows = lax.broadcasted_iota(jnp.int32, (HEADS * LEN, CH), 0) // LEN
    lanes = lax.broadcasted_iota(jnp.int32, (HEADS * LEN, CH), 1) // (CH // HEADS)
    return (rows == lanes).astype(F32).astype(BF16)


def spread_heads(v, mask):
    return jnp.concatenate([v] * HEADS, axis=0) * mask


def gather_heads(v):
    lane = lax.broadcasted_iota(jnp.int32, (LEN, CH), 1)
    size = CH // HEADS
    out = v[3 * LEN :]
    for h in (2, 1, 0):
        out = jnp.where(lane < (h + 1) * size, v[h * LEN : (h + 1) * LEN], out)
    return out


def rows_of(values, w):
    return values[w * LEN : (w + 1) * LEN]


def groups_of(tokens, group):
    count = tokens // LEN
    return [range(start, min(start + group, count)) for start in range(0, count, group)]


def in_stages(stages, groups):
    state = [None] * len(groups)
    for step in range(len(groups) + len(stages) - 1):
        for s in reversed(range(len(stages))):
            g = step - s
            if 0 <= g < len(groups):
                state[g] = stages[s](groups[g], state[g])
    return state


def attention(qkv, bias_t, mask, group):
    def scores(windows, _):
        parts = [rows_of(qkv, w) for w in windows]
        return parts, [nt(x[:, CH : 2 * CH], spread_heads(x[:, :CH], mask)) * SCALE + bias_t for x in parts]

    def softmax(_, state):
        parts, values = state
        e = [jnp.exp(x - jnp.max(x, axis=0, keepdims=True)) for x in values]
        return parts, [(x * (1.0 / jnp.sum(x, axis=0, keepdims=True))).astype(BF16) for x in e]

    def mix(_, state):
        parts, p = state
        o = [tn(x, y[:, 2 * CH :]) for x, y in zip(p, parts)]
        return [gather_heads(x).astype(BF16) for x in o], p

    done = in_stages((scores, softmax, mix), groups_of(qkv.shape[0], group))
    return jnp.concatenate(sum((x for x, _ in done), []), axis=0), jnp.concatenate(sum((x for _, x in done), []), axis=0)


def attention_back(d_o, qkv, p, mask, group):
    def spread(windows, _):
        parts = [rows_of(qkv, w) for w in windows]
        weights = [rows_of(p, w) for w in windows]
        do_spread = [spread_heads(rows_of(d_o, w), mask) for w in windows]
        dp = [nt(x[:, 2 * CH :], y) for x, y in zip(parts, do_spread)]
        return parts, weights, dp, [nn(x, y) for x, y in zip(weights, do_spread)]

    def softmax(_, state):
        parts, weights, dp, dv = state
        weights = [x.astype(F32) for x in weights]
        return parts, [x * (y - jnp.sum(y * x, axis=0, keepdims=True)) for x, y in zip(weights, dp)], dv

    def mix(_, state):
        parts, ds, dv = state
        dsb = [x.astype(BF16) for x in ds]
        dk = [nn(x, spread_heads(y[:, :CH], mask)) * SCALE for x, y in zip(dsb, parts)]
        dq = [gather_heads(tn(x, y[:, CH : 2 * CH])) * SCALE for x, y in zip(dsb, parts)]
        return [jnp.concatenate(x, axis=1).astype(BF16) for x in zip(dq, dk, dv)], sum(ds[1:], ds[0])

    done = in_stages((spread, softmax, mix), groups_of(qkv.shape[0], group))
    bias = sum((x for _, x in done[1:]), done[0][1])
    return jnp.concatenate(sum((x for x, _ in done), []), axis=0), bias


def gelu_and_slope(u):
    c = 0.7978845608028654
    sq = u * u
    s = 0.5 * jnp.tanh(u * (c + (c * 0.044715) * sq)) + 0.5
    m = u * s
    return m, s + m * (1.0 - s) * (2.0 * c + (6.0 * c * 0.044715) * sq)


def forward(x, w_qkv, w_proj, gains, bias, mask, group):
    hat1, inv1 = normalise(x)
    gain = gains()
    a1 = (hat1 * gain[0:1]).astype(BF16)
    qkv = nn(a1, w_qkv()).astype(BF16)
    o, p = attention(qkv, turned_bias(bias()), mask, group)
    h = (x + nn(o, w_proj())).astype(BF16).astype(F32)
    hat2, inv2 = normalise(h)
    a2 = (hat2 * gain[1:2]).astype(BF16)
    return h, (hat1, inv1, a1, p, o, hat2, inv2, a2), qkv


def backward(gy, kept, qkv, w_qkv, w_proj, w_up, w_down, g1, g2, mask, group):
    hat1, inv1, a1, p, o, hat2, inv2, a2 = kept
    m, slope = gelu_and_slope(nn(a2, w_up))
    m = m.astype(BF16)
    du = (nt(gy, w_down) * slope).astype(BF16)
    da2 = nt(du, w_up)
    down, up = tn(gy, m), tn(a2, du)
    gain2 = jnp.sum(da2 * hat2, axis=0, keepdims=True)
    dh = gy.astype(F32) + normalise_back(da2, hat2, inv2, g2)
    dhb = dh.astype(BF16)
    d_o = nt(dhb, w_proj).astype(BF16)
    proj = tn(o, dhb)
    dqkv, bias = attention_back(d_o, qkv, p, mask, group)
    da1 = nt(dqkv, w_qkv)
    grads = (tn(a1, dqkv), proj, up, down)
    gain1 = jnp.sum(da1 * hat1, axis=0, keepdims=True)
    dx = dh + normalise_back(da1, hat1, inv1, g1)
    return dx, grads, bias, gain1, gain2


def pack(pack_ref, grads, bias, gain1, gain2, old=None):
    qkv, proj, up, down = grads

    def put(at, value):
        rows = slice(at, at + value.shape[0])
        pack_ref[rows] = value if old is None else value + old[rows].astype(F32)

    for j in range(3):
        put(ROW_QKV + CH * j, qkv[:, CH * j : CH * (j + 1)])
    put(ROW_PROJ, proj)
    for j in range(4):
        put(ROW_UP + CH * j, up[:, CH * j : CH * (j + 1)])
        put(ROW_DOWN + CH * j, down[:, CH * j : CH * (j + 1)].T)
    put(ROW_BIAS, bias[:, :CH])
    put(ROW_BIAS + LEN, bias[:, CH:])
    put(ROW_GAIN, jnp.concatenate([gain1, gain2, jnp.zeros((ROWS - ROW_GAIN - 2, CH), F32)], axis=0))


def to_windows(tile):
    rows, cols, ch = tile.shape
    return tile.reshape(WIN, cols // WIN, WIN, ch).transpose(1, 0, 2, 3).reshape(-1, ch)


def from_windows(tokens):
    count = tokens.shape[0] // LEN
    return tokens.reshape(count, WIN, WIN, CH).transpose(1, 0, 2, 3).reshape(WIN, count * WIN, CH)


def turned_bias(bias):
    return jnp.concatenate([bias[h].T for h in range(HEADS)], axis=1)


def first_half(x, group, w_qkv, w_proj, w_up, w_down, gains, bias):
    h, kept, _ = forward(to_windows(x.astype(F32)), w_qkv, w_proj, gains, bias, head_mask(), group)
    m, _ = gelu_and_slope(nn(kept[7], w_up()))
    return from_windows(h + nn(m.astype(BF16), w_down()))


def first_kernel(*refs):
    sources, (top_ref, low_ref, edge_ref), refs = refs[:8], refs[8:11], refs[11:]
    targets, sem = refs[:8], refs[8]
    wide = sources[0].shape[1] // 2
    moves = [(sources[0].at[:, 0:wide], targets[0])]
    moves += [(source.at[0], target) for source, target in zip(sources[1:7], targets[1:7])]
    moves += [(sources[7].at[HALF:, 0:WIN], targets[7])]
    copies = [pltpu.make_async_copy(source, target, sem.at[i]) for i, (source, target) in enumerate(moves)]
    for i in (0, 5, 1, 6, 2, 3, 4, 7):
        copies[i].start(priority=1)

    def fetched(i):
        copies[i].wait()
        return targets[i][...]

    parts = [functools.partial(fetched, i) for i in range(1, 7)]
    tile = first_half(fetched(0), 8, *parts)
    top_ref[...] = tile[:HALF].astype(BF16)
    low_ref[...] = tile[HALF:].astype(BF16)
    edge_ref[0:HALF] = tile[HALF:, 0:WIN].astype(BF16)
    edge_ref[HALF:] = fetched(7)


def at(ref, i):
    return lambda: ref[i]


def next_kernel(x_ref, w_qkv_ref, w_proj_ref, w_up_ref, w_down_ref, gain_ref, bias_ref, top_ref, low_ref):
    wide = x_ref.shape[1] // 2
    parts = [at(ref, 0) for ref in (w_qkv_ref, w_proj_ref, w_up_ref, w_down_ref, gain_ref, bias_ref)]
    tile = first_half(x_ref[:, wide:], 4, *parts)
    top_ref[...] = tile[:HALF].astype(BF16)
    low_ref[...] = tile[HALF:].astype(BF16)


KEPT = (CH, CH, CH, HEADS * LEN, CH, CH, CH, CH)


def kept_slices():
    starts = [sum(KEPT[:i]) for i in range(len(KEPT))]
    return [slice(start, start + width) for start, width in zip(starts, KEPT)]


def keep_kernel(part, x_ref, w_qkv_ref, w_proj_ref, gain_ref, bias_ref, kept_ref):
    wide = x_ref.shape[1] // 2
    x = to_windows(x_ref[:, part * wide : (part + 1) * wide].astype(F32))
    _, kept, _ = forward(x, at(w_qkv_ref, 0), at(w_proj_ref, 0), at(gain_ref, 0), at(bias_ref, 0), head_mask(), (8, 2)[part])
    for place, value, width in zip(kept_slices(), kept, KEPT):
        kept_ref[:, place] = jnp.broadcast_to(value, (x.shape[0], width)).astype(BF16)


def second_half(x, gy, group, w_qkv_ref, w_proj_ref, w_up_ref, w_down_ref, gain_ref, bias_ref):
    mask = head_mask()
    _, kept, qkv = forward(
        to_windows(x), at(w_qkv_ref, 1), at(w_proj_ref, 1), at(gain_ref, 1), at(bias_ref, 1), mask, group
    )
    w_qkv, w_proj, w_up, w_down = w_qkv_ref[1], w_proj_ref[1], w_up_ref[1], w_down_ref[1]
    g1, g2 = gain_ref[1, 0:1], gain_ref[1, 1:2]
    return backward(to_windows(gy).astype(BF16), kept, qkv, w_qkv, w_proj, w_up, w_down, g1, g2, mask, group)


def second_kernel(*refs):
    low_ref, below_ref, g_own_ref, g_below_ref = refs[:4]
    weights, (dx_ref, pack_ref, frame_ref) = refs[4:10], refs[10:]
    wide = low_ref.shape[1]
    frame_ref[0:HALF, 0:wide] = low_ref[...].astype(F32)
    frame_ref[HALF:, 0:wide] = below_ref[...].astype(F32)
    x = frame_ref[:, HALF : wide - HALF]
    frame_ref[0:HALF, 0:wide] = g_own_ref[HALF:, 0:wide].astype(F32)
    frame_ref[HALF:, 0:wide] = g_below_ref[0:HALF, 0:wide].astype(F32)
    gy = frame_ref[:, HALF : wide - HALF]
    dx, *sums = second_half(x, gy, 7, *weights)
    dx_ref[...] = dx.astype(BF16)
    pack(pack_ref, *sums)


def third_kernel(*refs):
    low_a_ref, low_b_ref, below_a_ref, below_b_ref, g_own_ref, g_below_ref, edge_ref = refs[:7]
    weights, (dx_ref, old_ref, dtop_ref, dlow_ref, dedge_ref, pack_ref, frame_ref) = refs[7:13], refs[13:]
    wide, cols = low_a_ref.shape[1], g_own_ref.shape[1]
    span = cols - wide + WIN
    frame_ref[0:HALF, 0:WIN] = low_a_ref[:, wide - WIN :].astype(F32)
    frame_ref[HALF:, 0:WIN] = below_a_ref[:, wide - WIN :].astype(F32)
    frame_ref[0:HALF, WIN:span] = low_b_ref[...].astype(F32)
    frame_ref[HALF:, WIN:span] = below_b_ref[...].astype(F32)
    frame_ref[0:HALF, span : span + WIN] = edge_ref[0:HALF].astype(F32)
    frame_ref[HALF:, span : span + WIN] = edge_ref[WIN : WIN + HALF].astype(F32)
    x = frame_ref[:, HALF : span + HALF]
    frame_ref[0:HALF, 0:span] = g_own_ref[HALF:, wide - WIN :].astype(F32)
    frame_ref[HALF:, 0:span] = g_below_ref[0:HALF, wide - WIN :].astype(F32)
    frame_ref[0:HALF, span : span + WIN] = edge_ref[HALF:WIN].astype(F32)
    frame_ref[HALF:, span : span + WIN] = edge_ref[WIN + HALF :].astype(F32)
    gy = frame_ref[:, HALF : span + HALF]
    dx, *sums = second_half(x, gy, 9, *weights)
    pack(pack_ref, *sums, old_ref)
    tile = from_windows(jnp.concatenate([dx_ref[...].astype(F32), dx], axis=0))
    dtop_ref[...] = tile[:HALF].astype(BF16)
    dlow_ref[...] = tile[HALF:].astype(BF16)
    dedge_ref[...] = tile[:HALF, cols - WIN :].astype(BF16)


def last_kernel(*refs):
    (own, above, left), kept_refs, refs = refs[:3], refs[3:5], refs[5:]
    w_qkv_ref, w_proj_ref, w_up_ref, w_down_ref, gain_ref, other_ref, core_ref = refs[:7]
    dx_ref, keep_ref, send_ref, frame_ref, pack_ref = refs[7:]
    cols = own.shape[1]
    frame_ref[:, 0:WIN] = left[...].astype(F32)
    first = frame_ref[:, HALF:WIN]
    frame_ref[:, 0:HALF] = first
    frame_ref[HALF:, HALF : HALF + cols] = own[...].astype(F32)
    frame_ref[0:HALF, HALF : HALF + cols] = above[...].astype(F32)
    gy = to_windows(frame_ref[:, 0:cols]).astype(BF16)
    kept = [jnp.concatenate([ref[:, place] for ref in kept_refs], axis=0) for place in kept_slices()]
    kept = [v.astype(F32) if i in (0, 1, 5, 6) else v for i, v in enumerate(kept)]
    g1, g2 = gain_ref[0, 0:1], gain_ref[0, 1:2]
    dx, grads, bias, gain1, gain2 = backward(
        gy, kept, nn(kept[2], w_qkv_ref[0]).astype(BF16), w_qkv_ref[0], w_proj_ref[0], w_up_ref[0], w_down_ref[0], g1, g2, head_mask(), 4
    )
    dx_ref[...] = from_windows(dx).astype(BF16)
    pack(pack_ref, grads, bias, gain1, gain2)
    first_core = core_ref[0] == 0

    @pl.when(first_core)
    def _():
        keep_ref[...] = pack_ref[...]
        send_ref[...] = other_ref[...].astype(BF16)

    @pl.when(jnp.logical_not(first_core))
    def _():
        keep_ref[...] = other_ref[...]
        send_ref[...] = pack_ref[...].astype(BF16)


def unpack_kernel(core_ref, own_ref, other_ref, *refs):
    qkv_ref, proj_ref, up_ref, down_ref, gain_ref, bias_ref, whole_ref = refs
    at = pl.multiple_of(core_ref[0] * ROWS, ROWS)
    whole_ref[pl.ds(at, ROWS)] = own_ref[...].astype(F32)
    whole_ref[pl.ds(ROWS - at, ROWS)] = other_ref[...].astype(F32)
    for b in range(2):
        at = b * ROWS
        for j in range(3):
            qkv_ref[b, :, CH * j : CH * (j + 1)] = whole_ref[at + ROW_QKV + CH * j : at + ROW_QKV + CH * (j + 1)]
        proj_ref[b] = whole_ref[at + ROW_PROJ : at + ROW_PROJ + CH]
        for j in range(4):
            up_ref[b, :, CH * j : CH * (j + 1)] = whole_ref[at + ROW_UP + CH * j : at + ROW_UP + CH * (j + 1)]
        down_ref[b] = whole_ref[at + ROW_DOWN : at + ROW_DOWN + FFN]
        for j in range(2):
            turned = whole_ref[at + ROW_BIAS + LEN * j : at + ROW_BIAS + LEN * (j + 1)].T
            bias_ref[b, 2 * j] = turned[:LEN]
            bias_ref[b, 2 * j + 1] = turned[LEN:]
        gain_ref[b] = whole_ref[at + ROW_GAIN : at + ROW_GAIN + 2]


def vmem(count):
    return [pl.BlockSpec(memory_space=pltpu.VMEM)] * count


def cost(flops, moved):
    return pl.CostEstimate(flops=flops, bytes_accessed=moved, transcendentals=0)


def shift(value, down, right):
    tall, wide = 32, 8
    pairs = []
    for r in range(tall):
        for c in range(wide):
            pairs.append((r * wide + c, (r + down) % tall * wide + (c + right) % wide))
    return lax.ppermute(value, AXES, pairs)


def swap_core(value):
    return lax.ppermute(value, "core", [(0, 1), (1, 0)])


def scatter_sum(value, axis, count):
    pieces = value.astype(BF16).reshape(count, value.shape[0] // count, CH)
    return jnp.sum(lax.all_to_all(pieces, axis, 0, 0).astype(F32), axis=0)


def collect(value, axis, count):
    spread = jnp.broadcast_to(value[None], (count, *value.shape))
    return lax.all_to_all(spread, axis, 0, 0)


def sum_over_devices(keep, send):
    total = keep + swap_core(send).astype(F32)
    total = scatter_sum(total, PLANE, 16)
    total = jnp.sum(collect(total.astype(BF16), "z", 8).astype(F32), axis=0).astype(BF16)
    total = collect(total, PLANE, 16).reshape(ROWS, CH)
    return total, swap_core(total)


def body(latent, cotangent, w_qkv, w_proj, w_up, w_down, gains, attn_bias):
    cols = latent.shape[1]
    half = jax.ShapeDtypeStruct((HALF, cols, CH), BF16)
    params = pltpu.CompilerParams(vmem_limit_bytes=VMEM_LIMIT)
    packed = jax.ShapeDtypeStruct((ROWS, CH), F32)
    core = lax.axis_index("core").reshape(1)
    weights = (w_qkv, w_proj, w_up, w_down, gains)
    g_below = shift(cotangent, -1, 0)
    tokens = WIN * cols

    wide = cols // 2
    part_a = WIN * (wide - WIN)
    side = jax.ShapeDtypeStruct((HALF, wide, CH), BF16)
    corner = jax.ShapeDtypeStruct((WIN, WIN, CH), BF16)
    top_a, low_a, edge_own = pl.pallas_call(
        first_kernel,
        out_shape=(side, side, corner),
        in_specs=[pl.BlockSpec(memory_space=pltpu.HBM)] * 8,
        out_specs=vmem(3),
        scratch_shapes=[pltpu.VMEM((WIN, wide, CH), BF16)]
        + [pltpu.VMEM(w.shape[1:], w.dtype) for w in (*weights, attn_bias)]
        + [pltpu.VMEM((HALF, WIN, CH), BF16), pltpu.SemaphoreType.DMA((8,))],
        compiler_params=pltpu.CompilerParams(vmem_limit_bytes=FIRST_LIMIT),
        cost_estimate=cost(300_000_000, 1_500_000),
        name="forward_first",
    )(latent, *weights, attn_bias, cotangent)
    below_a = shift(top_a, -1, 0)
    top_b, low_b = pl.pallas_call(
        next_kernel,
        out_shape=(side, side),
        in_specs=vmem(7),
        out_specs=vmem(2),
        compiler_params=params,
        cost_estimate=cost(300_000_000, 1_500_000),
        name="forward_next",
    )(latent, *weights, attn_bias)
    below_b = shift(top_b, -1, 0)
    edge = shift(jnp.concatenate([edge_own, below_a[:, :WIN], g_below[:HALF, :WIN]], axis=0), 0, -1)
    weights = (*weights, attn_bias)
    frame = pltpu.VMEM((WIN, cols + 2 * WIN, CH), F32)
    dx_a, pack_a = pl.pallas_call(
        second_kernel,
        out_shape=(jax.ShapeDtypeStruct((part_a, CH), BF16), packed),
        in_specs=vmem(10),
        out_specs=vmem(2),
        scratch_shapes=[frame],
        compiler_params=params,
        cost_estimate=cost(700_000_000, 3_000_000),
        name="backward_second",
    )(low_a, below_a, cotangent, g_below, *weights)
    edge, below_b, dx_a = lax.optimization_barrier((edge, below_b, dx_a))
    d_top, d_low, d_edge, pack_two = pl.pallas_call(
        third_kernel,
        out_shape=(half, half, jax.ShapeDtypeStruct((HALF, WIN, CH), BF16), packed),
        in_specs=vmem(15),
        out_specs=vmem(4),
        scratch_shapes=[frame],
        compiler_params=params,
        cost_estimate=cost(800_000_000, 3_000_000),
        name="backward_third",
    )(low_a, low_b, below_a, below_b, cotangent, g_below, edge, *weights, dx_a, pack_a)
    d_above = shift(d_low, 1, 0)
    kept = []
    for part in range(2):
        made = pl.pallas_call(
            functools.partial(keep_kernel, part),
            out_shape=jax.ShapeDtypeStruct((WIN * wide, sum(KEPT)), BF16),
            in_specs=vmem(5),
            out_specs=vmem(1)[0],
            compiler_params=params,
            cost_estimate=cost(300_000_000, 2_000_000),
            name="keep_first",
        )(latent, w_qkv, w_proj, gains, attn_bias)
        if part == 0:
            d_above, made = lax.optimization_barrier((d_above, made))
            d_left = shift(jnp.concatenate([d_above[:, cols - WIN :], d_edge], axis=0), 0, 1)
        else:
            d_left, made = lax.optimization_barrier((d_left, made))
        kept.append(made)
    dx, keep, send = pl.pallas_call(
        last_kernel,
        out_shape=(
            jax.ShapeDtypeStruct(latent.shape, BF16),
            packed,
            jax.ShapeDtypeStruct((ROWS, CH), BF16),
        ),
        in_specs=vmem(11) + [pl.BlockSpec(memory_space=pltpu.SMEM)],
        out_specs=vmem(3),
        scratch_shapes=[frame, pltpu.VMEM((ROWS, CH), F32)],
        compiler_params=params,
        cost_estimate=cost(1_500_000_000, 4_000_000),
        name="backward_first",
    )(d_top, d_above, d_left, *kept, *weights[:5], pack_two, core)
    parts = sum_over_devices(keep, send)
    qkv, proj, up, down, gain, bias = pl.pallas_call(
        unpack_kernel,
        out_shape=(
            jax.ShapeDtypeStruct((2, CH, 3 * CH), F32),
            jax.ShapeDtypeStruct((2, CH, CH), F32),
            jax.ShapeDtypeStruct((2, CH, FFN), F32),
            jax.ShapeDtypeStruct((2, FFN, CH), F32),
            jax.ShapeDtypeStruct((2, 2, CH), F32),
            jax.ShapeDtypeStruct((2, HEADS, LEN, LEN), F32),
        ),
        in_specs=[pl.BlockSpec(memory_space=pltpu.SMEM)] + vmem(2),
        out_specs=vmem(6),
        scratch_shapes=[pltpu.VMEM((2 * ROWS, CH), F32)],
        compiler_params=params,
        cost_estimate=cost(1_000_000, 4_000_000),
        name="unpack",
    )(core, *parts)
    return dx, qkv, proj, up, down, gain, bias


def solution(mesh):
    fine = jax.sharding.Mesh(mesh.devices.reshape(8, 2, 2, 4, 2), AXES)
    tiles = P(("z", "yh", "core"), ("x", "yl"), None)
    in_specs = (tiles, tiles, P(), P(), P(), P(), P(), P())
    out_specs = (tiles, P(), P(), P(), P(), P(), P())
    return jax.shard_map(body, mesh=fine, in_specs=in_specs, out_specs=out_specs, check_vma=False)
```

```python
import functools

import jax
import jax.numpy as jnp
from jax import lax
from jax.experimental import pallas as pl
from jax.experimental.pallas import tpu as pltpu
from jax.sharding import PartitionSpec as P

WIN = 8
HALF = 4
LEN = 64
CH = 128
HEADS = 4
FFN = 512
EPS = 1e-05
SCALE = (CH // HEADS) ** -0.5
F32 = jnp.float32
BF16 = jnp.bfloat16
VMEM_LIMIT = 32 * 1024 * 1024
FIRST_LIMIT = 57 * 1000 * 1000

ROW_QKV, ROW_PROJ, ROW_UP, ROW_DOWN, ROW_BIAS, ROW_GAIN, ROWS = 0, 384, 512, 1024, 1536, 1664, 1792
AXES = ("z", "yh", "core", "x", "yl")
PLANE = ("yh", "x", "yl")


def nn(a, b):
    return lax.dot_general(a, b, (((1,), (0,)), ((), ())), preferred_element_type=F32)


def nt(a, b):
    return lax.dot_general(a, b, (((1,), (1,)), ((), ())), preferred_element_type=F32)


def tn(a, b):
    return lax.dot_general(a, b, (((0,), (0,)), ((), ())), preferred_element_type=F32)


def lane_means(parts):
    width = len(parts) * CH
    block = lax.broadcasted_iota(jnp.int32, (width, width), 0) // CH == lax.broadcasted_iota(jnp.int32, (width, width), 1) // CH
    ones = (block.astype(F32) * (1.0 / CH)).astype(BF16)
    sums = nn(jnp.concatenate([p.astype(BF16) for p in parts], axis=1), ones)
    return [sums[:, CH * i : CH * (i + 1)] for i in range(len(parts))]


def normalise(v):
    centre = v - jnp.mean(v, axis=-1, keepdims=True)
    spread = jnp.mean(centre * centre, axis=-1, keepdims=True)
    inv = lax.rsqrt(spread + EPS)
    return centre * inv, inv


def normalise_back(dn, hat, inv, gain):
    d_hat = dn * gain
    mean, along = lane_means([d_hat, d_hat * hat])
    return inv * (d_hat - mean - hat * along)


def head_mask():
    rows = lax.broadcasted_iota(jnp.int32, (HEADS * LEN, CH), 0) // LEN
    lanes = lax.broadcasted_iota(jnp.int32, (HEADS * LEN, CH), 1) // (CH // HEADS)
    return (rows == lanes).astype(F32).astype(BF16)


def spread_heads(v, mask):
    return jnp.concatenate([v] * HEADS, axis=0) * mask


def gather_heads(v):
    lane = lax.broadcasted_iota(jnp.int32, (LEN, CH), 1)
    size = CH // HEADS
    out = v[3 * LEN :]
    for h in (2, 1, 0):
        out = jnp.where(lane < (h + 1) * size, v[h * LEN : (h + 1) * LEN], out)
    return out


def rows_of(values, w):
    return values[w * LEN : (w + 1) * LEN]


def groups_of(tokens, group):
    count = tokens // LEN
    return [range(start, min(start + group, count)) for start in range(0, count, group)]


def in_stages(stages, groups):
    state = [None] * len(groups)
    for step in range(len(groups) + len(stages) - 1):
        for s in reversed(range(len(stages))):
            g = step - s
            if 0 <= g < len(groups):
                state[g] = stages[s](groups[g], state[g])
    return state


def attention(qkv, bias_t, mask, group):
    def scores(windows, _):
        parts = [rows_of(qkv, w) for w in windows]
        return parts, [nt(x[:, CH : 2 * CH], spread_heads(x[:, :CH], mask)) * SCALE + bias_t for x in parts]

    def softmax(_, state):
        parts, values = state
        e = [jnp.exp(x - jnp.max(x, axis=0, keepdims=True)) for x in values]
        return parts, [(x * (1.0 / jnp.sum(x, axis=0, keepdims=True))).astype(BF16) for x in e]

    def mix(_, state):
        parts, p = state
        o = [tn(x, y[:, 2 * CH :]) for x, y in zip(p, parts)]
        return [gather_heads(x).astype(BF16) for x in o], p

    done = in_stages((scores, softmax, mix), groups_of(qkv.shape[0], group))
    return jnp.concatenate(sum((x for x, _ in done), []), axis=0), jnp.concatenate(sum((x for _, x in done), []), axis=0)


def attention_back(d_o, qkv, p, mask, group):
    def spread(windows, _):
        parts = [rows_of(qkv, w) for w in windows]
        weights = [rows_of(p, w) for w in windows]
        do_spread = [spread_heads(rows_of(d_o, w), mask) for w in windows]
        dp = [nt(x[:, 2 * CH :], y) for x, y in zip(parts, do_spread)]
        return parts, weights, dp, [nn(x, y) for x, y in zip(weights, do_spread)]

    def softmax(_, state):
        parts, weights, dp, dv = state
        weights = [x.astype(F32) for x in weights]
        return parts, [x * (y - jnp.sum(y * x, axis=0, keepdims=True)) for x, y in zip(weights, dp)], dv

    def mix(_, state):
        parts, ds, dv = state
        dsb = [x.astype(BF16) for x in ds]
        dk = [nn(x, spread_heads(y[:, :CH], mask)) * SCALE for x, y in zip(dsb, parts)]
        dq = [gather_heads(tn(x, y[:, CH : 2 * CH])) * SCALE for x, y in zip(dsb, parts)]
        return [jnp.concatenate(x, axis=1).astype(BF16) for x in zip(dq, dk, dv)], sum(ds[1:], ds[0])

    done = in_stages((spread, softmax, mix), groups_of(qkv.shape[0], group))
    bias = sum((x for _, x in done[1:]), done[0][1])
    return jnp.concatenate(sum((x for x, _ in done), []), axis=0), bias


def gelu_and_slope(u):
    c = 0.7978845608028654
    sq = u * u
    s = 0.5 * jnp.tanh(u * (c + (c * 0.044715) * sq)) + 0.5
    m = u * s
    return m, s + m * (1.0 - s) * (2.0 * c + (6.0 * c * 0.044715) * sq)


def forward(x, w_qkv, w_proj, gains, bias, mask, group):
    hat1, inv1 = normalise(x)
    gain = gains()
    a1 = (hat1 * gain[0:1]).astype(BF16)
    qkv = nn(a1, w_qkv()).astype(BF16)
    o, p = attention(qkv, turned_bias(bias()), mask, group)
    h = (x + nn(o, w_proj())).astype(BF16).astype(F32)
    hat2, inv2 = normalise(h)
    a2 = (hat2 * gain[1:2]).astype(BF16)
    return h, (hat1, inv1, a1, p, o, hat2, inv2, a2), qkv


def backward(gy, kept, w_qkv, w_proj, w_up, w_down, g1, g2, mask, group):
    hat1, inv1, a1, p, o, hat2, inv2, a2, qkv = kept
    m, slope = gelu_and_slope(nn(a2, w_up))
    m = m.astype(BF16)
    du = (nt(gy, w_down) * slope).astype(BF16)
    da2 = nt(du, w_up)
    down, up = tn(gy, m), tn(a2, du)
    gain2 = jnp.sum(da2 * hat2, axis=0, keepdims=True)
    dh = gy.astype(F32) + normalise_back(da2, hat2, inv2, g2)
    dhb = dh.astype(BF16)
    d_o = nt(dhb, w_proj).astype(BF16)
    proj = tn(o, dhb)
    dqkv, bias = attention_back(d_o, qkv, p, mask, group)
    da1 = nt(dqkv, w_qkv)
    grads = (tn(a1, dqkv), proj, up, down)
    gain1 = jnp.sum(da1 * hat1, axis=0, keepdims=True)
    dx = dh + normalise_back(da1, hat1, inv1, g1)
    return dx, grads, bias, gain1, gain2


def pack(pack_ref, grads, bias, gain1, gain2, old=None):
    qkv, proj, up, down = grads

    def put(at, value):
        rows = slice(at, at + value.shape[0])
        pack_ref[rows] = value if old is None else value + old[rows].astype(F32)

    for j in range(3):
        put(ROW_QKV + CH * j, qkv[:, CH * j : CH * (j + 1)])
    put(ROW_PROJ, proj)
    for j in range(4):
        put(ROW_UP + CH * j, up[:, CH * j : CH * (j + 1)])
        put(ROW_DOWN + CH * j, down[:, CH * j : CH * (j + 1)].T)
    put(ROW_BIAS, bias[:, :CH])
    put(ROW_BIAS + LEN, bias[:, CH:])
    put(ROW_GAIN, jnp.concatenate([gain1, gain2, jnp.zeros((ROWS - ROW_GAIN - 2, CH), F32)], axis=0))


def to_windows(tile):
    rows, cols, ch = tile.shape
    return tile.reshape(WIN, cols // WIN, WIN, ch).transpose(1, 0, 2, 3).reshape(-1, ch)


def from_windows(tokens):
    count = tokens.shape[0] // LEN
    return tokens.reshape(count, WIN, WIN, CH).transpose(1, 0, 2, 3).reshape(WIN, count * WIN, CH)


def turned_bias(bias):
    return jnp.concatenate([bias[h].T for h in range(HEADS)], axis=1)


def first_half(x, group, w_qkv, w_proj, w_up, w_down, gains, bias):
    h, kept, _ = forward(to_windows(x.astype(F32)), w_qkv, w_proj, gains, bias, head_mask(), group)
    m, _ = gelu_and_slope(nn(kept[7], w_up()))
    return from_windows(h + nn(m.astype(BF16), w_down()))


def first_kernel(*refs):
    sources, (top_ref, low_ref, edge_ref), refs = refs[:8], refs[8:11], refs[11:]
    targets, sem = refs[:8], refs[8]
    wide = sources[0].shape[1] // 2
    moves = [(sources[0].at[:, 0:wide], targets[0])]
    moves += [(source.at[0], target) for source, target in zip(sources[1:7], targets[1:7])]
    moves += [(sources[7].at[HALF:, 0:WIN], targets[7])]
    copies = [pltpu.make_async_copy(source, target, sem.at[i]) for i, (source, target) in enumerate(moves)]
    for i in (0, 5, 1, 6, 2, 3, 4, 7):
        copies[i].start(priority=1)

    def fetched(i):
        copies[i].wait()
        return targets[i][...]

    parts = [functools.partial(fetched, i) for i in range(1, 7)]
    tile = first_half(fetched(0), 8, *parts)
    top_ref[...] = tile[:HALF].astype(BF16)
    low_ref[...] = tile[HALF:].astype(BF16)
    edge_ref[0:HALF] = tile[HALF:, 0:WIN].astype(BF16)
    edge_ref[HALF:] = fetched(7)


def at(ref, i):
    return lambda: ref[i]


def next_kernel(x_ref, w_qkv_ref, w_proj_ref, w_up_ref, w_down_ref, gain_ref, bias_ref, top_ref, low_ref):
    wide = x_ref.shape[1] // 2
    parts = [at(ref, 0) for ref in (w_qkv_ref, w_proj_ref, w_up_ref, w_down_ref, gain_ref, bias_ref)]
    tile = first_half(x_ref[:, wide:], 8, *parts)
    top_ref[...] = tile[:HALF].astype(BF16)
    low_ref[...] = tile[HALF:].astype(BF16)


KEPT = (CH, CH, CH, HEADS * LEN, CH, CH, CH, CH, 3 * CH)


def kept_slices():
    starts = [sum(KEPT[:i]) for i in range(len(KEPT))]
    return [slice(start, start + width) for start, width in zip(starts, KEPT)]


def keep_kernel(part, x_ref, w_qkv_ref, w_proj_ref, gain_ref, bias_ref, kept_ref):
    wide = x_ref.shape[1] // 2
    x = to_windows(x_ref[:, part * wide : (part + 1) * wide].astype(F32))
    _, kept, qkv = forward(x, at(w_qkv_ref, 0), at(w_proj_ref, 0), at(gain_ref, 0), at(bias_ref, 0), head_mask(), 8)
    kept += (qkv,)
    for place, value, width in zip(kept_slices(), kept, KEPT):
        kept_ref[:, place] = jnp.broadcast_to(value, (x.shape[0], width)).astype(BF16)


def second_half(x, gy, group, w_qkv_ref, w_proj_ref, w_up_ref, w_down_ref, gain_ref, bias_ref):
    mask = head_mask()
    _, kept, qkv = forward(
        to_windows(x), at(w_qkv_ref, 1), at(w_proj_ref, 1), at(gain_ref, 1), at(bias_ref, 1), mask, group
    )
    w_qkv, w_proj, w_up, w_down = w_qkv_ref[1], w_proj_ref[1], w_up_ref[1], w_down_ref[1]
    g1, g2 = gain_ref[1, 0:1], gain_ref[1, 1:2]
    return backward(to_windows(gy).astype(BF16), (*kept, qkv), w_qkv, w_proj, w_up, w_down, g1, g2, mask, group)


def second_kernel(*refs):
    low_ref, below_ref, g_own_ref, g_below_ref = refs[:4]
    weights, (dx_ref, pack_ref, frame_ref) = refs[4:10], refs[10:]
    wide = low_ref.shape[1]
    frame_ref[0:HALF, 0:wide] = low_ref[...].astype(F32)
    frame_ref[HALF:, 0:wide] = below_ref[...].astype(F32)
    x = frame_ref[:, HALF : wide - HALF]
    frame_ref[0:HALF, 0:wide] = g_own_ref[HALF:, 0:wide].astype(F32)
    frame_ref[HALF:, 0:wide] = g_below_ref[0:HALF, 0:wide].astype(F32)
    gy = frame_ref[:, HALF : wide - HALF]
    dx, *sums = second_half(x, gy, 7, *weights)
    dx_ref[...] = dx.astype(BF16)
    pack(pack_ref, *sums)


def third_kernel(*refs):
    low_a_ref, low_b_ref, below_a_ref, below_b_ref, g_own_ref, g_below_ref, edge_ref = refs[:7]
    weights, (dx_ref, old_ref, dtop_ref, dlow_ref, dedge_ref, dcorner_ref, pack_ref, frame_ref) = refs[7:13], refs[13:]
    wide, cols = low_a_ref.shape[1], g_own_ref.shape[1]
    span = cols - wide + WIN
    frame_ref[0:HALF, 0:WIN] = low_a_ref[:, wide - WIN :].astype(F32)
    frame_ref[HALF:, 0:WIN] = below_a_ref[:, wide - WIN :].astype(F32)
    frame_ref[0:HALF, WIN:span] = low_b_ref[...].astype(F32)
    frame_ref[HALF:, WIN:span] = below_b_ref[...].astype(F32)
    frame_ref[0:HALF, span : span + WIN] = edge_ref[0:HALF].astype(F32)
    frame_ref[HALF:, span : span + WIN] = edge_ref[WIN : WIN + HALF].astype(F32)
    x = frame_ref[:, HALF : span + HALF]
    frame_ref[0:HALF, 0:span] = g_own_ref[HALF:, wide - WIN :].astype(F32)
    frame_ref[HALF:, 0:span] = g_below_ref[0:HALF, wide - WIN :].astype(F32)
    frame_ref[0:HALF, span : span + WIN] = edge_ref[HALF:WIN].astype(F32)
    frame_ref[HALF:, span : span + WIN] = edge_ref[WIN + HALF :].astype(F32)
    gy = frame_ref[:, HALF : span + HALF]
    dx, *sums = second_half(x, gy, 9, *weights)
    pack(pack_ref, *sums, old_ref)
    tile = from_windows(jnp.concatenate([dx_ref[...].astype(F32), dx], axis=0))
    dtop_ref[...] = tile[:HALF].astype(BF16)
    dlow_ref[...] = tile[HALF:].astype(BF16)
    dedge_ref[...] = tile[:HALF, cols - WIN :].astype(BF16)
    dcorner_ref[...] = tile[HALF:, cols - WIN :].astype(BF16)


def last_kernel(*refs):
    (own, above, left, corner), kept_refs, refs = refs[:4], refs[4:6], refs[6:]
    w_qkv_ref, w_proj_ref, w_up_ref, w_down_ref, gain_ref, other_ref, core_ref = refs[:7]
    dx_ref, keep_ref, send_ref, frame_ref, pack_ref = refs[7:]
    cols = own.shape[1]
    frame_ref[HALF:, 0:WIN] = left[...].astype(F32)
    frame_ref[0:HALF, 0:WIN] = corner[...].astype(F32)
    first = frame_ref[:, HALF:WIN]
    frame_ref[:, 0:HALF] = first
    frame_ref[HALF:, HALF : HALF + cols] = own[...].astype(F32)
    frame_ref[0:HALF, HALF : HALF + cols] = above[...].astype(F32)
    gy = to_windows(frame_ref[:, 0:cols]).astype(BF16)
    kept = [jnp.concatenate([ref[:, place] for ref in kept_refs], axis=0) for place in kept_slices()]
    kept = [v.astype(F32) if i in (0, 1, 5, 6) else v for i, v in enumerate(kept)]
    g1, g2 = gain_ref[0, 0:1], gain_ref[0, 1:2]
    dx, grads, bias, gain1, gain2 = backward(
        gy, kept, w_qkv_ref[0], w_proj_ref[0], w_up_ref[0], w_down_ref[0], g1, g2, head_mask(), 16
    )
    dx_ref[...] = from_windows(dx).astype(BF16)
    pack(pack_ref, grads, bias, gain1, gain2)
    first_core = core_ref[0] == 0

    @pl.when(first_core)
    def _():
        keep_ref[...] = pack_ref[...]
        send_ref[...] = other_ref[...].astype(BF16)

    @pl.when(jnp.logical_not(first_core))
    def _():
        keep_ref[...] = other_ref[...]
        send_ref[...] = pack_ref[...].astype(BF16)


def unpack_kernel(core_ref, own_ref, other_ref, *refs):
    qkv_ref, proj_ref, up_ref, down_ref, gain_ref, bias_ref, whole_ref = refs
    at = pl.multiple_of(core_ref[0] * ROWS, ROWS)
    whole_ref[pl.ds(at, ROWS)] = own_ref[...].astype(F32)
    whole_ref[pl.ds(ROWS - at, ROWS)] = other_ref[...].astype(F32)
    for b in range(2):
        at = b * ROWS
        for j in range(3):
            qkv_ref[b, :, CH * j : CH * (j + 1)] = whole_ref[at + ROW_QKV + CH * j : at + ROW_QKV + CH * (j + 1)]
        proj_ref[b] = whole_ref[at + ROW_PROJ : at + ROW_PROJ + CH]
        for j in range(4):
            up_ref[b, :, CH * j : CH * (j + 1)] = whole_ref[at + ROW_UP + CH * j : at + ROW_UP + CH * (j + 1)]
        down_ref[b] = whole_ref[at + ROW_DOWN : at + ROW_DOWN + FFN]
        for j in range(2):
            turned = whole_ref[at + ROW_BIAS + LEN * j : at + ROW_BIAS + LEN * (j + 1)].T
            bias_ref[b, 2 * j] = turned[:LEN]
            bias_ref[b, 2 * j + 1] = turned[LEN:]
        gain_ref[b] = whole_ref[at + ROW_GAIN : at + ROW_GAIN + 2]


def vmem(count):
    return [pl.BlockSpec(memory_space=pltpu.VMEM)] * count


def cost(flops, moved):
    return pl.CostEstimate(flops=flops, bytes_accessed=moved, transcendentals=0)


def shift(value, down, right):
    tall, wide = 32, 8
    pairs = []
    for r in range(tall):
        for c in range(wide):
            pairs.append((r * wide + c, (r + down) % tall * wide + (c + right) % wide))
    return lax.ppermute(value, AXES, pairs)


def swap_core(value):
    return lax.ppermute(value, "core", [(0, 1), (1, 0)])


def scatter_sum(value, axis, count):
    pieces = value.astype(BF16).reshape(count, value.shape[0] // count, CH)
    return jnp.sum(lax.all_to_all(pieces, axis, 0, 0).astype(F32), axis=0)


def collect(value, axis, count):
    spread = jnp.broadcast_to(value[None], (count, *value.shape))
    return lax.all_to_all(spread, axis, 0, 0)


def sum_over_devices(keep, send):
    total = keep + swap_core(send).astype(F32)
    total = scatter_sum(total, PLANE, 16)
    total = jnp.sum(collect(total.astype(BF16), "z", 8).astype(F32), axis=0).astype(BF16)
    total = collect(total, PLANE, 16).reshape(ROWS, CH)
    return total, swap_core(total)


def body(latent, cotangent, w_qkv, w_proj, w_up, w_down, gains, attn_bias):
    cols = latent.shape[1]
    half = jax.ShapeDtypeStruct((HALF, cols, CH), BF16)
    params = pltpu.CompilerParams(vmem_limit_bytes=VMEM_LIMIT)
    packed = jax.ShapeDtypeStruct((ROWS, CH), F32)
    core = lax.axis_index("core").reshape(1)
    weights = (w_qkv, w_proj, w_up, w_down, gains)
    g_below = shift(cotangent, -1, 0)
    tokens = WIN * cols

    wide = cols // 2
    part_a = WIN * (wide - WIN)
    small = jax.ShapeDtypeStruct((HALF, WIN, CH), BF16)
    side = jax.ShapeDtypeStruct((HALF, wide, CH), BF16)
    corner = jax.ShapeDtypeStruct((WIN, WIN, CH), BF16)
    top_a, low_a, edge_own = pl.pallas_call(
        first_kernel,
        out_shape=(side, side, corner),
        in_specs=[pl.BlockSpec(memory_space=pltpu.HBM)] * 8,
        out_specs=vmem(3),
        scratch_shapes=[pltpu.VMEM((WIN, wide, CH), BF16)]
        + [pltpu.VMEM(w.shape[1:], w.dtype) for w in (*weights, attn_bias)]
        + [pltpu.VMEM((HALF, WIN, CH), BF16), pltpu.SemaphoreType.DMA((8,))],
        compiler_params=pltpu.CompilerParams(vmem_limit_bytes=FIRST_LIMIT),
        cost_estimate=cost(300_000_000, 1_500_000),
        name="forward_first",
    )(latent, *weights, attn_bias, cotangent)
    below_a = shift(top_a, -1, 0)
    top_b, low_b = pl.pallas_call(
        next_kernel,
        out_shape=(side, side),
        in_specs=vmem(7),
        out_specs=vmem(2),
        compiler_params=params,
        cost_estimate=cost(300_000_000, 1_500_000),
        name="forward_next",
    )(latent, *weights, attn_bias)
    below_b = shift(top_b, -1, 0)
    edge = shift(jnp.concatenate([edge_own, below_a[:, :WIN], g_below[:HALF, :WIN]], axis=0), 0, -1)
    weights = (*weights, attn_bias)
    frame = pltpu.VMEM((WIN, cols + 2 * WIN, CH), F32)
    dx_a, pack_a = pl.pallas_call(
        second_kernel,
        out_shape=(jax.ShapeDtypeStruct((part_a, CH), BF16), packed),
        in_specs=vmem(10),
        out_specs=vmem(2),
        scratch_shapes=[frame],
        compiler_params=params,
        cost_estimate=cost(700_000_000, 3_000_000),
        name="backward_second",
    )(low_a, below_a, cotangent, g_below, *weights)
    edge, below_b, dx_a = lax.optimization_barrier((edge, below_b, dx_a))
    d_top, d_low, d_edge, d_corner, pack_two = pl.pallas_call(
        third_kernel,
        out_shape=(half, half, small, small, packed),
        in_specs=vmem(15),
        out_specs=vmem(5),
        scratch_shapes=[frame],
        compiler_params=params,
        cost_estimate=cost(800_000_000, 3_000_000),
        name="backward_third",
    )(low_a, low_b, below_a, below_b, cotangent, g_below, edge, *weights, dx_a, pack_a)
    d_above, d_left, d_corner = shift(d_low, 1, 0), shift(d_edge, 0, 1), shift(d_corner, 1, 1)
    kept = []
    for part in range(2):
        made = pl.pallas_call(
            functools.partial(keep_kernel, part),
            out_shape=jax.ShapeDtypeStruct((WIN * wide, sum(KEPT)), BF16),
            in_specs=vmem(5),
            out_specs=vmem(1)[0],
            compiler_params=params,
            cost_estimate=cost(300_000_000, 2_000_000),
            name="keep_first",
        )(latent, w_qkv, w_proj, gains, attn_bias)
        kept.append(made)
    dx, keep, send = pl.pallas_call(
        last_kernel,
        out_shape=(
            jax.ShapeDtypeStruct(latent.shape, BF16),
            packed,
            jax.ShapeDtypeStruct((ROWS, CH), BF16),
        ),
        in_specs=vmem(12) + [pl.BlockSpec(memory_space=pltpu.SMEM)],
        out_specs=vmem(3),
        scratch_shapes=[frame, pltpu.VMEM((ROWS, CH), F32)],
        compiler_params=params,
        cost_estimate=cost(1_500_000_000, 4_000_000),
        name="backward_first",
    )(d_top, d_above, d_left, d_corner, *kept, *weights[:5], pack_two, core)
    parts = sum_over_devices(keep, send)
    qkv, proj, up, down, gain, bias = pl.pallas_call(
        unpack_kernel,
        out_shape=(
            jax.ShapeDtypeStruct((2, CH, 3 * CH), F32),
            jax.ShapeDtypeStruct((2, CH, CH), F32),
            jax.ShapeDtypeStruct((2, CH, FFN), F32),
            jax.ShapeDtypeStruct((2, FFN, CH), F32),
            jax.ShapeDtypeStruct((2, 2, CH), F32),
            jax.ShapeDtypeStruct((2, HEADS, LEN, LEN), F32),
        ),
        in_specs=[pl.BlockSpec(memory_space=pltpu.SMEM)] + vmem(2),
        out_specs=vmem(6),
        scratch_shapes=[pltpu.VMEM((2 * ROWS, CH), F32)],
        compiler_params=params,
        cost_estimate=cost(1_000_000, 4_000_000),
        name="unpack",
    )(core, *parts)
    return dx, qkv, proj, up, down, gain, bias


def solution(mesh):
    fine = jax.sharding.Mesh(mesh.devices.reshape(8, 2, 2, 4, 2), AXES)
    tiles = P(("z", "yh", "core"), ("x", "yl"), None)
    in_specs = (tiles, tiles, P(), P(), P(), P(), P(), P())
    out_specs = (tiles, P(), P(), P(), P(), P(), P())
    return jax.shard_map(body, mesh=fine, in_specs=in_specs, out_specs=out_specs, check_vma=False)
```

```python
import functools

import jax
import jax.numpy as jnp
from jax import lax
from jax.experimental import pallas as pl
from jax.experimental.pallas import tpu as pltpu
from jax.sharding import PartitionSpec as P

WIN = 8
HALF = 4
LEN = 64
CH = 128
HEADS = 4
FFN = 512
EPS = 1e-05
SCALE = (CH // HEADS) ** -0.5
F32 = jnp.float32
BF16 = jnp.bfloat16
VMEM_LIMIT = 16 * 1024 * 1024
FIRST_LIMIT = 57 * 1000 * 1000

ROW_QKV, ROW_PROJ, ROW_UP, ROW_DOWN, ROW_BIAS, ROW_GAIN, ROWS = 0, 384, 512, 1024, 1536, 1664, 1792
AXES = ("z", "yh", "core", "x", "yl")
PLANE = ("yh", "x", "yl")


def nn(a, b):
    return lax.dot_general(a, b, (((1,), (0,)), ((), ())), preferred_element_type=F32)


def nt(a, b):
    return lax.dot_general(a, b, (((1,), (1,)), ((), ())), preferred_element_type=F32)


def tn(a, b):
    return lax.dot_general(a, b, (((0,), (0,)), ((), ())), preferred_element_type=F32)


def lane_means(parts):
    width = len(parts) * CH
    block = lax.broadcasted_iota(jnp.int32, (width, width), 0) // CH == lax.broadcasted_iota(jnp.int32, (width, width), 1) // CH
    ones = (block.astype(F32) * (1.0 / CH)).astype(BF16)
    sums = nn(jnp.concatenate([p.astype(BF16) for p in parts], axis=1), ones)
    return [sums[:, CH * i : CH * (i + 1)] for i in range(len(parts))]


def normalise(v):
    centre = v - jnp.mean(v, axis=-1, keepdims=True)
    spread = jnp.mean(centre * centre, axis=-1, keepdims=True)
    inv = lax.rsqrt(spread + EPS)
    return centre * inv, inv


def normalise_back(dn, hat, inv, gain):
    d_hat = dn * gain
    mean, along = lane_means([d_hat, d_hat * hat])
    return inv * (d_hat - mean - hat * along)


def head_mask():
    rows = lax.broadcasted_iota(jnp.int32, (HEADS * LEN, CH), 0) // LEN
    lanes = lax.broadcasted_iota(jnp.int32, (HEADS * LEN, CH), 1) // (CH // HEADS)
    return (rows == lanes).astype(F32).astype(BF16)


def spread_heads(v, mask):
    return jnp.concatenate([v] * HEADS, axis=0) * mask


def gather_heads(v):
    lane = lax.broadcasted_iota(jnp.int32, (LEN, CH), 1)
    size = CH // HEADS
    out = v[3 * LEN :]
    for h in (2, 1, 0):
        out = jnp.where(lane < (h + 1) * size, v[h * LEN : (h + 1) * LEN], out)
    return out


def rows_of(values, w):
    return values[w * LEN : (w + 1) * LEN]


def groups_of(tokens, group):
    count = tokens // LEN
    return [range(start, min(start + group, count)) for start in range(0, count, group)]


def in_stages(stages, groups):
    state = [None] * len(groups)
    for step in range(len(groups) + len(stages) - 1):
        for s in reversed(range(len(stages))):
            g = step - s
            if 0 <= g < len(groups):
                state[g] = stages[s](groups[g], state[g])
    return state


def attention(qkv, bias_t, mask, group):
    def scores(windows, _):
        parts = [rows_of(qkv, w) for w in windows]
        return parts, [nt(x[:, CH : 2 * CH], spread_heads(x[:, :CH], mask)) * SCALE + bias_t for x in parts]

    def softmax(_, state):
        parts, values = state
        e = [jnp.exp(x - jnp.max(x, axis=0, keepdims=True)) for x in values]
        return parts, [(x * (1.0 / jnp.sum(x, axis=0, keepdims=True))).astype(BF16) for x in e]

    def mix(_, state):
        parts, p = state
        o = [tn(x, y[:, 2 * CH :]) for x, y in zip(p, parts)]
        return [gather_heads(x).astype(BF16) for x in o], p

    done = in_stages((scores, softmax, mix), groups_of(qkv.shape[0], group))
    return jnp.concatenate(sum((x for x, _ in done), []), axis=0), jnp.concatenate(sum((x for _, x in done), []), axis=0)


def attention_back(d_o, qkv, p, mask, group):
    def spread(windows, _):
        parts = [rows_of(qkv, w) for w in windows]
        weights = [rows_of(p, w) for w in windows]
        do_spread = [spread_heads(rows_of(d_o, w), mask) for w in windows]
        dp = [nt(x[:, 2 * CH :], y) for x, y in zip(parts, do_spread)]
        return parts, weights, dp, [nn(x, y) for x, y in zip(weights, do_spread)]

    def softmax(_, state):
        parts, weights, dp, dv = state
        weights = [x.astype(F32) for x in weights]
        return parts, [x * (y - jnp.sum(y * x, axis=0, keepdims=True)) for x, y in zip(weights, dp)], dv

    def mix(_, state):
        parts, ds, dv = state
        dsb = [x.astype(BF16) for x in ds]
        dk = [nn(x, spread_heads(y[:, :CH], mask)) * SCALE for x, y in zip(dsb, parts)]
        dq = [gather_heads(tn(x, y[:, CH : 2 * CH])) * SCALE for x, y in zip(dsb, parts)]
        return [jnp.concatenate(x, axis=1).astype(BF16) for x in zip(dq, dk, dv)], sum(ds[1:], ds[0])

    done = in_stages((spread, softmax, mix), groups_of(qkv.shape[0], group))
    bias = sum((x for _, x in done[1:]), done[0][1])
    return jnp.concatenate(sum((x for x, _ in done), []), axis=0), bias


def gelu_and_slope(u):
    c = 0.7978845608028654
    sq = u * u
    s = 0.5 * jnp.tanh(u * (c + (c * 0.044715) * sq)) + 0.5
    m = u * s
    return m, s + m * (1.0 - s) * (2.0 * c + (6.0 * c * 0.044715) * sq)


def forward(x, w_qkv, w_proj, gains, bias, mask, group):
    hat1, inv1 = normalise(x)
    gain = gains()
    a1 = (hat1 * gain[0:1]).astype(BF16)
    qkv = nn(a1, w_qkv()).astype(BF16)
    o, p = attention(qkv, turned_bias(bias()), mask, group)
    h = (x + nn(o, w_proj())).astype(BF16).astype(F32)
    hat2, inv2 = normalise(h)
    a2 = (hat2 * gain[1:2]).astype(BF16)
    return h, (hat1, inv1, a1, p, o, hat2, inv2, a2), qkv


def backward(gy, kept, qkv, w_qkv, w_proj, w_up, w_down, g1, g2, mask, group):
    hat1, inv1, a1, p, o, hat2, inv2, a2 = kept
    m, slope = gelu_and_slope(nn(a2, w_up))
    m = m.astype(BF16)
    du = (nt(gy, w_down) * slope).astype(BF16)
    da2 = nt(du, w_up)
    down, up = tn(gy, m), tn(a2, du)
    gain2 = jnp.sum(da2 * hat2, axis=0, keepdims=True)
    dh = gy.astype(F32) + normalise_back(da2, hat2, inv2, g2)
    dhb = dh.astype(BF16)
    d_o = nt(dhb, w_proj).astype(BF16)
    proj = tn(o, dhb)
    dqkv, bias = attention_back(d_o, qkv, p, mask, group)
    da1 = nt(dqkv, w_qkv)
    grads = (tn(a1, dqkv), proj, up, down)
    gain1 = jnp.sum(da1 * hat1, axis=0, keepdims=True)
    dx = dh + normalise_back(da1, hat1, inv1, g1)
    return dx, grads, bias, gain1, gain2


def pack(pack_ref, grads, bias, gain1, gain2, old=None):
    qkv, proj, up, down = grads

    def put(at, value):
        rows = slice(at, at + value.shape[0])
        pack_ref[rows] = value if old is None else value + old[rows].astype(F32)

    for j in range(3):
        put(ROW_QKV + CH * j, qkv[:, CH * j : CH * (j + 1)])
    put(ROW_PROJ, proj)
    for j in range(4):
        put(ROW_UP + CH * j, up[:, CH * j : CH * (j + 1)])
        put(ROW_DOWN + CH * j, down[:, CH * j : CH * (j + 1)].T)
    put(ROW_BIAS, bias[:, :CH])
    put(ROW_BIAS + LEN, bias[:, CH:])
    put(ROW_GAIN, jnp.concatenate([gain1, gain2, jnp.zeros((ROWS - ROW_GAIN - 2, CH), F32)], axis=0))


def to_windows(tile):
    rows, cols, ch = tile.shape
    return tile.reshape(WIN, cols // WIN, WIN, ch).transpose(1, 0, 2, 3).reshape(-1, ch)


def from_windows(tokens):
    count = tokens.shape[0] // LEN
    return tokens.reshape(count, WIN, WIN, CH).transpose(1, 0, 2, 3).reshape(WIN, count * WIN, CH)


def turned_bias(bias):
    return jnp.concatenate([bias[h].T for h in range(HEADS)], axis=1)


def first_half(x, group, w_qkv, w_proj, w_up, w_down, gains, bias):
    h, kept, _ = forward(to_windows(x.astype(F32)), w_qkv, w_proj, gains, bias, head_mask(), group)
    m, _ = gelu_and_slope(nn(kept[7], w_up()))
    return from_windows(h + nn(m.astype(BF16), w_down()))


def first_kernel(*refs):
    sources, (top_ref, low_ref, edge_ref), refs = refs[:8], refs[8:11], refs[11:]
    targets, sem = refs[:8], refs[8]
    wide = sources[0].shape[1] // 2
    moves = [(sources[0].at[:, 0:wide], targets[0])]
    moves += [(source.at[0], target) for source, target in zip(sources[1:7], targets[1:7])]
    moves += [(sources[7].at[HALF:, 0:WIN], targets[7])]
    copies = [pltpu.make_async_copy(source, target, sem.at[i]) for i, (source, target) in enumerate(moves)]
    for i in (0, 5, 1, 6, 2, 3, 4, 7):
        copies[i].start(priority=1)

    def fetched(i):
        copies[i].wait()
        return targets[i][...]

    parts = [functools.partial(fetched, i) for i in range(1, 7)]
    tile = first_half(fetched(0), 8, *parts)
    top_ref[...] = tile[:HALF].astype(BF16)
    low_ref[...] = tile[HALF:].astype(BF16)
    edge_ref[0:HALF] = tile[HALF:, 0:WIN].astype(BF16)
    edge_ref[HALF:] = fetched(7)


def at(ref, i):
    return lambda: ref[i]


def next_kernel(x_ref, w_qkv_ref, w_proj_ref, w_up_ref, w_down_ref, gain_ref, bias_ref, top_ref, low_ref):
    wide = x_ref.shape[1] // 2
    parts = [at(ref, 0) for ref in (w_qkv_ref, w_proj_ref, w_up_ref, w_down_ref, gain_ref, bias_ref)]
    tile = first_half(x_ref[:, wide:], 8, *parts)
    top_ref[...] = tile[:HALF].astype(BF16)
    low_ref[...] = tile[HALF:].astype(BF16)


KEPT = (CH, CH, CH, HEADS * LEN, CH, CH, CH, CH)


def kept_slices():
    starts = [sum(KEPT[:i]) for i in range(len(KEPT))]
    return [slice(start, start + width) for start, width in zip(starts, KEPT)]


def keep_kernel(part, x_ref, w_qkv_ref, w_proj_ref, gain_ref, bias_ref, kept_ref):
    wide = x_ref.shape[1] // 2
    x = to_windows(x_ref[:, part * wide : (part + 1) * wide].astype(F32))
    _, kept, _ = forward(x, at(w_qkv_ref, 0), at(w_proj_ref, 0), at(gain_ref, 0), at(bias_ref, 0), head_mask(), 8)
    for place, value, width in zip(kept_slices(), kept, KEPT):
        kept_ref[:, place] = jnp.broadcast_to(value, (x.shape[0], width)).astype(BF16)


def second_half(x, gy, group, w_qkv_ref, w_proj_ref, w_up_ref, w_down_ref, gain_ref, bias_ref):
    mask = head_mask()
    _, kept, qkv = forward(
        to_windows(x), at(w_qkv_ref, 1), at(w_proj_ref, 1), at(gain_ref, 1), at(bias_ref, 1), mask, group
    )
    w_qkv, w_proj, w_up, w_down = w_qkv_ref[1], w_proj_ref[1], w_up_ref[1], w_down_ref[1]
    g1, g2 = gain_ref[1, 0:1], gain_ref[1, 1:2]
    return backward(to_windows(gy).astype(BF16), kept, qkv, w_qkv, w_proj, w_up, w_down, g1, g2, mask, group)


def second_kernel(*refs):
    low_ref, below_ref, g_own_ref, g_below_ref = refs[:4]
    weights, (dx_ref, pack_ref, frame_ref) = refs[4:10], refs[10:]
    wide = low_ref.shape[1]
    frame_ref[0:HALF, 0:wide] = low_ref[...].astype(F32)
    frame_ref[HALF:, 0:wide] = below_ref[...].astype(F32)
    x = frame_ref[:, HALF : wide - HALF]
    frame_ref[0:HALF, 0:wide] = g_own_ref[HALF:, 0:wide].astype(F32)
    frame_ref[HALF:, 0:wide] = g_below_ref[0:HALF, 0:wide].astype(F32)
    gy = frame_ref[:, HALF : wide - HALF]
    dx, *sums = second_half(x, gy, 7, *weights)
    dx_ref[...] = dx.astype(BF16)
    pack(pack_ref, *sums)


def third_kernel(*refs):
    low_a_ref, low_b_ref, below_a_ref, below_b_ref, g_own_ref, g_below_ref, edge_ref = refs[:7]
    weights, (dx_ref, old_ref, dtop_ref, dlow_ref, dedge_ref, dcorner_ref, pack_ref, frame_ref) = refs[7:13], refs[13:]
    wide, cols = low_a_ref.shape[1], g_own_ref.shape[1]
    span = cols - wide + WIN
    frame_ref[0:HALF, 0:WIN] = low_a_ref[:, wide - WIN :].astype(F32)
    frame_ref[HALF:, 0:WIN] = below_a_ref[:, wide - WIN :].astype(F32)
    frame_ref[0:HALF, WIN:span] = low_b_ref[...].astype(F32)
    frame_ref[HALF:, WIN:span] = below_b_ref[...].astype(F32)
    frame_ref[0:HALF, span : span + WIN] = edge_ref[0:HALF].astype(F32)
    frame_ref[HALF:, span : span + WIN] = edge_ref[WIN : WIN + HALF].astype(F32)
    x = frame_ref[:, HALF : span + HALF]
    frame_ref[0:HALF, 0:span] = g_own_ref[HALF:, wide - WIN :].astype(F32)
    frame_ref[HALF:, 0:span] = g_below_ref[0:HALF, wide - WIN :].astype(F32)
    frame_ref[0:HALF, span : span + WIN] = edge_ref[HALF:WIN].astype(F32)
    frame_ref[HALF:, span : span + WIN] = edge_ref[WIN + HALF :].astype(F32)
    gy = frame_ref[:, HALF : span + HALF]
    dx, *sums = second_half(x, gy, 9, *weights)
    pack(pack_ref, *sums, old_ref)
    tile = from_windows(jnp.concatenate([dx_ref[...].astype(F32), dx], axis=0))
    dtop_ref[...] = tile[:HALF].astype(BF16)
    dlow_ref[...] = tile[HALF:].astype(BF16)
    dedge_ref[...] = tile[:HALF, cols - WIN :].astype(BF16)
    dcorner_ref[...] = tile[HALF:, cols - WIN :].astype(BF16)


def last_kernel(*refs):
    (own, above, left, corner), kept_refs, refs = refs[:4], refs[4:6], refs[6:]
    w_qkv_ref, w_proj_ref, w_up_ref, w_down_ref, gain_ref, other_ref, core_ref = refs[:7]
    dx_ref, keep_ref, send_ref, frame_ref, pack_ref = refs[7:]
    cols = own.shape[1]
    frame_ref[HALF:, 0:WIN] = left[...].astype(F32)
    frame_ref[0:HALF, 0:WIN] = corner[...].astype(F32)
    first = frame_ref[:, HALF:WIN]
    frame_ref[:, 0:HALF] = first
    frame_ref[HALF:, HALF : HALF + cols] = own[...].astype(F32)
    frame_ref[0:HALF, HALF : HALF + cols] = above[...].astype(F32)
    gy = to_windows(frame_ref[:, 0:cols]).astype(BF16)
    kept = [jnp.concatenate([ref[:, place] for ref in kept_refs], axis=0) for place in kept_slices()]
    kept = [v.astype(F32) if i in (0, 1, 5, 6) else v for i, v in enumerate(kept)]
    g1, g2 = gain_ref[0, 0:1], gain_ref[0, 1:2]
    dx, grads, bias, gain1, gain2 = backward(
        gy, kept, nn(kept[2], w_qkv_ref[0]).astype(BF16), w_qkv_ref[0], w_proj_ref[0], w_up_ref[0], w_down_ref[0], g1, g2, head_mask(), 8
    )
    dx_ref[...] = from_windows(dx).astype(BF16)
    pack(pack_ref, grads, bias, gain1, gain2)
    first_core = core_ref[0] == 0

    @pl.when(first_core)
    def _():
        keep_ref[...] = pack_ref[...]
        send_ref[...] = other_ref[...].astype(BF16)

    @pl.when(jnp.logical_not(first_core))
    def _():
        keep_ref[...] = other_ref[...]
        send_ref[...] = pack_ref[...].astype(BF16)


def unpack_kernel(core_ref, own_ref, other_ref, *refs):
    qkv_ref, proj_ref, up_ref, down_ref, gain_ref, bias_ref, whole_ref = refs
    at = pl.multiple_of(core_ref[0] * ROWS, ROWS)
    whole_ref[pl.ds(at, ROWS)] = own_ref[...].astype(F32)
    whole_ref[pl.ds(ROWS - at, ROWS)] = other_ref[...].astype(F32)
    for b in range(2):
        at = b * ROWS
        for j in range(3):
            qkv_ref[b, :, CH * j : CH * (j + 1)] = whole_ref[at + ROW_QKV + CH * j : at + ROW_QKV + CH * (j + 1)]
        proj_ref[b] = whole_ref[at + ROW_PROJ : at + ROW_PROJ + CH]
        for j in range(4):
            up_ref[b, :, CH * j : CH * (j + 1)] = whole_ref[at + ROW_UP + CH * j : at + ROW_UP + CH * (j + 1)]
        down_ref[b] = whole_ref[at + ROW_DOWN : at + ROW_DOWN + FFN]
        for j in range(2):
            turned = whole_ref[at + ROW_BIAS + LEN * j : at + ROW_BIAS + LEN * (j + 1)].T
            bias_ref[b, 2 * j] = turned[:LEN]
            bias_ref[b, 2 * j + 1] = turned[LEN:]
        gain_ref[b] = whole_ref[at + ROW_GAIN : at + ROW_GAIN + 2]


def vmem(count):
    return [pl.BlockSpec(memory_space=pltpu.VMEM)] * count


def cost(flops, moved):
    return pl.CostEstimate(flops=flops, bytes_accessed=moved, transcendentals=0)


def shift(value, down, right):
    tall, wide = 32, 8
    pairs = []
    for r in range(tall):
        for c in range(wide):
            pairs.append((r * wide + c, (r + down) % tall * wide + (c + right) % wide))
    return lax.ppermute(value, AXES, pairs)


def swap_core(value):
    return lax.ppermute(value, "core", [(0, 1), (1, 0)])


def scatter_sum(value, axis, count):
    pieces = value.astype(BF16).reshape(count, value.shape[0] // count, CH)
    return jnp.sum(lax.all_to_all(pieces, axis, 0, 0).astype(F32), axis=0)


def collect(value, axis, count):
    spread = jnp.broadcast_to(value[None], (count, *value.shape))
    return lax.all_to_all(spread, axis, 0, 0)


def sum_over_devices(keep, send):
    total = keep + swap_core(send).astype(F32)
    total = scatter_sum(total, PLANE, 16)
    total = jnp.sum(collect(total.astype(BF16), "z", 8).astype(F32), axis=0).astype(BF16)
    total = collect(total, PLANE, 16).reshape(ROWS, CH)
    return total, swap_core(total)


def body(latent, cotangent, w_qkv, w_proj, w_up, w_down, gains, attn_bias):
    cols = latent.shape[1]
    half = jax.ShapeDtypeStruct((HALF, cols, CH), BF16)
    params = pltpu.CompilerParams(vmem_limit_bytes=VMEM_LIMIT)
    packed = jax.ShapeDtypeStruct((ROWS, CH), F32)
    core = lax.axis_index("core").reshape(1)
    weights = (w_qkv, w_proj, w_up, w_down, gains)
    g_below = shift(cotangent, -1, 0)
    tokens = WIN * cols

    wide = cols // 2
    part_a = WIN * (wide - WIN)
    small = jax.ShapeDtypeStruct((HALF, WIN, CH), BF16)
    side = jax.ShapeDtypeStruct((HALF, wide, CH), BF16)
    corner = jax.ShapeDtypeStruct((WIN, WIN, CH), BF16)
    top_a, low_a, edge_own = pl.pallas_call(
        first_kernel,
        out_shape=(side, side, corner),
        in_specs=[pl.BlockSpec(memory_space=pltpu.HBM)] * 8,
        out_specs=vmem(3),
        scratch_shapes=[pltpu.VMEM((WIN, wide, CH), BF16)]
        + [pltpu.VMEM(w.shape[1:], w.dtype) for w in (*weights, attn_bias)]
        + [pltpu.VMEM((HALF, WIN, CH), BF16), pltpu.SemaphoreType.DMA((8,))],
        compiler_params=pltpu.CompilerParams(vmem_limit_bytes=FIRST_LIMIT),
        cost_estimate=cost(300_000_000, 1_500_000),
        name="forward_first",
    )(latent, *weights, attn_bias, cotangent)
    below_a = shift(top_a, -1, 0)
    top_b, low_b = pl.pallas_call(
        next_kernel,
        out_shape=(side, side),
        in_specs=vmem(7),
        out_specs=vmem(2),
        compiler_params=params,
        cost_estimate=cost(300_000_000, 1_500_000),
        name="forward_next",
    )(latent, *weights, attn_bias)
    below_b = shift(top_b, -1, 0)
    edge = shift(jnp.concatenate([edge_own, below_a[:, :WIN], g_below[:HALF, :WIN]], axis=0), 0, -1)
    weights = (*weights, attn_bias)
    frame = pltpu.VMEM((WIN, cols + 2 * WIN, CH), F32)
    dx_a, pack_a = pl.pallas_call(
        second_kernel,
        out_shape=(jax.ShapeDtypeStruct((part_a, CH), BF16), packed),
        in_specs=vmem(10),
        out_specs=vmem(2),
        scratch_shapes=[frame],
        compiler_params=params,
        cost_estimate=cost(700_000_000, 3_000_000),
        name="backward_second",
    )(low_a, below_a, cotangent, g_below, *weights)
    edge, below_b, dx_a = lax.optimization_barrier((edge, below_b, dx_a))
    d_top, d_low, d_edge, d_corner, pack_two = pl.pallas_call(
        third_kernel,
        out_shape=(half, half, small, small, packed),
        in_specs=vmem(15),
        out_specs=vmem(5),
        scratch_shapes=[frame],
        compiler_params=params,
        cost_estimate=cost(800_000_000, 3_000_000),
        name="backward_third",
    )(low_a, low_b, below_a, below_b, cotangent, g_below, edge, *weights, dx_a, pack_a)
    d_above, d_left, d_corner = shift(d_low, 1, 0), shift(d_edge, 0, 1), shift(d_corner, 1, 1)
    kept = []
    for part in range(2):
        made = pl.pallas_call(
            functools.partial(keep_kernel, part),
            out_shape=jax.ShapeDtypeStruct((WIN * wide, sum(KEPT)), BF16),
            in_specs=vmem(5),
            out_specs=vmem(1)[0],
            compiler_params=params,
            cost_estimate=cost(300_000_000, 2_000_000),
            name="keep_first",
        )(latent, w_qkv, w_proj, gains, attn_bias)
        kept.append(made)
    dx, keep, send = pl.pallas_call(
        last_kernel,
        out_shape=(
            jax.ShapeDtypeStruct(latent.shape, BF16),
            packed,
            jax.ShapeDtypeStruct((ROWS, CH), BF16),
        ),
        in_specs=vmem(12) + [pl.BlockSpec(memory_space=pltpu.SMEM)],
        out_specs=vmem(3),
        scratch_shapes=[frame, pltpu.VMEM((ROWS, CH), F32)],
        compiler_params=params,
        cost_estimate=cost(1_500_000_000, 4_000_000),
        name="backward_first",
    )(d_top, d_above, d_left, d_corner, *kept, *weights[:5], pack_two, core)
    parts = sum_over_devices(keep, send)
    qkv, proj, up, down, gain, bias = pl.pallas_call(
        unpack_kernel,
        out_shape=(
            jax.ShapeDtypeStruct((2, CH, 3 * CH), F32),
            jax.ShapeDtypeStruct((2, CH, CH), F32),
            jax.ShapeDtypeStruct((2, CH, FFN), F32),
            jax.ShapeDtypeStruct((2, FFN, CH), F32),
            jax.ShapeDtypeStruct((2, 2, CH), F32),
            jax.ShapeDtypeStruct((2, HEADS, LEN, LEN), F32),
        ),
        in_specs=[pl.BlockSpec(memory_space=pltpu.SMEM)] + vmem(2),
        out_specs=vmem(6),
        scratch_shapes=[pltpu.VMEM((2 * ROWS, CH), F32)],
        compiler_params=params,
        cost_estimate=cost(1_000_000, 4_000_000),
        name="unpack",
    )(core, *parts)
    return dx, qkv, proj, up, down, gain, bias


def solution(mesh):
    fine = jax.sharding.Mesh(mesh.devices.reshape(8, 2, 2, 4, 2), AXES)
    tiles = P(("z", "yh", "core"), ("x", "yl"), None)
    in_specs = (tiles, tiles, P(), P(), P(), P(), P(), P())
    out_specs = (tiles, P(), P(), P(), P(), P(), P())
    return jax.shard_map(body, mesh=fine, in_specs=in_specs, out_specs=out_specs, check_vma=False)
```

```python
import functools

import jax
import jax.numpy as jnp
from jax import lax
from jax.experimental import pallas as pl
from jax.experimental.pallas import tpu as pltpu
from jax.sharding import PartitionSpec as P

WIN = 8
HALF = 4
LEN = 64
CH = 128
HEADS = 4
FFN = 512
EPS = 1e-05
SCALE = (CH // HEADS) ** -0.5
F32 = jnp.float32
BF16 = jnp.bfloat16
VMEM_LIMIT = 16 * 1024 * 1024
FIRST_LIMIT = 57 * 1000 * 1000

ROW_QKV, ROW_PROJ, ROW_UP, ROW_DOWN, ROW_BIAS, ROW_GAIN, ROWS = 0, 384, 512, 1024, 1536, 1664, 1792
AXES = ("z", "yh", "core", "x", "yl")
PLANE = ("yh", "x", "yl")


def nn(a, b):
    return lax.dot_general(a, b, (((1,), (0,)), ((), ())), preferred_element_type=F32)


def nt(a, b):
    return lax.dot_general(a, b, (((1,), (1,)), ((), ())), preferred_element_type=F32)


def tn(a, b):
    return lax.dot_general(a, b, (((0,), (0,)), ((), ())), preferred_element_type=F32)


def lane_means(parts):
    width = len(parts) * CH
    block = lax.broadcasted_iota(jnp.int32, (width, width), 0) // CH == lax.broadcasted_iota(jnp.int32, (width, width), 1) // CH
    ones = (block.astype(F32) * (1.0 / CH)).astype(BF16)
    sums = nn(jnp.concatenate([p.astype(BF16) for p in parts], axis=1), ones)
    return [sums[:, CH * i : CH * (i + 1)] for i in range(len(parts))]


def normalise(v):
    centre = v - jnp.mean(v, axis=-1, keepdims=True)
    spread = jnp.mean(centre * centre, axis=-1, keepdims=True)
    inv = lax.rsqrt(spread + EPS)
    return centre * inv, inv


def normalise_back(dn, hat, inv, gain):
    d_hat = dn * gain
    mean, along = lane_means([d_hat, d_hat * hat])
    return inv * (d_hat - mean - hat * along)


def head_mask():
    rows = lax.broadcasted_iota(jnp.int32, (HEADS * LEN, CH), 0) // LEN
    lanes = lax.broadcasted_iota(jnp.int32, (HEADS * LEN, CH), 1) // (CH // HEADS)
    return (rows == lanes).astype(F32).astype(BF16)


def spread_heads(v, mask):
    return jnp.concatenate([v] * HEADS, axis=0) * mask


def gather_heads(v):
    lane = lax.broadcasted_iota(jnp.int32, (LEN, CH), 1)
    size = CH // HEADS
    out = v[3 * LEN :]
    for h in (2, 1, 0):
        out = jnp.where(lane < (h + 1) * size, v[h * LEN : (h + 1) * LEN], out)
    return out


def rows_of(values, w):
    return values[w * LEN : (w + 1) * LEN]


def groups_of(tokens, group):
    count = tokens // LEN
    return [range(start, min(start + group, count)) for start in range(0, count, group)]


def in_stages(stages, groups):
    state = [None] * len(groups)
    for step in range(len(groups) + len(stages) - 1):
        for s in reversed(range(len(stages))):
            g = step - s
            if 0 <= g < len(groups):
                state[g] = stages[s](groups[g], state[g])
    return state


def attention(qkv, bias_t, mask, group):
    def scores(windows, _):
        parts = [rows_of(qkv, w) for w in windows]
        return parts, [nt(x[:, CH : 2 * CH], spread_heads(x[:, :CH], mask)) * SCALE + bias_t for x in parts]

    def softmax(_, state):
        parts, values = state
        e = [jnp.exp(x - jnp.max(x, axis=0, keepdims=True)) for x in values]
        return parts, [(x * (1.0 / jnp.sum(x, axis=0, keepdims=True))).astype(BF16) for x in e]

    def mix(_, state):
        parts, p = state
        o = [tn(x, y[:, 2 * CH :]) for x, y in zip(p, parts)]
        return [gather_heads(x).astype(BF16) for x in o], p

    done = in_stages((scores, softmax, mix), groups_of(qkv.shape[0], group))
    return jnp.concatenate(sum((x for x, _ in done), []), axis=0), jnp.concatenate(sum((x for _, x in done), []), axis=0)


def attention_back(d_o, qkv, p, mask, group):
    def spread(windows, _):
        parts = [rows_of(qkv, w) for w in windows]
        weights = [rows_of(p, w) for w in windows]
        do_spread = [spread_heads(rows_of(d_o, w), mask) for w in windows]
        dp = [nt(x[:, 2 * CH :], y) for x, y in zip(parts, do_spread)]
        return parts, weights, dp, [nn(x, y) for x, y in zip(weights, do_spread)]

    def softmax(_, state):
        parts, weights, dp, dv = state
        weights = [x.astype(F32) for x in weights]
        return parts, [x * (y - jnp.sum(y * x, axis=0, keepdims=True)) for x, y in zip(weights, dp)], dv

    def mix(_, state):
        parts, ds, dv = state
        dsb = [x.astype(BF16) for x in ds]
        dk = [nn(x, spread_heads(y[:, :CH], mask)) * SCALE for x, y in zip(dsb, parts)]
        dq = [gather_heads(tn(x, y[:, CH : 2 * CH])) * SCALE for x, y in zip(dsb, parts)]
        return [jnp.concatenate(x, axis=1).astype(BF16) for x in zip(dq, dk, dv)], sum(ds[1:], ds[0])

    done = in_stages((spread, softmax, mix), groups_of(qkv.shape[0], group))
    bias = sum((x for _, x in done[1:]), done[0][1])
    return jnp.concatenate(sum((x for x, _ in done), []), axis=0), bias


def gelu_and_slope(u):
    c = 0.7978845608028654
    sq = u * u
    s = 0.5 * jnp.tanh(u * (c + (c * 0.044715) * sq)) + 0.5
    m = u * s
    return m, s + m * (1.0 - s) * (2.0 * c + (6.0 * c * 0.044715) * sq)


def forward(x, w_qkv, w_proj, gains, bias, mask, group):
    hat1, inv1 = normalise(x)
    gain = gains()
    a1 = (hat1 * gain[0:1]).astype(BF16)
    qkv = nn(a1, w_qkv()).astype(BF16)
    o, p = attention(qkv, turned_bias(bias()), mask, group)
    h = (x + nn(o, w_proj())).astype(BF16).astype(F32)
    hat2, inv2 = normalise(h)
    a2 = (hat2 * gain[1:2]).astype(BF16)
    return h, (hat1, inv1, a1, p, o, hat2, inv2, a2), qkv


def backward(gy, kept, qkv, w_qkv, w_proj, w_up, w_down, g1, g2, mask, group):
    hat1, inv1, a1, p, o, hat2, inv2, a2 = kept
    m, slope = gelu_and_slope(nn(a2, w_up))
    m = m.astype(BF16)
    du = (nt(gy, w_down) * slope).astype(BF16)
    da2 = nt(du, w_up)
    down, up = tn(gy, m), tn(a2, du)
    gain2 = jnp.sum(da2 * hat2, axis=0, keepdims=True)
    dh = gy.astype(F32) + normalise_back(da2, hat2, inv2, g2)
    dhb = dh.astype(BF16)
    d_o = nt(dhb, w_proj).astype(BF16)
    proj = tn(o, dhb)
    dqkv, bias = attention_back(d_o, qkv, p, mask, group)
    da1 = nt(dqkv, w_qkv)
    grads = (tn(a1, dqkv), proj, up, down)
    gain1 = jnp.sum(da1 * hat1, axis=0, keepdims=True)
    dx = dh + normalise_back(da1, hat1, inv1, g1)
    return dx, grads, bias, gain1, gain2


def pack(pack_ref, grads, bias, gain1, gain2, old=None):
    qkv, proj, up, down = grads

    def put(at, value):
        rows = slice(at, at + value.shape[0])
        pack_ref[rows] = value if old is None else value + old[rows].astype(F32)

    for j in range(3):
        put(ROW_QKV + CH * j, qkv[:, CH * j : CH * (j + 1)])
    put(ROW_PROJ, proj)
    for j in range(4):
        put(ROW_UP + CH * j, up[:, CH * j : CH * (j + 1)])
        put(ROW_DOWN + CH * j, down[:, CH * j : CH * (j + 1)].T)
    put(ROW_BIAS, bias[:, :CH])
    put(ROW_BIAS + LEN, bias[:, CH:])
    put(ROW_GAIN, jnp.concatenate([gain1, gain2, jnp.zeros((ROWS - ROW_GAIN - 2, CH), F32)], axis=0))


def to_windows(tile):
    rows, cols, ch = tile.shape
    return tile.reshape(WIN, cols // WIN, WIN, ch).transpose(1, 0, 2, 3).reshape(-1, ch)


def from_windows(tokens):
    count = tokens.shape[0] // LEN
    return tokens.reshape(count, WIN, WIN, CH).transpose(1, 0, 2, 3).reshape(WIN, count * WIN, CH)


def turned_bias(bias):
    return jnp.concatenate([bias[h].T for h in range(HEADS)], axis=1)


def first_half(x, group, w_qkv, w_proj, w_up, w_down, gains, bias):
    h, kept, _ = forward(to_windows(x.astype(F32)), w_qkv, w_proj, gains, bias, head_mask(), group)
    m, _ = gelu_and_slope(nn(kept[7], w_up()))
    return from_windows(h + nn(m.astype(BF16), w_down()))


def first_kernel(*refs):
    sources, (top_ref, low_ref, edge_ref), refs = refs[:8], refs[8:11], refs[11:]
    targets, sem = refs[:8], refs[8]
    wide = sources[0].shape[1] // 2
    moves = [(sources[0].at[:, 0:wide], targets[0])]
    moves += [(source.at[0], target) for source, target in zip(sources[1:7], targets[1:7])]
    moves += [(sources[7].at[HALF:, 0:WIN], targets[7])]
    copies = [pltpu.make_async_copy(source, target, sem.at[i]) for i, (source, target) in enumerate(moves)]
    for i in (0, 5, 1, 6, 2, 3, 4, 7):
        copies[i].start(priority=1)

    def fetched(i):
        copies[i].wait()
        return targets[i][...]

    parts = [functools.partial(fetched, i) for i in range(1, 7)]
    tile = first_half(fetched(0), 8, *parts)
    top_ref[...] = tile[:HALF].astype(BF16)
    low_ref[...] = tile[HALF:].astype(BF16)
    edge_ref[0:HALF] = tile[HALF:, 0:WIN].astype(BF16)
    edge_ref[HALF:] = fetched(7)


def at(ref, i):
    return lambda: ref[i]


def next_kernel(x_ref, w_qkv_ref, w_proj_ref, w_up_ref, w_down_ref, gain_ref, bias_ref, top_ref, low_ref):
    wide = x_ref.shape[1] // 2
    parts = [at(ref, 0) for ref in (w_qkv_ref, w_proj_ref, w_up_ref, w_down_ref, gain_ref, bias_ref)]
    tile = first_half(x_ref[:, wide:], 8, *parts)
    top_ref[...] = tile[:HALF].astype(BF16)
    low_ref[...] = tile[HALF:].astype(BF16)


KEPT = (CH, CH, CH, HEADS * LEN, CH, CH, CH, CH)


def kept_slices():
    starts = [sum(KEPT[:i]) for i in range(len(KEPT))]
    return [slice(start, start + width) for start, width in zip(starts, KEPT)]


def keep_kernel(part, x_ref, w_qkv_ref, w_proj_ref, gain_ref, bias_ref, *refs):
    kept_ref = refs[len(refs) // 2]
    for source, target in zip(refs[: len(refs) // 2], refs[len(refs) // 2 + 1 :]):
        target[...] = source[...]
    wide = x_ref.shape[1] // 2
    x = to_windows(x_ref[:, part * wide : (part + 1) * wide].astype(F32))
    _, kept, _ = forward(x, at(w_qkv_ref, 0), at(w_proj_ref, 0), at(gain_ref, 0), at(bias_ref, 0), head_mask(), 8)
    for place, value, width in zip(kept_slices(), kept, KEPT):
        kept_ref[:, place] = jnp.broadcast_to(value, (x.shape[0], width)).astype(BF16)


def second_half(x, gy, group, w_qkv_ref, w_proj_ref, w_up_ref, w_down_ref, gain_ref, bias_ref):
    mask = head_mask()
    _, kept, qkv = forward(
        to_windows(x), at(w_qkv_ref, 1), at(w_proj_ref, 1), at(gain_ref, 1), at(bias_ref, 1), mask, group
    )
    w_qkv, w_proj, w_up, w_down = w_qkv_ref[1], w_proj_ref[1], w_up_ref[1], w_down_ref[1]
    g1, g2 = gain_ref[1, 0:1], gain_ref[1, 1:2]
    return backward(to_windows(gy).astype(BF16), kept, qkv, w_qkv, w_proj, w_up, w_down, g1, g2, mask, group)


def second_kernel(*refs):
    low_ref, below_ref, g_own_ref, g_below_ref = refs[:4]
    weights, (dx_ref, pack_ref, frame_ref) = refs[4:10], refs[10:]
    wide = low_ref.shape[1]
    frame_ref[0:HALF, 0:wide] = low_ref[...].astype(F32)
    frame_ref[HALF:, 0:wide] = below_ref[...].astype(F32)
    x = frame_ref[:, HALF : wide - HALF]
    frame_ref[0:HALF, 0:wide] = g_own_ref[HALF:, 0:wide].astype(F32)
    frame_ref[HALF:, 0:wide] = g_below_ref[0:HALF, 0:wide].astype(F32)
    gy = frame_ref[:, HALF : wide - HALF]
    dx, *sums = second_half(x, gy, 7, *weights)
    dx_ref[...] = dx.astype(BF16)
    pack(pack_ref, *sums)


def third_kernel(*refs):
    low_a_ref, low_b_ref, below_a_ref, below_b_ref, g_own_ref, g_below_ref, edge_ref = refs[:7]
    weights, (dx_ref, old_ref, dtop_ref, dlow_ref, dedge_ref, dcorner_ref, pack_ref, frame_ref) = refs[7:13], refs[13:]
    wide, cols = low_a_ref.shape[1], g_own_ref.shape[1]
    span = cols - wide + WIN
    frame_ref[0:HALF, 0:WIN] = low_a_ref[:, wide - WIN :].astype(F32)
    frame_ref[HALF:, 0:WIN] = below_a_ref[:, wide - WIN :].astype(F32)
    frame_ref[0:HALF, WIN:span] = low_b_ref[...].astype(F32)
    frame_ref[HALF:, WIN:span] = below_b_ref[...].astype(F32)
    frame_ref[0:HALF, span : span + WIN] = edge_ref[0:HALF].astype(F32)
    frame_ref[HALF:, span : span + WIN] = edge_ref[WIN : WIN + HALF].astype(F32)
    x = frame_ref[:, HALF : span + HALF]
    frame_ref[0:HALF, 0:span] = g_own_ref[HALF:, wide - WIN :].astype(F32)
    frame_ref[HALF:, 0:span] = g_below_ref[0:HALF, wide - WIN :].astype(F32)
    frame_ref[0:HALF, span : span + WIN] = edge_ref[HALF:WIN].astype(F32)
    frame_ref[HALF:, span : span + WIN] = edge_ref[WIN + HALF :].astype(F32)
    gy = frame_ref[:, HALF : span + HALF]
    dx, *sums = second_half(x, gy, 9, *weights)
    pack(pack_ref, *sums, old_ref)
    tile = from_windows(jnp.concatenate([dx_ref[...].astype(F32), dx], axis=0))
    dtop_ref[...] = tile[:HALF].astype(BF16)
    dlow_ref[...] = tile[HALF:].astype(BF16)
    dedge_ref[...] = tile[:HALF, cols - WIN :].astype(BF16)
    dcorner_ref[...] = tile[HALF:, cols - WIN :].astype(BF16)


def last_kernel(*refs):
    (own, above, left, corner), kept_refs, refs = refs[:4], refs[4:6], refs[6:]
    w_qkv_ref, w_proj_ref, w_up_ref, w_down_ref, gain_ref, other_ref, core_ref = refs[:7]
    dx_ref, keep_ref, send_ref, frame_ref, pack_ref = refs[7:]
    cols = own.shape[1]
    frame_ref[HALF:, 0:WIN] = left[...].astype(F32)
    frame_ref[0:HALF, 0:WIN] = corner[...].astype(F32)
    first = frame_ref[:, HALF:WIN]
    frame_ref[:, 0:HALF] = first
    frame_ref[HALF:, HALF : HALF + cols] = own[...].astype(F32)
    frame_ref[0:HALF, HALF : HALF + cols] = above[...].astype(F32)
    gy = to_windows(frame_ref[:, 0:cols]).astype(BF16)
    kept = [jnp.concatenate([ref[:, place] for ref in kept_refs], axis=0) for place in kept_slices()]
    kept = [v.astype(F32) if i in (0, 1, 5, 6) else v for i, v in enumerate(kept)]
    g1, g2 = gain_ref[0, 0:1], gain_ref[0, 1:2]
    dx, grads, bias, gain1, gain2 = backward(
        gy, kept, nn(kept[2], w_qkv_ref[0]).astype(BF16), w_qkv_ref[0], w_proj_ref[0], w_up_ref[0], w_down_ref[0], g1, g2, head_mask(), 8
    )
    dx_ref[...] = from_windows(dx).astype(BF16)
    pack(pack_ref, grads, bias, gain1, gain2)
    first_core = core_ref[0] == 0

    @pl.when(first_core)
    def _():
        keep_ref[...] = pack_ref[...]
        send_ref[...] = other_ref[...].astype(BF16)

    @pl.when(jnp.logical_not(first_core))
    def _():
        keep_ref[...] = other_ref[...]
        send_ref[...] = pack_ref[...].astype(BF16)


def unpack_kernel(mine, core_ref, part_ref, *refs):
    outs, places, sem = refs[-13:-7], refs[-7:-1], refs[-1]
    qkv, proj, up, down, gain, bias = places
    for j in range(3):
        qkv[:, CH * j : CH * (j + 1)] = part_ref[ROW_QKV + CH * j : ROW_QKV + CH * (j + 1)].astype(F32)
    proj[...] = part_ref[ROW_PROJ : ROW_PROJ + CH].astype(F32)
    for j in range(4):
        up[:, CH * j : CH * (j + 1)] = part_ref[ROW_UP + CH * j : ROW_UP + CH * (j + 1)].astype(F32)
    down[...] = part_ref[ROW_DOWN : ROW_DOWN + FFN].astype(F32)
    for j in range(2):
        turned = part_ref[ROW_BIAS + LEN * j : ROW_BIAS + LEN * (j + 1)].astype(F32).T
        bias[2 * j] = turned[:LEN]
        bias[2 * j + 1] = turned[LEN:]
    gain[...] = part_ref[ROW_GAIN : ROW_GAIN + 16].astype(F32)[0:2]
    block = core_ref[0] if mine else 1 - core_ref[0]
    copies = [pltpu.make_async_copy(a, b.at[block], sem.at[i]) for i, (a, b) in enumerate(zip(places, outs))]
    for copy in copies:
        copy.start()
    for copy in copies:
        copy.wait()


def vmem(count):
    return [pl.BlockSpec(memory_space=pltpu.VMEM)] * count


def cost(flops, moved):
    return pl.CostEstimate(flops=flops, bytes_accessed=moved, transcendentals=0)


def shift(value, down, right):
    tall, wide = 32, 8
    pairs = []
    for r in range(tall):
        for c in range(wide):
            pairs.append((r * wide + c, (r + down) % tall * wide + (c + right) % wide))
    return lax.ppermute(value, AXES, pairs)


def swap_core(value):
    return lax.ppermute(value, "core", [(0, 1), (1, 0)])


def scatter_sum(value, axis, count):
    pieces = value.astype(BF16).reshape(count, value.shape[0] // count, CH)
    return jnp.sum(lax.all_to_all(pieces, axis, 0, 0).astype(F32), axis=0)


def collect(value, axis, count):
    spread = jnp.broadcast_to(value[None], (count, *value.shape))
    return lax.all_to_all(spread, axis, 0, 0)


def sum_over_devices(keep, send):
    total = keep + swap_core(send).astype(F32)
    total = scatter_sum(total, PLANE, 16)
    total = jnp.sum(collect(total.astype(BF16), "z", 8).astype(F32), axis=0).astype(BF16)
    total = collect(total, PLANE, 16).reshape(ROWS, CH)
    return total, swap_core(total)


def body(latent, cotangent, w_qkv, w_proj, w_up, w_down, gains, attn_bias):
    cols = latent.shape[1]
    half = jax.ShapeDtypeStruct((HALF, cols, CH), BF16)
    params = pltpu.CompilerParams(vmem_limit_bytes=VMEM_LIMIT)
    packed = jax.ShapeDtypeStruct((ROWS, CH), F32)
    core = lax.axis_index("core").reshape(1)
    weights = (w_qkv, w_proj, w_up, w_down, gains)
    g_below = shift(cotangent, -1, 0)
    tokens = WIN * cols

    wide = cols // 2
    part_a = WIN * (wide - WIN)
    small = jax.ShapeDtypeStruct((HALF, WIN, CH), BF16)
    side = jax.ShapeDtypeStruct((HALF, wide, CH), BF16)
    corner = jax.ShapeDtypeStruct((WIN, WIN, CH), BF16)
    top_a, low_a, edge_own = pl.pallas_call(
        first_kernel,
        out_shape=(side, side, corner),
        in_specs=[pl.BlockSpec(memory_space=pltpu.HBM)] * 8,
        out_specs=vmem(3),
        scratch_shapes=[pltpu.VMEM((WIN, wide, CH), BF16)]
        + [pltpu.VMEM(w.shape[1:], w.dtype) for w in (*weights, attn_bias)]
        + [pltpu.VMEM((HALF, WIN, CH), BF16), pltpu.SemaphoreType.DMA((8,))],
        compiler_params=pltpu.CompilerParams(vmem_limit_bytes=FIRST_LIMIT),
        cost_estimate=cost(300_000_000, 1_500_000),
        name="forward_first",
    )(latent, *weights, attn_bias, cotangent)
    below_a = shift(top_a, -1, 0)
    top_b, low_b = pl.pallas_call(
        next_kernel,
        out_shape=(side, side),
        in_specs=vmem(7),
        out_specs=vmem(2),
        compiler_params=params,
        cost_estimate=cost(300_000_000, 1_500_000),
        name="forward_next",
    )(latent, *weights, attn_bias)
    below_b = shift(top_b, -1, 0)
    edge = shift(jnp.concatenate([edge_own, below_a[:, :WIN], g_below[:HALF, :WIN]], axis=0), 0, -1)
    weights = (*weights, attn_bias)
    frame = pltpu.VMEM((WIN, cols + 2 * WIN, CH), F32)
    dx_a, pack_a = pl.pallas_call(
        second_kernel,
        out_shape=(jax.ShapeDtypeStruct((part_a, CH), BF16), packed),
        in_specs=vmem(10),
        out_specs=vmem(2),
        scratch_shapes=[frame],
        compiler_params=params,
        cost_estimate=cost(700_000_000, 3_000_000),
        name="backward_second",
    )(low_a, below_a, cotangent, g_below, *weights)
    edge, below_b, dx_a = lax.optimization_barrier((edge, below_b, dx_a))
    d_top, d_low, d_edge, d_corner, pack_two = pl.pallas_call(
        third_kernel,
        out_shape=(half, half, small, small, packed),
        in_specs=vmem(15),
        out_specs=vmem(5),
        scratch_shapes=[frame],
        compiler_params=params,
        cost_estimate=cost(800_000_000, 3_000_000),
        name="backward_third",
    )(low_a, low_b, below_a, below_b, cotangent, g_below, edge, *weights, dx_a, pack_a)
    d_above, d_left, d_corner = shift(d_low, 1, 0), shift(d_edge, 0, 1), shift(d_corner, 1, 1)
    passed = ()
    for part, arrays in enumerate(((), (pack_two, d_top))):
        arrays = (*passed, *arrays)
        passed = pl.pallas_call(
            functools.partial(keep_kernel, part),
            out_shape=(
                jax.ShapeDtypeStruct((WIN * wide, sum(KEPT)), BF16),
                *[jax.ShapeDtypeStruct(a.shape, a.dtype) for a in arrays],
            ),
            in_specs=vmem(5 + len(arrays)),
            out_specs=vmem(1 + len(arrays)),
            compiler_params=params,
            cost_estimate=cost(300_000_000, 2_000_000),
            name="keep_first",
        )(latent, w_qkv, w_proj, gains, attn_bias, *arrays)
    kept_b, kept_a, pack_two, d_top = passed
    dx, keep, send = pl.pallas_call(
        last_kernel,
        out_shape=(
            jax.ShapeDtypeStruct(latent.shape, BF16),
            packed,
            jax.ShapeDtypeStruct((ROWS, CH), BF16),
        ),
        in_specs=vmem(12) + [pl.BlockSpec(memory_space=pltpu.SMEM)],
        out_specs=vmem(3),
        scratch_shapes=[frame, pltpu.VMEM((ROWS, CH), F32)],
        compiler_params=params,
        cost_estimate=cost(1_500_000_000, 4_000_000),
        name="backward_first",
    )(d_top, d_above, d_left, d_corner, kept_a, kept_b, *weights[:5], pack_two, core)
    parts = sum_over_devices(keep, send)
    shapes = ((CH, 3 * CH), (CH, CH), (CH, FFN), (FFN, CH), (2, CH), (HEADS, LEN, LEN))
    outs = ()
    for mine, part in zip((True, False), parts):
        outs = pl.pallas_call(
            functools.partial(unpack_kernel, mine),
            out_shape=[jax.ShapeDtypeStruct((2, *shape), F32) for shape in shapes],
            in_specs=[pl.BlockSpec(memory_space=pltpu.SMEM)]
            + vmem(1)
            + [pl.BlockSpec(memory_space=pl.ANY)] * len(outs),
            out_specs=[pl.BlockSpec(memory_space=pl.ANY)] * 6,
            scratch_shapes=[pltpu.VMEM(shape, F32) for shape in shapes] + [pltpu.SemaphoreType.DMA((6,))],
            input_output_aliases={2 + i: i for i in range(len(outs))},
            compiler_params=params,
            cost_estimate=cost(1_000_000, 2_000_000),
            name="unpack",
        )(core, part, *outs)
    qkv, proj, up, down, gain, bias = outs
    return dx, qkv, proj, up, down, gain, bias


def solution(mesh):
    fine = jax.sharding.Mesh(mesh.devices.reshape(8, 2, 2, 4, 2), AXES)
    tiles = P(("z", "yh", "core"), ("x", "yl"), None)
    in_specs = (tiles, tiles, P(), P(), P(), P(), P(), P())
    out_specs = (tiles, P(), P(), P(), P(), P(), P())
    return jax.shard_map(body, mesh=fine, in_specs=in_specs, out_specs=out_specs, check_vma=False)
```

```python
import functools

import jax
import jax.numpy as jnp
from jax import lax
from jax.experimental import pallas as pl
from jax.experimental.pallas import tpu as pltpu
from jax.sharding import PartitionSpec as P

WIN = 8
HALF = 4
LEN = 64
CH = 128
HEADS = 4
FFN = 512
EPS = 1e-05
SCALE = (CH // HEADS) ** -0.5
F32 = jnp.float32
BF16 = jnp.bfloat16
VMEM_LIMIT = 16 * 1024 * 1024
FIRST_LIMIT = 57 * 1000 * 1000

ROW_QKV, ROW_PROJ, ROW_UP, ROW_DOWN, ROW_BIAS, ROW_GAIN, ROWS = 0, 384, 512, 1024, 1536, 1664, 1792
AXES = ("z", "yh", "core", "x", "yl")
PLANE = ("yh", "x", "yl")


def nn(a, b):
    return lax.dot_general(a, b, (((1,), (0,)), ((), ())), preferred_element_type=F32)


def nt(a, b):
    return lax.dot_general(a, b, (((1,), (1,)), ((), ())), preferred_element_type=F32)


def tn(a, b):
    return lax.dot_general(a, b, (((0,), (0,)), ((), ())), preferred_element_type=F32)


def lane_means(parts):
    width = len(parts) * CH
    block = lax.broadcasted_iota(jnp.int32, (width, width), 0) // CH == lax.broadcasted_iota(jnp.int32, (width, width), 1) // CH
    ones = (block.astype(F32) * (1.0 / CH)).astype(BF16)
    sums = nn(jnp.concatenate([p.astype(BF16) for p in parts], axis=1), ones)
    return [sums[:, CH * i : CH * (i + 1)] for i in range(len(parts))]


def normalise(v):
    centre = v - jnp.mean(v, axis=-1, keepdims=True)
    spread = jnp.mean(centre * centre, axis=-1, keepdims=True)
    inv = lax.rsqrt(spread + EPS)
    return centre * inv, inv


def normalise_back(dn, hat, inv, gain):
    d_hat = dn * gain
    mean, along = lane_means([d_hat, d_hat * hat])
    return inv * (d_hat - mean - hat * along)


def head_mask():
    rows = lax.broadcasted_iota(jnp.int32, (HEADS * LEN, CH), 0) // LEN
    lanes = lax.broadcasted_iota(jnp.int32, (HEADS * LEN, CH), 1) // (CH // HEADS)
    return (rows == lanes).astype(F32).astype(BF16)


def spread_heads(v, mask):
    return jnp.concatenate([v] * HEADS, axis=0) * mask


def gather_heads(v):
    lane = lax.broadcasted_iota(jnp.int32, (LEN, CH), 1)
    size = CH // HEADS
    out = v[3 * LEN :]
    for h in (2, 1, 0):
        out = jnp.where(lane < (h + 1) * size, v[h * LEN : (h + 1) * LEN], out)
    return out


def rows_of(values, w):
    return values[w * LEN : (w + 1) * LEN]


def groups_of(tokens, group):
    count = tokens // LEN
    return [range(start, min(start + group, count)) for start in range(0, count, group)]


def in_stages(stages, groups):
    state = [None] * len(groups)
    for step in range(len(groups) + len(stages) - 1):
        for s in reversed(range(len(stages))):
            g = step - s
            if 0 <= g < len(groups):
                state[g] = stages[s](groups[g], state[g])
    return state


def attention(qkv, bias_t, mask, group):
    def scores(windows, _):
        parts = [rows_of(qkv, w) for w in windows]
        return parts, [nt(x[:, CH : 2 * CH], spread_heads(x[:, :CH], mask)) * SCALE + bias_t for x in parts]

    def softmax(_, state):
        parts, values = state
        e = [jnp.exp(x - jnp.max(x, axis=0, keepdims=True)) for x in values]
        return parts, [(x * (1.0 / jnp.sum(x, axis=0, keepdims=True))).astype(BF16) for x in e]

    def mix(_, state):
        parts, p = state
        o = [tn(x, y[:, 2 * CH :]) for x, y in zip(p, parts)]
        return [gather_heads(x).astype(BF16) for x in o], p

    done = in_stages((scores, softmax, mix), groups_of(qkv.shape[0], group))
    return jnp.concatenate(sum((x for x, _ in done), []), axis=0), jnp.concatenate(sum((x for _, x in done), []), axis=0)


def attention_back(d_o, qkv, p, mask, group):
    def spread(windows, _):
        parts = [rows_of(qkv, w) for w in windows]
        weights = [rows_of(p, w) for w in windows]
        do_spread = [spread_heads(rows_of(d_o, w), mask) for w in windows]
        dp = [nt(x[:, 2 * CH :], y) for x, y in zip(parts, do_spread)]
        return parts, weights, dp, [nn(x, y) for x, y in zip(weights, do_spread)]

    def softmax(_, state):
        parts, weights, dp, dv = state
        weights = [x.astype(F32) for x in weights]
        return parts, [x * (y - jnp.sum(y * x, axis=0, keepdims=True)) for x, y in zip(weights, dp)], dv

    def mix(_, state):
        parts, ds, dv = state
        dsb = [x.astype(BF16) for x in ds]
        dk = [nn(x, spread_heads(y[:, :CH], mask)) * SCALE for x, y in zip(dsb, parts)]
        dq = [gather_heads(tn(x, y[:, CH : 2 * CH])) * SCALE for x, y in zip(dsb, parts)]
        return [jnp.concatenate(x, axis=1).astype(BF16) for x in zip(dq, dk, dv)], sum(ds[1:], ds[0])

    done = in_stages((spread, softmax, mix), groups_of(qkv.shape[0], group))
    bias = sum((x for _, x in done[1:]), done[0][1])
    return jnp.concatenate(sum((x for x, _ in done), []), axis=0), bias


def gelu_and_slope(u):
    c = 0.7978845608028654
    sq = u * u
    s = 0.5 * jnp.tanh(u * (c + (c * 0.044715) * sq)) + 0.5
    m = u * s
    return m, s + m * (1.0 - s) * (2.0 * c + (6.0 * c * 0.044715) * sq)


def forward(x, w_qkv, w_proj, gains, bias, mask, group):
    hat1, inv1 = normalise(x)
    gain = gains()
    a1 = (hat1 * gain[0:1]).astype(BF16)
    qkv = nn(a1, w_qkv()).astype(BF16)
    o, p = attention(qkv, turned_bias(bias()), mask, group)
    h = (x + nn(o, w_proj())).astype(BF16).astype(F32)
    hat2, inv2 = normalise(h)
    a2 = (hat2 * gain[1:2]).astype(BF16)
    return h, (hat1, inv1, a1, p, o, hat2, inv2, a2), qkv


def backward(gy, kept, qkv, w_qkv, w_proj, w_up, w_down, g1, g2, mask, group):
    hat1, inv1, a1, p, o, hat2, inv2, a2 = kept
    m, slope = gelu_and_slope(nn(a2, w_up))
    m = m.astype(BF16)
    du = (nt(gy, w_down) * slope).astype(BF16)
    da2 = nt(du, w_up)
    down, up = tn(gy, m), tn(a2, du)
    gain2 = jnp.sum(da2 * hat2, axis=0, keepdims=True)
    dh = gy.astype(F32) + normalise_back(da2, hat2, inv2, g2)
    dhb = dh.astype(BF16)
    d_o = nt(dhb, w_proj).astype(BF16)
    proj = tn(o, dhb)
    dqkv, bias = attention_back(d_o, qkv, p, mask, group)
    da1 = nt(dqkv, w_qkv)
    grads = (tn(a1, dqkv), proj, up, down)
    gain1 = jnp.sum(da1 * hat1, axis=0, keepdims=True)
    dx = dh + normalise_back(da1, hat1, inv1, g1)
    return dx, grads, bias, gain1, gain2


def pack(pack_ref, grads, bias, gain1, gain2, old=None):
    qkv, proj, up, down = grads

    def put(at, value):
        rows = slice(at, at + value.shape[0])
        pack_ref[rows] = value if old is None else value + old[rows].astype(F32)

    for j in range(3):
        put(ROW_QKV + CH * j, qkv[:, CH * j : CH * (j + 1)])
    put(ROW_PROJ, proj)
    for j in range(4):
        put(ROW_UP + CH * j, up[:, CH * j : CH * (j + 1)])
        put(ROW_DOWN + CH * j, down[:, CH * j : CH * (j + 1)].T)
    put(ROW_BIAS, bias[:, :CH])
    put(ROW_BIAS + LEN, bias[:, CH:])
    put(ROW_GAIN, jnp.concatenate([gain1, gain2, jnp.zeros((ROWS - ROW_GAIN - 2, CH), F32)], axis=0))


def to_windows(tile):
    rows, cols, ch = tile.shape
    return tile.reshape(WIN, cols // WIN, WIN, ch).transpose(1, 0, 2, 3).reshape(-1, ch)


def from_windows(tokens):
    count = tokens.shape[0] // LEN
    return tokens.reshape(count, WIN, WIN, CH).transpose(1, 0, 2, 3).reshape(WIN, count * WIN, CH)


def turned_bias(bias):
    return jnp.concatenate([bias[h].T for h in range(HEADS)], axis=1)


def first_half(x, group, w_qkv, w_proj, w_up, w_down, gains, bias):
    h, kept, _ = forward(to_windows(x.astype(F32)), w_qkv, w_proj, gains, bias, head_mask(), group)
    m, _ = gelu_and_slope(nn(kept[7], w_up()))
    return from_windows(h + nn(m.astype(BF16), w_down()))


def first_kernel(*refs):
    sources, (top_ref, low_ref, edge_ref), refs = refs[:8], refs[8:11], refs[11:]
    targets, sem = refs[:8], refs[8]
    wide = sources[0].shape[1] // 2
    moves = [(sources[0].at[:, 0:wide], targets[0])]
    moves += [(source.at[0], target) for source, target in zip(sources[1:7], targets[1:7])]
    moves += [(sources[7].at[HALF:, 0:WIN], targets[7])]
    copies = [pltpu.make_async_copy(source, target, sem.at[i]) for i, (source, target) in enumerate(moves)]
    for i in (0, 5, 1, 6, 2, 3, 4, 7):
        copies[i].start(priority=1)

    def fetched(i):
        copies[i].wait()
        return targets[i][...]

    parts = [functools.partial(fetched, i) for i in range(1, 7)]
    tile = first_half(fetched(0), 8, *parts)
    top_ref[...] = tile[:HALF].astype(BF16)
    low_ref[...] = tile[HALF:].astype(BF16)
    edge_ref[0:HALF] = tile[HALF:, 0:WIN].astype(BF16)
    edge_ref[HALF:] = fetched(7)


def at(ref, i):
    return lambda: ref[i]


def next_kernel(x_ref, w_qkv_ref, w_proj_ref, w_up_ref, w_down_ref, gain_ref, bias_ref, top_ref, low_ref):
    wide = x_ref.shape[1] // 2
    parts = [at(ref, 0) for ref in (w_qkv_ref, w_proj_ref, w_up_ref, w_down_ref, gain_ref, bias_ref)]
    tile = first_half(x_ref[:, wide:], 8, *parts)
    top_ref[...] = tile[:HALF].astype(BF16)
    low_ref[...] = tile[HALF:].astype(BF16)


KEPT = (CH, CH, CH, HEADS * LEN, CH, CH, CH, CH)


def kept_slices():
    starts = [sum(KEPT[:i]) for i in range(len(KEPT))]
    return [slice(start, start + width) for start, width in zip(starts, KEPT)]


def keep_kernel(part, x_ref, w_qkv_ref, w_proj_ref, gain_ref, bias_ref, *refs):
    kept_ref = refs[len(refs) // 2]
    for source, target in zip(refs[: len(refs) // 2], refs[len(refs) // 2 + 1 :]):
        target[...] = source[...]
    wide = x_ref.shape[1] // 2
    x = to_windows(x_ref[:, part * wide : (part + 1) * wide].astype(F32))
    _, kept, _ = forward(x, at(w_qkv_ref, 0), at(w_proj_ref, 0), at(gain_ref, 0), at(bias_ref, 0), head_mask(), 8)
    for place, value, width in zip(kept_slices(), kept, KEPT):
        kept_ref[:, place] = jnp.broadcast_to(value, (x.shape[0], width)).astype(BF16)


def second_half(x, gy, group, w_qkv_ref, w_proj_ref, w_up_ref, w_down_ref, gain_ref, bias_ref):
    mask = head_mask()
    _, kept, qkv = forward(
        to_windows(x), at(w_qkv_ref, 1), at(w_proj_ref, 1), at(gain_ref, 1), at(bias_ref, 1), mask, group
    )
    w_qkv, w_proj, w_up, w_down = w_qkv_ref[1], w_proj_ref[1], w_up_ref[1], w_down_ref[1]
    g1, g2 = gain_ref[1, 0:1], gain_ref[1, 1:2]
    return backward(to_windows(gy).astype(BF16), kept, qkv, w_qkv, w_proj, w_up, w_down, g1, g2, mask, group)


def second_kernel(*refs):
    low_ref, below_ref, g_own_ref, g_below_ref = refs[:4]
    weights, (dx_ref, pack_ref, frame_ref) = refs[4:10], refs[10:]
    wide = low_ref.shape[1]
    frame_ref[0:HALF, 0:wide] = low_ref[...].astype(F32)
    frame_ref[HALF:, 0:wide] = below_ref[...].astype(F32)
    x = frame_ref[:, HALF : wide - HALF]
    frame_ref[0:HALF, 0:wide] = g_own_ref[HALF:, 0:wide].astype(F32)
    frame_ref[HALF:, 0:wide] = g_below_ref[0:HALF, 0:wide].astype(F32)
    gy = frame_ref[:, HALF : wide - HALF]
    dx, *sums = second_half(x, gy, 7, *weights)
    dx_ref[...] = dx.astype(BF16)
    pack(pack_ref, *sums)


def third_kernel(*refs):
    low_a_ref, low_b_ref, below_a_ref, below_b_ref, g_own_ref, g_below_ref, edge_ref = refs[:7]
    weights, (dx_ref, old_ref, dtop_ref, dlow_ref, dedge_ref, dcorner_ref, pack_ref, frame_ref) = refs[7:13], refs[13:]
    wide, cols = low_a_ref.shape[1], g_own_ref.shape[1]
    span = cols - wide + WIN
    frame_ref[0:HALF, 0:WIN] = low_a_ref[:, wide - WIN :].astype(F32)
    frame_ref[HALF:, 0:WIN] = below_a_ref[:, wide - WIN :].astype(F32)
    frame_ref[0:HALF, WIN:span] = low_b_ref[...].astype(F32)
    frame_ref[HALF:, WIN:span] = below_b_ref[...].astype(F32)
    frame_ref[0:HALF, span : span + WIN] = edge_ref[0:HALF].astype(F32)
    frame_ref[HALF:, span : span + WIN] = edge_ref[WIN : WIN + HALF].astype(F32)
    x = frame_ref[:, HALF : span + HALF]
    frame_ref[0:HALF, 0:span] = g_own_ref[HALF:, wide - WIN :].astype(F32)
    frame_ref[HALF:, 0:span] = g_below_ref[0:HALF, wide - WIN :].astype(F32)
    frame_ref[0:HALF, span : span + WIN] = edge_ref[HALF:WIN].astype(F32)
    frame_ref[HALF:, span : span + WIN] = edge_ref[WIN + HALF :].astype(F32)
    gy = frame_ref[:, HALF : span + HALF]
    dx, *sums = second_half(x, gy, 9, *weights)
    pack(pack_ref, *sums, old_ref)
    tile = from_windows(jnp.concatenate([dx_ref[...].astype(F32), dx], axis=0))
    dtop_ref[...] = tile[:HALF].astype(BF16)
    dlow_ref[...] = tile[HALF:].astype(BF16)
    dedge_ref[...] = tile[:HALF, cols - WIN :].astype(BF16)
    dcorner_ref[...] = tile[HALF:, cols - WIN :].astype(BF16)


def last_kernel(*refs):
    (own, above, left, corner), kept_refs, refs = refs[:4], refs[4:6], refs[6:]
    w_qkv_ref, w_proj_ref, w_up_ref, w_down_ref, gain_ref, other_ref, core_ref = refs[:7]
    dx_ref, keep_ref, send_ref, frame_ref, pack_ref = refs[7:]
    cols = own.shape[1]
    frame_ref[HALF:, 0:WIN] = left[...].astype(F32)
    frame_ref[0:HALF, 0:WIN] = corner[...].astype(F32)
    first = frame_ref[:, HALF:WIN]
    frame_ref[:, 0:HALF] = first
    frame_ref[HALF:, HALF : HALF + cols] = own[...].astype(F32)
    frame_ref[0:HALF, HALF : HALF + cols] = above[...].astype(F32)
    gy = to_windows(frame_ref[:, 0:cols]).astype(BF16)
    kept = [jnp.concatenate([ref[:, place] for ref in kept_refs], axis=0) for place in kept_slices()]
    kept = [v.astype(F32) if i in (0, 1, 5, 6) else v for i, v in enumerate(kept)]
    g1, g2 = gain_ref[0, 0:1], gain_ref[0, 1:2]
    dx, grads, bias, gain1, gain2 = backward(
        gy, kept, nn(kept[2], w_qkv_ref[0]).astype(BF16), w_qkv_ref[0], w_proj_ref[0], w_up_ref[0], w_down_ref[0], g1, g2, head_mask(), 8
    )
    dx_ref[...] = from_windows(dx).astype(BF16)
    pack(pack_ref, grads, bias, gain1, gain2)
    first_core = core_ref[0] == 0

    @pl.when(first_core)
    def _():
        keep_ref[...] = pack_ref[...]
        send_ref[...] = other_ref[...].astype(BF16)

    @pl.when(jnp.logical_not(first_core))
    def _():
        keep_ref[...] = other_ref[...]
        send_ref[...] = pack_ref[...].astype(BF16)


def unpack_kernel(mine, core_ref, part_ref, *refs):
    outs, places, sem = refs[-13:-7], refs[-7:-1], refs[-1]
    qkv, proj, up, down, gain, bias = places
    for j in range(3):
        qkv[:, CH * j : CH * (j + 1)] = part_ref[ROW_QKV + CH * j : ROW_QKV + CH * (j + 1)].astype(F32)
    proj[...] = part_ref[ROW_PROJ : ROW_PROJ + CH].astype(F32)
    for j in range(4):
        up[:, CH * j : CH * (j + 1)] = part_ref[ROW_UP + CH * j : ROW_UP + CH * (j + 1)].astype(F32)
    down[...] = part_ref[ROW_DOWN : ROW_DOWN + FFN].astype(F32)
    for j in range(2):
        turned = part_ref[ROW_BIAS + LEN * j : ROW_BIAS + LEN * (j + 1)].astype(F32).T
        bias[2 * j] = turned[:LEN]
        bias[2 * j + 1] = turned[LEN:]
    gain[...] = part_ref[ROW_GAIN : ROW_GAIN + 16].astype(F32)[0:2]
    block = core_ref[0] if mine else 1 - core_ref[0]
    copies = [pltpu.make_async_copy(a, b.at[block], sem.at[i]) for i, (a, b) in enumerate(zip(places, outs))]
    for copy in copies:
        copy.start()
    for copy in copies:
        copy.wait()


def vmem(count):
    return [pl.BlockSpec(memory_space=pltpu.VMEM)] * count


def cost(flops, moved):
    return pl.CostEstimate(flops=flops, bytes_accessed=moved, transcendentals=0)


def shift(value, down, right):
    tall, wide = 32, 8
    pairs = []
    for r in range(tall):
        for c in range(wide):
            pairs.append((r * wide + c, (r + down) % tall * wide + (c + right) % wide))
    return lax.ppermute(value, AXES, pairs)


def swap_core(value):
    return lax.ppermute(value, "core", [(0, 1), (1, 0)])


def scatter_sum(value, axis, count):
    pieces = value.astype(BF16).reshape(count, value.shape[0] // count, CH)
    return jnp.sum(lax.all_to_all(pieces, axis, 0, 0).astype(F32), axis=0)


def collect(value, axis, count):
    spread = jnp.broadcast_to(value[None], (count, *value.shape))
    return lax.all_to_all(spread, axis, 0, 0)


def sum_over_devices(keep, send):
    total = keep + swap_core(send).astype(F32)
    total = scatter_sum(total, PLANE, 16)
    total = jnp.sum(collect(total.astype(BF16), "z", 8).astype(F32), axis=0).astype(BF16)
    total = collect(total, PLANE, 16).reshape(ROWS, CH)
    return total, swap_core(total)


def body(latent, cotangent, w_qkv, w_proj, w_up, w_down, gains, attn_bias):
    cols = latent.shape[1]
    half = jax.ShapeDtypeStruct((HALF, cols, CH), BF16)
    params = pltpu.CompilerParams(vmem_limit_bytes=VMEM_LIMIT)
    packed = jax.ShapeDtypeStruct((ROWS, CH), F32)
    core = lax.axis_index("core").reshape(1)
    weights = (w_qkv, w_proj, w_up, w_down, gains)
    g_below = shift(cotangent, -1, 0)
    tokens = WIN * cols

    wide = cols // 2
    part_a = WIN * (wide - WIN)
    small = jax.ShapeDtypeStruct((HALF, WIN, CH), BF16)
    side = jax.ShapeDtypeStruct((HALF, wide, CH), BF16)
    corner = jax.ShapeDtypeStruct((WIN, WIN, CH), BF16)
    top_a, low_a, edge_own = pl.pallas_call(
        first_kernel,
        out_shape=(side, side, corner),
        in_specs=[pl.BlockSpec(memory_space=pltpu.HBM)] * 8,
        out_specs=vmem(3),
        scratch_shapes=[pltpu.VMEM((WIN, wide, CH), BF16)]
        + [pltpu.VMEM(w.shape[1:], w.dtype) for w in (*weights, attn_bias)]
        + [pltpu.VMEM((HALF, WIN, CH), BF16), pltpu.SemaphoreType.DMA((8,))],
        compiler_params=pltpu.CompilerParams(vmem_limit_bytes=FIRST_LIMIT),
        cost_estimate=cost(300_000_000, 1_500_000),
        name="forward_first",
    )(latent, *weights, attn_bias, cotangent)
    below_a = shift(top_a, -1, 0)
    top_b, low_b = pl.pallas_call(
        next_kernel,
        out_shape=(side, side),
        in_specs=vmem(7),
        out_specs=vmem(2),
        compiler_params=params,
        cost_estimate=cost(300_000_000, 1_500_000),
        name="forward_next",
    )(latent, *weights, attn_bias)
    below_b = shift(top_b, -1, 0)
    edge = shift(jnp.concatenate([edge_own, below_a[:, :WIN], g_below[:HALF, :WIN]], axis=0), 0, -1)
    weights = (*weights, attn_bias)
    frame = pltpu.VMEM((WIN, cols + 2 * WIN, CH), F32)
    dx_a, pack_a = pl.pallas_call(
        second_kernel,
        out_shape=(jax.ShapeDtypeStruct((part_a, CH), BF16), packed),
        in_specs=vmem(10),
        out_specs=vmem(2),
        scratch_shapes=[frame],
        compiler_params=params,
        cost_estimate=cost(700_000_000, 3_000_000),
        name="backward_second",
    )(low_a, below_a, cotangent, g_below, *weights)
    edge, below_b, dx_a = lax.optimization_barrier((edge, below_b, dx_a))
    d_top, d_low, d_edge, d_corner, pack_two = pl.pallas_call(
        third_kernel,
        out_shape=(half, half, small, small, packed),
        in_specs=vmem(15),
        out_specs=vmem(5),
        scratch_shapes=[frame],
        compiler_params=params,
        cost_estimate=cost(800_000_000, 3_000_000),
        name="backward_third",
    )(low_a, low_b, below_a, below_b, cotangent, g_below, edge, *weights, dx_a, pack_a)
    d_above, d_left, d_corner = shift(d_low, 1, 0), shift(d_edge, 0, 1), shift(d_corner, 1, 1)
    passed = ()
    for part, arrays in enumerate(((), (pack_two, d_top))):
        arrays = (*passed, *arrays)
        passed = pl.pallas_call(
            functools.partial(keep_kernel, part),
            out_shape=(
                jax.ShapeDtypeStruct((WIN * wide, sum(KEPT)), BF16),
                *[jax.ShapeDtypeStruct(a.shape, a.dtype) for a in arrays],
            ),
            in_specs=vmem(5 + len(arrays)),
            out_specs=vmem(1 + len(arrays)),
            compiler_params=params,
            cost_estimate=cost(30_000_000, 200_000),
            name="keep_first",
        )(latent, w_qkv, w_proj, gains, attn_bias, *arrays)
    kept_b, kept_a, pack_two, d_top = passed
    dx, keep, send = pl.pallas_call(
        last_kernel,
        out_shape=(
            jax.ShapeDtypeStruct(latent.shape, BF16),
            packed,
            jax.ShapeDtypeStruct((ROWS, CH), BF16),
        ),
        in_specs=vmem(12) + [pl.BlockSpec(memory_space=pltpu.SMEM)],
        out_specs=vmem(3),
        scratch_shapes=[frame, pltpu.VMEM((ROWS, CH), F32)],
        compiler_params=params,
        cost_estimate=cost(1_500_000_000, 4_000_000),
        name="backward_first",
    )(d_top, d_above, d_left, d_corner, kept_a, kept_b, *weights[:5], pack_two, core)
    parts = sum_over_devices(keep, send)
    shapes = ((CH, 3 * CH), (CH, CH), (CH, FFN), (FFN, CH), (2, CH), (HEADS, LEN, LEN))
    outs = ()
    for mine, part in zip((True, False), parts):
        outs = pl.pallas_call(
            functools.partial(unpack_kernel, mine),
            out_shape=[jax.ShapeDtypeStruct((2, *shape), F32) for shape in shapes],
            in_specs=[pl.BlockSpec(memory_space=pltpu.SMEM)]
            + vmem(1)
            + [pl.BlockSpec(memory_space=pl.ANY)] * len(outs),
            out_specs=[pl.BlockSpec(memory_space=pl.ANY)] * 6,
            scratch_shapes=[pltpu.VMEM(shape, F32) for shape in shapes] + [pltpu.SemaphoreType.DMA((6,))],
            input_output_aliases={2 + i: i for i in range(len(outs))},
            compiler_params=params,
            cost_estimate=cost(1_000_000, 2_000_000),
            name="unpack",
        )(core, part, *outs)
    qkv, proj, up, down, gain, bias = outs
    return dx, qkv, proj, up, down, gain, bias


def solution(mesh):
    fine = jax.sharding.Mesh(mesh.devices.reshape(8, 2, 2, 4, 2), AXES)
    tiles = P(("z", "yh", "core"), ("x", "yl"), None)
    in_specs = (tiles, tiles, P(), P(), P(), P(), P(), P())
    out_specs = (tiles, P(), P(), P(), P(), P(), P())
    return jax.shard_map(body, mesh=fine, in_specs=in_specs, out_specs=out_specs, check_vma=False)
```

```python
import functools

import jax
import jax.numpy as jnp
from jax import lax
from jax.experimental import pallas as pl
from jax.experimental.pallas import tpu as pltpu
from jax.sharding import PartitionSpec as P

WIN = 8
HALF = 4
LEN = 64
CH = 128
HEADS = 4
FFN = 512
EPS = 1e-05
SCALE = (CH // HEADS) ** -0.5
F32 = jnp.float32
BF16 = jnp.bfloat16
VMEM_LIMIT = 16 * 1024 * 1024
FIRST_LIMIT = 57 * 1000 * 1000

ROW_QKV, ROW_PROJ, ROW_UP, ROW_DOWN, ROW_BIAS, ROW_GAIN, ROWS = 0, 384, 512, 1024, 1536, 1664, 1792
AXES = ("z", "yh", "core", "x", "yl")
PLANE = ("yh", "x", "yl")


def nn(a, b):
    return lax.dot_general(a, b, (((1,), (0,)), ((), ())), preferred_element_type=F32)


def nt(a, b):
    return lax.dot_general(a, b, (((1,), (1,)), ((), ())), preferred_element_type=F32)


def tn(a, b):
    return lax.dot_general(a, b, (((0,), (0,)), ((), ())), preferred_element_type=F32)


def lane_means(parts):
    width = len(parts) * CH
    block = lax.broadcasted_iota(jnp.int32, (width, width), 0) // CH == lax.broadcasted_iota(jnp.int32, (width, width), 1) // CH
    ones = (block.astype(F32) * (1.0 / CH)).astype(BF16)
    sums = nn(jnp.concatenate([p.astype(BF16) for p in parts], axis=1), ones)
    return [sums[:, CH * i : CH * (i + 1)] for i in range(len(parts))]


def normalise(v):
    centre = v - nn(v.astype(BF16), jnp.full((CH, CH), 1.0 / CH, BF16))
    square = centre * centre
    high = square.astype(BF16)
    low = (square - high.astype(F32)).astype(BF16)
    spread = nn(jnp.concatenate([high, low], axis=1), jnp.full((2 * CH, CH), 1.0 / CH, BF16))
    inv = lax.rsqrt(spread + EPS)
    return centre * inv, inv


def normalise_back(dn, hat, inv, gain):
    d_hat = dn * gain
    mean, along = lane_means([d_hat, d_hat * hat])
    return inv * (d_hat - mean - hat * along)


def head_mask():
    rows = lax.broadcasted_iota(jnp.int32, (HEADS * LEN, CH), 0) // LEN
    lanes = lax.broadcasted_iota(jnp.int32, (HEADS * LEN, CH), 1) // (CH // HEADS)
    return (rows == lanes).astype(F32).astype(BF16)


def spread_heads(v, mask):
    return jnp.concatenate([v] * HEADS, axis=0) * mask


def gather_heads(v):
    lane = lax.broadcasted_iota(jnp.int32, (LEN, CH), 1)
    size = CH // HEADS
    out = v[3 * LEN :]
    for h in (2, 1, 0):
        out = jnp.where(lane < (h + 1) * size, v[h * LEN : (h + 1) * LEN], out)
    return out


def rows_of(values, w):
    return values[w * LEN : (w + 1) * LEN]


def groups_of(tokens, group):
    count = tokens // LEN
    return [range(start, min(start + group, count)) for start in range(0, count, group)]


def in_stages(stages, groups):
    state = [None] * len(groups)
    for step in range(len(groups) + len(stages) - 1):
        for s in reversed(range(len(stages))):
            g = step - s
            if 0 <= g < len(groups):
                state[g] = stages[s](groups[g], state[g])
    return state


def attention(qkv, bias_t, mask, group):
    def scores(windows, _):
        parts = [rows_of(qkv, w) for w in windows]
        return parts, [nt(x[:, CH : 2 * CH], spread_heads(x[:, :CH], mask)) * SCALE + bias_t for x in parts]

    def softmax(_, state):
        parts, values = state
        e = [jnp.exp(x - jnp.max(x, axis=0, keepdims=True)) for x in values]
        return parts, [(x * (1.0 / jnp.sum(x, axis=0, keepdims=True))).astype(BF16) for x in e]

    def mix(_, state):
        parts, p = state
        o = [tn(x, y[:, 2 * CH :]) for x, y in zip(p, parts)]
        return [gather_heads(x).astype(BF16) for x in o], p

    done = in_stages((scores, softmax, mix), groups_of(qkv.shape[0], group))
    return jnp.concatenate(sum((x for x, _ in done), []), axis=0), jnp.concatenate(sum((x for _, x in done), []), axis=0)


def attention_back(d_o, qkv, p, mask, group):
    def spread(windows, _):
        parts = [rows_of(qkv, w) for w in windows]
        weights = [rows_of(p, w) for w in windows]
        do_spread = [spread_heads(rows_of(d_o, w), mask) for w in windows]
        dp = [nt(x[:, 2 * CH :], y) for x, y in zip(parts, do_spread)]
        return parts, weights, dp, [nn(x, y) for x, y in zip(weights, do_spread)]

    def softmax(_, state):
        parts, weights, dp, dv = state
        weights = [x.astype(F32) for x in weights]
        return parts, [x * (y - jnp.sum(y * x, axis=0, keepdims=True)) for x, y in zip(weights, dp)], dv

    def mix(_, state):
        parts, ds, dv = state
        dsb = [x.astype(BF16) for x in ds]
        dk = [nn(x, spread_heads(y[:, :CH], mask)) * SCALE for x, y in zip(dsb, parts)]
        dq = [gather_heads(tn(x, y[:, CH : 2 * CH])) * SCALE for x, y in zip(dsb, parts)]
        return [jnp.concatenate(x, axis=1).astype(BF16) for x in zip(dq, dk, dv)], sum(ds[1:], ds[0])

    done = in_stages((spread, softmax, mix), groups_of(qkv.shape[0], group))
    bias = sum((x for _, x in done[1:]), done[0][1])
    return jnp.concatenate(sum((x for x, _ in done), []), axis=0), bias


def gelu_and_slope(u):
    c = 0.7978845608028654
    sq = u * u
    s = 0.5 * jnp.tanh(u * (c + (c * 0.044715) * sq)) + 0.5
    m = u * s
    return m, s + m * (1.0 - s) * (2.0 * c + (6.0 * c * 0.044715) * sq)


def forward(x, w_qkv, w_proj, gains, bias, mask, group):
    hat1, inv1 = normalise(x)
    gain = gains()
    a1 = (hat1 * gain[0:1]).astype(BF16)
    qkv = nn(a1, w_qkv()).astype(BF16)
    o, p = attention(qkv, turned_bias(bias()), mask, group)
    h = (x + nn(o, w_proj())).astype(BF16).astype(F32)
    hat2, inv2 = normalise(h)
    a2 = (hat2 * gain[1:2]).astype(BF16)
    return h, (hat1, inv1, a1, p, o, hat2, inv2, a2), qkv


def backward(gy, kept, qkv, w_qkv, w_proj, w_up, w_down, g1, g2, mask, group):
    hat1, inv1, a1, p, o, hat2, inv2, a2 = kept
    m, slope = gelu_and_slope(nn(a2, w_up))
    m = m.astype(BF16)
    du = (nt(gy, w_down) * slope).astype(BF16)
    da2 = nt(du, w_up)
    down, up = tn(gy, m), tn(a2, du)
    gain2 = jnp.sum(da2 * hat2, axis=0, keepdims=True)
    dh = gy.astype(F32) + normalise_back(da2, hat2, inv2, g2)
    dhb = dh.astype(BF16)
    d_o = nt(dhb, w_proj).astype(BF16)
    proj = tn(o, dhb)
    dqkv, bias = attention_back(d_o, qkv, p, mask, group)
    da1 = nt(dqkv, w_qkv)
    grads = (tn(a1, dqkv), proj, up, down)
    gain1 = jnp.sum(da1 * hat1, axis=0, keepdims=True)
    dx = dh + normalise_back(da1, hat1, inv1, g1)
    return dx, grads, bias, gain1, gain2


def pack(pack_ref, grads, bias, gain1, gain2, old=None):
    qkv, proj, up, down = grads

    def put(at, value):
        rows = slice(at, at + value.shape[0])
        pack_ref[rows] = value if old is None else value + old[rows].astype(F32)

    for j in range(3):
        put(ROW_QKV + CH * j, qkv[:, CH * j : CH * (j + 1)])
    put(ROW_PROJ, proj)
    for j in range(4):
        put(ROW_UP + CH * j, up[:, CH * j : CH * (j + 1)])
        put(ROW_DOWN + CH * j, down[:, CH * j : CH * (j + 1)].T)
    put(ROW_BIAS, bias[:, :CH])
    put(ROW_BIAS + LEN, bias[:, CH:])
    put(ROW_GAIN, jnp.concatenate([gain1, gain2, jnp.zeros((ROWS - ROW_GAIN - 2, CH), F32)], axis=0))


def to_windows(tile):
    rows, cols, ch = tile.shape
    return tile.reshape(WIN, cols // WIN, WIN, ch).transpose(1, 0, 2, 3).reshape(-1, ch)


def from_windows(tokens):
    count = tokens.shape[0] // LEN
    return tokens.reshape(count, WIN, WIN, CH).transpose(1, 0, 2, 3).reshape(WIN, count * WIN, CH)


def turned_bias(bias):
    return jnp.concatenate([bias[h].T for h in range(HEADS)], axis=1)


def first_half(x, group, w_qkv, w_proj, w_up, w_down, gains, bias):
    h, kept, _ = forward(to_windows(x.astype(F32)), w_qkv, w_proj, gains, bias, head_mask(), group)
    m, _ = gelu_and_slope(nn(kept[7], w_up()))
    return from_windows(h + nn(m.astype(BF16), w_down()))


def first_kernel(*refs):
    sources, (top_ref, low_ref, edge_ref), refs = refs[:8], refs[8:11], refs[11:]
    targets, sem = refs[:8], refs[8]
    wide = sources[0].shape[1] // 2
    moves = [(sources[0].at[:, 0:wide], targets[0])]
    moves += [(source.at[0], target) for source, target in zip(sources[1:7], targets[1:7])]
    moves += [(sources[7].at[HALF:, 0:WIN], targets[7])]
    copies = [pltpu.make_async_copy(source, target, sem.at[i]) for i, (source, target) in enumerate(moves)]
    for i in (0, 5, 1, 6, 2, 3, 4, 7):
        copies[i].start(priority=1)

    def fetched(i):
        copies[i].wait()
        return targets[i][...]

    parts = [functools.partial(fetched, i) for i in range(1, 7)]
    tile = first_half(fetched(0), 8, *parts)
    top_ref[...] = tile[:HALF].astype(BF16)
    low_ref[...] = tile[HALF:].astype(BF16)
    edge_ref[0:HALF] = tile[HALF:, 0:WIN].astype(BF16)
    edge_ref[HALF:] = fetched(7)


def at(ref, i):
    return lambda: ref[i]


def next_kernel(x_ref, w_qkv_ref, w_proj_ref, w_up_ref, w_down_ref, gain_ref, bias_ref, top_ref, low_ref):
    wide = x_ref.shape[1] // 2
    parts = [at(ref, 0) for ref in (w_qkv_ref, w_proj_ref, w_up_ref, w_down_ref, gain_ref, bias_ref)]
    tile = first_half(x_ref[:, wide:], 8, *parts)
    top_ref[...] = tile[:HALF].astype(BF16)
    low_ref[...] = tile[HALF:].astype(BF16)


KEPT = (CH, CH, CH, HEADS * LEN, CH, CH, CH, CH)


def kept_slices():
    starts = [sum(KEPT[:i]) for i in range(len(KEPT))]
    return [slice(start, start + width) for start, width in zip(starts, KEPT)]


def keep_kernel(part, x_ref, w_qkv_ref, w_proj_ref, gain_ref, bias_ref, *refs):
    kept_ref = refs[len(refs) // 2]
    for source, target in zip(refs[: len(refs) // 2], refs[len(refs) // 2 + 1 :]):
        target[...] = source[...]
    wide = x_ref.shape[1] // 2
    x = to_windows(x_ref[:, part * wide : (part + 1) * wide].astype(F32))
    _, kept, _ = forward(x, at(w_qkv_ref, 0), at(w_proj_ref, 0), at(gain_ref, 0), at(bias_ref, 0), head_mask(), 8)
    for place, value, width in zip(kept_slices(), kept, KEPT):
        kept_ref[:, place] = jnp.broadcast_to(value, (x.shape[0], width)).astype(BF16)


def second_half(x, gy, group, w_qkv_ref, w_proj_ref, w_up_ref, w_down_ref, gain_ref, bias_ref):
    mask = head_mask()
    _, kept, qkv = forward(
        to_windows(x), at(w_qkv_ref, 1), at(w_proj_ref, 1), at(gain_ref, 1), at(bias_ref, 1), mask, group
    )
    w_qkv, w_proj, w_up, w_down = w_qkv_ref[1], w_proj_ref[1], w_up_ref[1], w_down_ref[1]
    g1, g2 = gain_ref[1, 0:1], gain_ref[1, 1:2]
    return backward(to_windows(gy).astype(BF16), kept, qkv, w_qkv, w_proj, w_up, w_down, g1, g2, mask, group)


def second_kernel(*refs):
    low_ref, below_ref, g_own_ref, g_below_ref = refs[:4]
    weights, (dx_ref, pack_ref, frame_ref) = refs[4:10], refs[10:]
    wide = low_ref.shape[1]
    frame_ref[0:HALF, 0:wide] = low_ref[...].astype(F32)
    frame_ref[HALF:, 0:wide] = below_ref[...].astype(F32)
    x = frame_ref[:, HALF : wide - HALF]
    frame_ref[0:HALF, 0:wide] = g_own_ref[HALF:, 0:wide].astype(F32)
    frame_ref[HALF:, 0:wide] = g_below_ref[0:HALF, 0:wide].astype(F32)
    gy = frame_ref[:, HALF : wide - HALF]
    dx, *sums = second_half(x, gy, 7, *weights)
    dx_ref[...] = dx.astype(BF16)
    pack(pack_ref, *sums)


def third_kernel(*refs):
    low_a_ref, low_b_ref, below_a_ref, below_b_ref, g_own_ref, g_below_ref, edge_ref = refs[:7]
    weights, (dx_ref, old_ref, dtop_ref, dlow_ref, dedge_ref, dcorner_ref, pack_ref, frame_ref) = refs[7:13], refs[13:]
    wide, cols = low_a_ref.shape[1], g_own_ref.shape[1]
    span = cols - wide + WIN
    frame_ref[0:HALF, 0:WIN] = low_a_ref[:, wide - WIN :].astype(F32)
    frame_ref[HALF:, 0:WIN] = below_a_ref[:, wide - WIN :].astype(F32)
    frame_ref[0:HALF, WIN:span] = low_b_ref[...].astype(F32)
    frame_ref[HALF:, WIN:span] = below_b_ref[...].astype(F32)
    frame_ref[0:HALF, span : span + WIN] = edge_ref[0:HALF].astype(F32)
    frame_ref[HALF:, span : span + WIN] = edge_ref[WIN : WIN + HALF].astype(F32)
    x = frame_ref[:, HALF : span + HALF]
    frame_ref[0:HALF, 0:span] = g_own_ref[HALF:, wide - WIN :].astype(F32)
    frame_ref[HALF:, 0:span] = g_below_ref[0:HALF, wide - WIN :].astype(F32)
    frame_ref[0:HALF, span : span + WIN] = edge_ref[HALF:WIN].astype(F32)
    frame_ref[HALF:, span : span + WIN] = edge_ref[WIN + HALF :].astype(F32)
    gy = frame_ref[:, HALF : span + HALF]
    dx, *sums = second_half(x, gy, 9, *weights)
    pack(pack_ref, *sums, old_ref)
    tile = from_windows(jnp.concatenate([dx_ref[...].astype(F32), dx], axis=0))
    dtop_ref[...] = tile[:HALF].astype(BF16)
    dlow_ref[...] = tile[HALF:].astype(BF16)
    dedge_ref[...] = tile[:HALF, cols - WIN :].astype(BF16)
    dcorner_ref[...] = tile[HALF:, cols - WIN :].astype(BF16)


def last_kernel(*refs):
    (own, above, left, corner), kept_refs, refs = refs[:4], refs[4:6], refs[6:]
    w_qkv_ref, w_proj_ref, w_up_ref, w_down_ref, gain_ref, other_ref, core_ref = refs[:7]
    dx_ref, keep_ref, send_ref, frame_ref, pack_ref = refs[7:]
    cols = own.shape[1]
    frame_ref[HALF:, 0:WIN] = left[...].astype(F32)
    frame_ref[0:HALF, 0:WIN] = corner[...].astype(F32)
    first = frame_ref[:, HALF:WIN]
    frame_ref[:, 0:HALF] = first
    frame_ref[HALF:, HALF : HALF + cols] = own[...].astype(F32)
    frame_ref[0:HALF, HALF : HALF + cols] = above[...].astype(F32)
    gy = to_windows(frame_ref[:, 0:cols]).astype(BF16)
    kept = [jnp.concatenate([ref[:, place] for ref in kept_refs], axis=0) for place in kept_slices()]
    kept = [v.astype(F32) if i in (0, 1, 5, 6) else v for i, v in enumerate(kept)]
    g1, g2 = gain_ref[0, 0:1], gain_ref[0, 1:2]
    dx, grads, bias, gain1, gain2 = backward(
        gy, kept, nn(kept[2], w_qkv_ref[0]).astype(BF16), w_qkv_ref[0], w_proj_ref[0], w_up_ref[0], w_down_ref[0], g1, g2, head_mask(), 8
    )
    dx_ref[...] = from_windows(dx).astype(BF16)
    pack(pack_ref, grads, bias, gain1, gain2)
    first_core = core_ref[0] == 0

    @pl.when(first_core)
    def _():
        keep_ref[...] = pack_ref[...]
        send_ref[...] = other_ref[...].astype(BF16)

    @pl.when(jnp.logical_not(first_core))
    def _():
        keep_ref[...] = other_ref[...]
        send_ref[...] = pack_ref[...].astype(BF16)


def unpack_kernel(mine, core_ref, part_ref, *refs):
    outs, places, sem = refs[-13:-7], refs[-7:-1], refs[-1]
    qkv, proj, up, down, gain, bias = places
    for j in range(3):
        qkv[:, CH * j : CH * (j + 1)] = part_ref[ROW_QKV + CH * j : ROW_QKV + CH * (j + 1)].astype(F32)
    proj[...] = part_ref[ROW_PROJ : ROW_PROJ + CH].astype(F32)
    for j in range(4):
        up[:, CH * j : CH * (j + 1)] = part_ref[ROW_UP + CH * j : ROW_UP + CH * (j + 1)].astype(F32)
    down[...] = part_ref[ROW_DOWN : ROW_DOWN + FFN].astype(F32)
    for j in range(2):
        turned = part_ref[ROW_BIAS + LEN * j : ROW_BIAS + LEN * (j + 1)].astype(F32).T
        bias[2 * j] = turned[:LEN]
        bias[2 * j + 1] = turned[LEN:]
    gain[...] = part_ref[ROW_GAIN : ROW_GAIN + 16].astype(F32)[0:2]
    block = core_ref[0] if mine else 1 - core_ref[0]
    copies = [pltpu.make_async_copy(a, b.at[block], sem.at[i]) for i, (a, b) in enumerate(zip(places, outs))]
    for copy in copies:
        copy.start()
    for copy in copies:
        copy.wait()


def vmem(count):
    return [pl.BlockSpec(memory_space=pltpu.VMEM)] * count


def cost(flops, moved):
    return pl.CostEstimate(flops=flops, bytes_accessed=moved, transcendentals=0)


def shift(value, down, right):
    tall, wide = 32, 8
    pairs = []
    for r in range(tall):
        for c in range(wide):
            pairs.append((r * wide + c, (r + down) % tall * wide + (c + right) % wide))
    return lax.ppermute(value, AXES, pairs)


def swap_core(value):
    return lax.ppermute(value, "core", [(0, 1), (1, 0)])


def scatter_sum(value, axis, count):
    pieces = value.astype(BF16).reshape(count, value.shape[0] // count, CH)
    return jnp.sum(lax.all_to_all(pieces, axis, 0, 0).astype(F32), axis=0)


def collect(value, axis, count):
    spread = jnp.broadcast_to(value[None], (count, *value.shape))
    return lax.all_to_all(spread, axis, 0, 0)


def sum_over_devices(keep, send):
    total = keep + swap_core(send).astype(F32)
    total = scatter_sum(total, PLANE, 16)
    total = jnp.sum(collect(total.astype(BF16), "z", 8).astype(F32), axis=0).astype(BF16)
    total = collect(total, PLANE, 16).reshape(ROWS, CH)
    return total, swap_core(total)


def body(latent, cotangent, w_qkv, w_proj, w_up, w_down, gains, attn_bias):
    cols = latent.shape[1]
    half = jax.ShapeDtypeStruct((HALF, cols, CH), BF16)
    params = pltpu.CompilerParams(vmem_limit_bytes=VMEM_LIMIT)
    packed = jax.ShapeDtypeStruct((ROWS, CH), F32)
    core = lax.axis_index("core").reshape(1)
    weights = (w_qkv, w_proj, w_up, w_down, gains)
    g_below = shift(cotangent, -1, 0)
    tokens = WIN * cols

    wide = cols // 2
    part_a = WIN * (wide - WIN)
    small = jax.ShapeDtypeStruct((HALF, WIN, CH), BF16)
    side = jax.ShapeDtypeStruct((HALF, wide, CH), BF16)
    corner = jax.ShapeDtypeStruct((WIN, WIN, CH), BF16)
    top_a, low_a, edge_own = pl.pallas_call(
        first_kernel,
        out_shape=(side, side, corner),
        in_specs=[pl.BlockSpec(memory_space=pltpu.HBM)] * 8,
        out_specs=vmem(3),
        scratch_shapes=[pltpu.VMEM((WIN, wide, CH), BF16)]
        + [pltpu.VMEM(w.shape[1:], w.dtype) for w in (*weights, attn_bias)]
        + [pltpu.VMEM((HALF, WIN, CH), BF16), pltpu.SemaphoreType.DMA((8,))],
        compiler_params=pltpu.CompilerParams(vmem_limit_bytes=FIRST_LIMIT),
        cost_estimate=cost(300_000_000, 1_500_000),
        name="forward_first",
    )(latent, *weights, attn_bias, cotangent)
    below_a = shift(top_a, -1, 0)
    top_b, low_b = pl.pallas_call(
        next_kernel,
        out_shape=(side, side),
        in_specs=vmem(7),
        out_specs=vmem(2),
        compiler_params=params,
        cost_estimate=cost(300_000_000, 1_500_000),
        name="forward_next",
    )(latent, *weights, attn_bias)
    below_b = shift(top_b, -1, 0)
    edge = shift(jnp.concatenate([edge_own, below_a[:, :WIN], g_below[:HALF, :WIN]], axis=0), 0, -1)
    weights = (*weights, attn_bias)
    frame = pltpu.VMEM((WIN, cols + 2 * WIN, CH), F32)
    dx_a, pack_a = pl.pallas_call(
        second_kernel,
        out_shape=(jax.ShapeDtypeStruct((part_a, CH), BF16), packed),
        in_specs=vmem(10),
        out_specs=vmem(2),
        scratch_shapes=[frame],
        compiler_params=params,
        cost_estimate=cost(700_000_000, 3_000_000),
        name="backward_second",
    )(low_a, below_a, cotangent, g_below, *weights)
    edge, below_b, dx_a = lax.optimization_barrier((edge, below_b, dx_a))
    d_top, d_low, d_edge, d_corner, pack_two = pl.pallas_call(
        third_kernel,
        out_shape=(half, half, small, small, packed),
        in_specs=vmem(15),
        out_specs=vmem(5),
        scratch_shapes=[frame],
        compiler_params=params,
        cost_estimate=cost(800_000_000, 3_000_000),
        name="backward_third",
    )(low_a, low_b, below_a, below_b, cotangent, g_below, edge, *weights, dx_a, pack_a)
    d_above, d_left, d_corner = shift(d_low, 1, 0), shift(d_edge, 0, 1), shift(d_corner, 1, 1)
    passed = ()
    for part, arrays in enumerate(((), (pack_two, d_top))):
        arrays = (*passed, *arrays)
        passed = pl.pallas_call(
            functools.partial(keep_kernel, part),
            out_shape=(
                jax.ShapeDtypeStruct((WIN * wide, sum(KEPT)), BF16),
                *[jax.ShapeDtypeStruct(a.shape, a.dtype) for a in arrays],
            ),
            in_specs=vmem(5 + len(arrays)),
            out_specs=vmem(1 + len(arrays)),
            compiler_params=params,
            cost_estimate=cost(30_000_000, 200_000),
            name="keep_first",
        )(latent, w_qkv, w_proj, gains, attn_bias, *arrays)
    kept_b, kept_a, pack_two, d_top = passed
    dx, keep, send = pl.pallas_call(
        last_kernel,
        out_shape=(
            jax.ShapeDtypeStruct(latent.shape, BF16),
            packed,
            jax.ShapeDtypeStruct((ROWS, CH), BF16),
        ),
        in_specs=vmem(12) + [pl.BlockSpec(memory_space=pltpu.SMEM)],
        out_specs=vmem(3),
        scratch_shapes=[frame, pltpu.VMEM((ROWS, CH), F32)],
        compiler_params=params,
        cost_estimate=cost(1_500_000_000, 4_000_000),
        name="backward_first",
    )(d_top, d_above, d_left, d_corner, kept_a, kept_b, *weights[:5], pack_two, core)
    parts = sum_over_devices(keep, send)
    shapes = ((CH, 3 * CH), (CH, CH), (CH, FFN), (FFN, CH), (2, CH), (HEADS, LEN, LEN))
    outs = ()
    for mine, part in zip((True, False), parts):
        outs = pl.pallas_call(
            functools.partial(unpack_kernel, mine),
            out_shape=[jax.ShapeDtypeStruct((2, *shape), F32) for shape in shapes],
            in_specs=[pl.BlockSpec(memory_space=pltpu.SMEM)]
            + vmem(1)
            + [pl.BlockSpec(memory_space=pl.ANY)] * len(outs),
            out_specs=[pl.BlockSpec(memory_space=pl.ANY)] * 6,
            scratch_shapes=[pltpu.VMEM(shape, F32) for shape in shapes] + [pltpu.SemaphoreType.DMA((6,))],
            input_output_aliases={2 + i: i for i in range(len(outs))},
            compiler_params=params,
            cost_estimate=cost(1_000_000, 2_000_000),
            name="unpack",
        )(core, part, *outs)
    qkv, proj, up, down, gain, bias = outs
    return dx, qkv, proj, up, down, gain, bias


def solution(mesh):
    fine = jax.sharding.Mesh(mesh.devices.reshape(8, 2, 2, 4, 2), AXES)
    tiles = P(("z", "yh", "core"), ("x", "yl"), None)
    in_specs = (tiles, tiles, P(), P(), P(), P(), P(), P())
    out_specs = (tiles, P(), P(), P(), P(), P(), P())
    return jax.shard_map(body, mesh=fine, in_specs=in_specs, out_specs=out_specs, check_vma=False)
```
